32 devices in a mesh: grp: 4 (over x, core), blk: 8 (over z, y).
Axes of the slice: x: 2, y: 2, z: 4, core: 2. Of those that a mesh axis runs over, the one named last changes fastest.
Arguments:
- obs: bfloat16 [196608, 256], P(('grp', 'blk')), may hold values from -6 to 6
- mask_bits: int32 [196608, 32], P(('grp', 'blk')), may hold values from 0 to 255
- factors: bfloat16 [196608, 256], P(('grp', 'blk')), may hold values from -0.375 to 0.375
- x_blocks: float32 [4, 256, 2048], P('grp', None, 'blk'), may hold values from -6 to 6
- first_moment: float32 [4, 256, 2048], P('grp', None, 'blk'), may hold values from -0.6 to 0.6
- second_moment: float32 [4, 256, 2048], P('grp', None, 'blk'), may hold values from 0.001 to 0.1
- ar_weights: float32 [25, 256], replicated, may hold values from -0.25 to 0.25
- stratum: int32 [1], replicated, may hold values from 0 to 7
Outputs:
- factors_next: bfloat16 [196608, 256], P(('grp', 'blk'))
- x_next: float32 [4, 256, 2048], P('grp', None, 'blk')
- first_next: float32 [4, 256, 2048], P('grp', None, 'blk')
- second_next: float32 [4, 256, 2048], P('grp', None, 'blk')
The draws below stay inside these ranges and needn't reach their ends.
All inputs are finite; a program needn't handle non-finite values.
Results may differ from the reference program's by a relative error of at most 0.0013.
Values sent between devices are 32-bit elements; how exact they have to be, the bound alone decides.
No kernel may reach another device: no remote copies, remote signals or barrier semaphores. Data moves between devices by JAX's collectives and lax.ppermute only.
A program may use at most 64 MiB of HBM per device.

```python
import math
import jax
import jax.numpy as jnp
from jax import lax

RANK = 256
SHORT = 24
SEASON = 168
TB = 256
SER_DEV = 6144
LAGS = 25
WORDS = 32
SERIES = 196608
TIME = 2048
N_GRP = 4
N_BLK = 8


def with_ends(entries, key, low, high):
    extent = entries.shape
    spot = [jax.random.randint(jax.random.fold_in(key, axis), (), 0, extent[axis]) for axis in range(len(extent))]
    entries = entries.at[tuple(spot)].set(low)
    longest = extent.index(max(extent))
    spot[longest] = (spot[longest] + 1) % extent[longest]
    return entries.at[tuple(spot)].set(high)


def level_of(key, shape, pieces, least, top_value):
    def one(position, parts):
        draws = jax.random.uniform(jax.random.fold_in(jax.random.fold_in(key, 6), position), (parts,), jnp.float32, least / len(pieces), top_value / len(pieces))
        return jnp.repeat(jnp.exp(draws), shape[position] // parts).reshape((-1,) + (1,) * (len(shape) - position - 1))

    factor_of = one(*pieces[0])
    for cut in pieces[1:]:
        factor_of = factor_of * one(*cut)
    return factor_of


def bell_draw(own_key, dims, scale, reach, pieces=(), kind=jnp.bfloat16):
    values = jax.random.normal(own_key, dims, jnp.float32) * scale
    if len(pieces) > 0:
        values = level_of(own_key, dims, pieces, -0.22, 0.18) * values
    return jnp.clip(values, min=-reach, max=reach).astype(kind)


def setup_inputs(seed: int = 0) -> dict:
    key_list = jax.random.split(jax.random.key(seed), 9)
    obs = bell_draw(key_list[0], (SERIES, TB), 1.0, 6.0, ((0, 32),))
    mask_bits = with_ends(jax.random.randint(key_list[1], (SERIES, WORDS), 0, 256), jax.random.fold_in(key_list[1], 1), 0, 255).astype(jnp.int32)
    factors = bell_draw(key_list[2], (SERIES, RANK), RANK ** -0.5, 0.375, ((0, 32),))
    x_blocks = bell_draw(key_list[3], (N_GRP, RANK, TIME), 1.0, 6.0, ((0, 4), (2, 8)), jnp.float32)
    first_moment = bell_draw(key_list[4], (N_GRP, RANK, TIME), 0.1, 0.6, ((0, 4), (2, 8)), jnp.float32)
    second_moment = jnp.clip(jnp.exp(math.log(0.1) - 4.6051702 * jax.random.uniform(key_list[5], (N_GRP, RANK, TIME), jnp.float32) ** level_of(key_list[5], (N_GRP, RANK, TIME), ((0, 4), (2, 8)), -0.2, 0.2)), 0.001, 0.1)
    ar_weights = jnp.clip(jax.random.uniform(key_list[6], (LAGS, RANK), jnp.float32, -0.25, 0.25), -0.25, 0.25)
    stratum = jax.random.randint(key_list[7], (1,), 0, N_BLK).astype(jnp.int32)
    return dict(obs=obs, mask_bits=mask_bits, factors=factors, x_blocks=x_blocks, first_moment=first_moment, second_moment=second_moment, ar_weights=ar_weights, stratum=stratum)


beta_one = 0.9
beta_two = 0.999
adam_eps = 1e-08
step_rate = 0.05
factor_rate = 0.002
data_scale = 0.25

def unpack_mask(bits):
    shifts = jnp.arange(8, dtype=jnp.int32)
    flags = jnp.bitwise_and(jnp.right_shift(bits[:, :, None], shifts[None, None, :]), 1)
    return flags.reshape(bits.shape[0], bits.shape[1] * 8).astype(jnp.float32)

def local_update(obs_tile, bits, factor_tile, block, first, second, halo, ar_weights):
    width = block.shape[1]
    mask = unpack_mask(bits)
    block_half = block.astype(jnp.bfloat16)
    predicted = jnp.dot(factor_tile, block_half, preferred_element_type=jnp.float32)
    error = (mask * (predicted - obs_tile.astype(jnp.float32))).astype(jnp.bfloat16)
    grad_factor = lax.dot_general(error, block_half, (((1,), (1,)), ((), ())), preferred_element_type=jnp.float32)
    grad_data = lax.dot_general(factor_tile, error, (((0,), (0,)), ((), ())), preferred_element_type=jnp.float32)
    extended = jnp.concatenate([halo, block], axis=1)
    lag_list = list(range(1, SHORT + 1)) + [SEASON]
    fitted = jnp.zeros_like(block)
    for index, lag in enumerate(lag_list):
        fitted = fitted + ar_weights[index][:, None] * extended[:, SEASON - lag:SEASON - lag + width]
    resid = block - fitted
    backward = jnp.zeros_like(block)
    for index, lag in enumerate(lag_list):
        later = jnp.pad(resid[:, lag:], ((0, 0), (0, lag)))
        backward = backward + ar_weights[index][:, None] * later
    gradient = data_scale * grad_data + resid - backward
    first_new = beta_one * first + (1.0 - beta_one) * gradient
    second_new = beta_two * second + (1.0 - beta_two) * gradient * gradient
    block_new = block - step_rate * first_new / (jnp.sqrt(second_new) + adam_eps)
    factor_new = (factor_tile.astype(jnp.float32) - factor_rate * grad_factor).astype(jnp.bfloat16)
    return (factor_new, block_new, first_new, second_new)

def reference(obs, mask_bits, factors, x_blocks, first_moment, second_moment, ar_weights, stratum):
    groups = N_GRP
    blocks = N_BLK

    def split(arr):
        return arr.reshape(groups, RANK, blocks, TB).transpose(0, 2, 1, 3)
    x_split = split(x_blocks)
    m_split = split(first_moment)
    v_split = split(second_moment)
    halo_all = jnp.roll(x_split, 1, axis=1)[..., TB - SEASON:]
    slots = jnp.arange(blocks, dtype=jnp.int32)
    block_index = (slots + stratum[0]) % blocks
    keep = (block_index != 0).astype(jnp.float32)
    halo_all = halo_all * keep[None, :, None, None]
    obs_split = obs.reshape(groups * blocks, SER_DEV, TB)
    bits_split = mask_bits.reshape(groups * blocks, SER_DEV, TB // 8)
    fac_split = factors.reshape(groups * blocks, SER_DEV, RANK)

    def one_tile(tile):
        group = tile // blocks
        slot = tile % blocks
        return local_update(obs_split[tile], bits_split[tile], fac_split[tile], x_split[group, slot], m_split[group, slot], v_split[group, slot], halo_all[group, slot], ar_weights)
    fac_new, x_new, m_new, v_new = lax.map(one_tile, jnp.arange(groups * blocks, dtype=jnp.int32))

    def finish(arr):
        whole = arr.reshape(groups, blocks, RANK, TB)
        mean = lax.optimization_barrier(jnp.sum(whole, axis=0)) / groups
        turned = jnp.roll(mean, -1, axis=0)
        spread = jnp.broadcast_to(turned[None], (groups, blocks, RANK, TB))
        return spread.transpose(0, 2, 1, 3).reshape(groups, RANK, blocks * TB)
    return (fac_new.reshape(groups * blocks * SER_DEV, RANK), finish(x_new), finish(m_new), finish(v_new))
```

```python
import functools

import jax
import jax.numpy as jnp
from jax import lax
from jax.experimental import pallas as pl
from jax.experimental.pallas import tpu as pltpu
from jax.sharding import PartitionSpec as P

SEASON = 168

beta_one = 0.9
beta_two = 0.999
adam_eps = 1e-08
step_rate = 0.05
factor_rate = 0.002
data_scale = 0.25

LIMIT = 32 * 1024 * 1024
F32 = jnp.float32
BF16 = jnp.bfloat16


def whole():
    return pl.BlockSpec(memory_space=pltpu.VMEM)


def scalars():
    return pl.BlockSpec(memory_space=pltpu.SMEM)


def params(**more):
    return pltpu.CompilerParams(vmem_limit_bytes=LIMIT, **more)


def cost(flops, moved):
    return pl.CostEstimate(flops=int(flops), bytes_accessed=int(moved), transcendentals=0)


def rows_of(total, most):
    best = total
    for rows in range(128, most + 1, 128):
        if total % rows == 0:
            best = rows
    return best


def prepare_kernel(share, count, here, x_ref, m_ref, v_ref, tail_ref, *early):
    group = here[0]
    tail_ref[...] = x_ref[0, :, :].T[x_ref.shape[2] - SEASON :, :]
    for step in range(1, count):
        start = pl.multiple_of((group ^ step) * share, share)
        early[step - 1][0] = x_ref[0, pl.ds(start, share), :]
        early[step - 1][1] = m_ref[0, pl.ds(start, share), :]
        early[step - 1][2] = v_ref[0, pl.ds(start, share), :]


def prepare(here, x, m, v, count):
    rank, width = x.shape[1:]
    share = rank // count
    outs = [jax.ShapeDtypeStruct((SEASON, rank), F32)]
    outs += [jax.ShapeDtypeStruct((3, share, width), F32)] * (count - 1)
    return pl.pallas_call(
        functools.partial(prepare_kernel, share, count),
        out_shape=tuple(outs),
        in_specs=[scalars()] + [whole()] * 3,
        out_specs=tuple([whole()] * count),
        compiler_params=params(),
        cost_estimate=cost(0, 6 * rank * width * 4),
        name="prepare",
    )(here, x, m, v)


def error_kernel(obs_ref, bits_ref, f_ref, x_ref, err_ref, gd_ref, half_ref):
    step = pl.program_id(0)
    words, rows = bits_ref.shape
    width = obs_ref.shape[1]
    per = width // words

    @pl.when(step == 0)
    def _():
        half_ref[...] = x_ref[0].astype(BF16)

    lane = lax.broadcasted_iota(jnp.int32, (words, width), 1)
    word = lax.broadcasted_iota(jnp.int32, (words, width), 0)
    spread = (lane // per == word).astype(BF16)
    value = lax.dot_general(
        bits_ref[...].astype(F32).astype(BF16),
        spread,
        (((0,), (0,)), ((), ())),
        preferred_element_type=F32,
    ).astype(jnp.int32)
    flag = jnp.left_shift(1, lax.broadcasted_iota(jnp.int32, (1, width), 1) % per)
    predicted = jnp.dot(f_ref[...], half_ref[...], preferred_element_type=F32)
    error = jnp.where(
        jnp.bitwise_and(value, flag) != 0, predicted - obs_ref[...].astype(F32), 0.0
    ).astype(BF16)
    err_ref[...] = error
    part = lax.dot_general(
        f_ref[...], error, (((0,), (0,)), ((), ())), preferred_element_type=F32
    )

    @pl.when(step == 0)
    def _():
        gd_ref[...] = part

    @pl.when(step != 0)
    def _():
        gd_ref[...] += part


def error_step(obs, bits, factors, x):
    series, width = obs.shape
    rank = factors.shape[1]
    words = bits.shape[0]
    rows = rows_of(series, 1024)
    return pl.pallas_call(
        error_kernel,
        out_shape=(
            jax.ShapeDtypeStruct((series, width), BF16),
            jax.ShapeDtypeStruct((rank, width), F32),
        ),
        grid=(series // rows,),
        in_specs=[
            pl.BlockSpec((rows, width), lambda i: (i, 0)),
            pl.BlockSpec((words, rows), lambda i: (0, i)),
            pl.BlockSpec((rows, rank), lambda i: (i, 0)),
            pl.BlockSpec((1, rank, width), lambda i: (0, 0, 0)),
        ],
        out_specs=(
            pl.BlockSpec((rows, width), lambda i: (i, 0)),
            pl.BlockSpec((rank, width), lambda i: (0, 0)),
        ),
        scratch_shapes=[pltpu.VMEM((rank, width), BF16)],
        compiler_params=params(),
        cost_estimate=cost(6 * series * width * rank, series * (3 * width * 2 + words * 4)),
        name="errors",
    )(obs, bits, factors, x)


def factor_kernel(f_ref, err_ref, x_ref, out_ref, half_ref):
    @pl.when(pl.program_id(0) == 0)
    def _():
        half_ref[...] = x_ref[0].astype(BF16)

    gradient = lax.dot_general(
        err_ref[...], half_ref[...], (((1,), (1,)), ((), ())), preferred_element_type=F32
    )
    out_ref[...] = (f_ref[...].astype(F32) - factor_rate * gradient).astype(BF16)


def factor_step(factors, err, x):
    series, rank = factors.shape
    width = err.shape[1]
    rows = rows_of(series, 1024)
    return pl.pallas_call(
        factor_kernel,
        out_shape=jax.ShapeDtypeStruct((series, rank), BF16),
        grid=(series // rows,),
        in_specs=[
            pl.BlockSpec((rows, rank), lambda i: (i, 0)),
            pl.BlockSpec((rows, width), lambda i: (i, 0)),
            pl.BlockSpec((1, rank, width), lambda i: (0, 0, 0)),
        ],
        out_specs=pl.BlockSpec((rows, rank), lambda i: (i, 0)),
        scratch_shapes=[pltpu.VMEM((rank, width), BF16)],
        compiler_params=params(),
        cost_estimate=cost(2 * series * width * rank, series * 3 * width * 2),
        name="factors",
    )(factors, err, x)


def gradient_kernel(share, count, lanes, here, halo_ref, x_ref, w_ref, gd_ref, *rest):
    outs, (z_ref, r_ref) = rest[:count], rest[count:]
    group, first_block = here[0], here[1]
    rank, width = x_ref.shape[1:]
    lags = list(range(1, w_ref.shape[0])) + [SEASON]
    turned = x_ref[0].T
    for part in range(rank // lanes):
        columns = slice(part * lanes, (part + 1) * lanes)
        halo = halo_ref[:, columns]
        z_ref[part, :SEASON, :] = jnp.where(first_block == 0, 0.0, halo)
        z_ref[part, SEASON:, :] = turned[:, columns]
        resid = z_ref[part, SEASON:, :]
        for index, lag in enumerate(lags):
            begin = SEASON - lag
            resid = resid - w_ref[index : index + 1, columns] * z_ref[part, begin : begin + width, :]
        r_ref[part, :width, :] = resid
        r_ref[part, width:, :] = jnp.zeros((SEASON, lanes), F32)
        back = resid
        for index, lag in enumerate(lags):
            back = back - w_ref[index : index + 1, columns] * r_ref[part, lag : lag + width, :]
        z_ref[part, :width, :] = back
    for part in range(rank // lanes):
        rows = slice(part * lanes, (part + 1) * lanes)
        gd_ref[rows, :] = data_scale * gd_ref[rows, :] + z_ref[part, :width, :].T
    for step in range(count):
        start = pl.multiple_of((group ^ step) * share, share)
        outs[step][...] = gd_ref[pl.ds(start, share), :]


def gradient_step(here, halo, x, weights, gd, count):
    rank, width = gd.shape
    share = rank // count
    lanes = 128 if rank % 128 == 0 else rank

    def kernel(here, halo_ref, x_ref, w_ref, gd_ref, *rest):
        work = rest[-1]
        work[...] = gd_ref[...]
        gradient_kernel(share, count, lanes, here, halo_ref, x_ref, w_ref, work, *rest[:-1])

    return pl.pallas_call(
        kernel,
        out_shape=tuple([jax.ShapeDtypeStruct((share, width), F32)] * count),
        in_specs=[scalars()] + [whole()] * 4,
        out_specs=tuple([whole()] * count),
        scratch_shapes=[
            pltpu.VMEM((rank // lanes, SEASON + width, lanes), F32),
            pltpu.VMEM((rank // lanes, SEASON + width, lanes), F32),
            pltpu.VMEM((rank, width), F32),
        ],
        compiler_params=params(),
        cost_estimate=cost(100 * rank * width, 4 * rank * width * 4),
        name="gradient",
    )(here, halo, x, weights, gd)


def adam_kernel(share, count, here, x_ref, m_ref, v_ref, *rest):
    grads, early, out_ref = rest[:count], rest[count:-1], rest[-1]
    start = pl.multiple_of(here[0] * share, share)
    total = [0.0, 0.0, 0.0]
    for step in range(count):
        if step == 0:
            own = [ref[0, pl.ds(start, share), :] for ref in (x_ref, m_ref, v_ref)]
        else:
            own = [early[step - 1][which] for which in range(3)]
        block, first, second = own
        gradient = grads[step][...]
        first = beta_one * first + (1.0 - beta_one) * gradient
        second = beta_two * second + (1.0 - beta_two) * gradient * gradient
        block = block - step_rate * first / (jnp.sqrt(second) + adam_eps)
        total = [total[0] + block, total[1] + first, total[2] + second]
    for which in range(3):
        out_ref[which] = total[which] / count


def adam_step(here, x, m, v, grads, early):
    count = len(grads)
    share, width = grads[0].shape
    return pl.pallas_call(
        functools.partial(adam_kernel, share, count),
        out_shape=jax.ShapeDtypeStruct((3, share, width), F32),
        in_specs=[scalars()] + [whole()] * (3 + count + count - 1),
        out_specs=whole(),
        compiler_params=params(),
        cost_estimate=cost(80 * share * width, 20 * share * width * 4),
        name="adam",
    )(here, x, m, v, *grads, *early)


def place_kernel(share, here, *rest):
    parts, outs = rest[:-3], rest[-3:]
    for step, part in enumerate(parts):
        start = pl.multiple_of((here[0] ^ step) * share, share)
        for which in range(3):
            outs[which][0, pl.ds(start, share), :] = part[which]


def place(here, parts):
    count = len(parts)
    _, share, width = parts[0].shape
    out = jax.ShapeDtypeStruct((1, count * share, width), F32)
    return pl.pallas_call(
        functools.partial(place_kernel, share),
        out_shape=(out, out, out),
        in_specs=[scalars()] + [whole()] * count,
        out_specs=(whole(), whole(), whole()),
        compiler_params=params(),
        cost_estimate=cost(0, 6 * count * share * width * 4),
        name="place",
    )(here, *parts)


def crossed(value, step):
    count = lax.axis_size("grp")
    return lax.ppermute(value, "grp", [(source, source ^ step) for source in range(count)])


def shifted(value, steps):
    count = lax.axis_size("blk")
    return lax.ppermute(value, "blk", [(source, (source + steps) % count) for source in range(count)])


def body(obs, mask_bits, factors, x_blocks, first_moment, second_moment, ar_weights, stratum):
    cycle = lax.axis_size("blk")
    count = lax.axis_size("grp")
    group = lax.axis_index("grp")
    block_index = (lax.axis_index("blk") + stratum[0]) % cycle
    here = jnp.stack([group, block_index]).astype(jnp.int32)

    tail, *early = prepare(here, x_blocks, first_moment, second_moment, count)
    halo = shifted(tail, 1)
    early = [crossed(value, step + 1) for step, value in enumerate(early)]
    err, gd = error_step(obs, mask_bits.T, factors, x_blocks)
    grads = gradient_step(here, halo, x_blocks, ar_weights, gd, count)
    grads = [grads[0]] + [crossed(grads[step], step) for step in range(1, count)]
    means = adam_step(here, x_blocks, first_moment, second_moment, grads, early)
    moved = shifted(means, -1)
    factor_new = factor_step(factors, err, x_blocks)
    parts = [moved]
    span = 1
    while span < count:
        span *= 2
    level = span // 2
    known = {0: moved}
    while level >= 1:
        for key in list(known):
            known[key ^ level] = crossed(known[key], level)
        level //= 2
    parts = [known[key] for key in range(count)]
    outs = place(here, parts)
    return (factor_new, *outs)


def solution(mesh):
    rows = P(("grp", "blk"), None)
    blocks = P("grp", None, "blk")
    return jax.shard_map(
        body,
        mesh=mesh,
        in_specs=(rows, rows, rows, blocks, blocks, blocks, P(), P()),
        out_specs=(rows, blocks, blocks, blocks),
        check_vma=False,
    )
```

```python
import functools

import jax
import jax.numpy as jnp
from jax import lax
from jax.experimental import pallas as pl
from jax.experimental.pallas import tpu as pltpu
from jax.sharding import PartitionSpec as P

SEASON = 168

beta_one = 0.9
beta_two = 0.999
adam_eps = 1e-08
step_rate = 0.05
factor_rate = 0.002
data_scale = 0.25

LIMIT = 32 * 1024 * 1024
F32 = jnp.float32
BF16 = jnp.bfloat16


def whole():
    return pl.BlockSpec(memory_space=pltpu.VMEM)


def far():
    return pl.BlockSpec(memory_space=pltpu.HBM)


def held(value):
    return pltpu.with_memory_space_constraint(value, pltpu.HBM)


def scalars():
    return pl.BlockSpec(memory_space=pltpu.SMEM)


def params(**more):
    return pltpu.CompilerParams(vmem_limit_bytes=LIMIT, **more)


def cost(flops, moved):
    return pl.CostEstimate(flops=int(flops), bytes_accessed=int(moved), transcendentals=0)


def rows_of(total, most):
    best = total
    for rows in range(128, most + 1, 128):
        if total % rows == 0:
            best = rows
    return best


def prepare_kernel(share, count, here, x_hbm, m_hbm, v_hbm, tail_ref, turned_ref, x_ref, own_ref, *rest):
    early, (x_sem, sems) = rest[:-2], rest[-2:]
    group = here[0]
    whole_copy = pltpu.make_async_copy(x_hbm.at[0], x_ref, x_sem)
    whole_copy.start()
    copies = []
    for step in range(count):
        target = own_ref if step == 0 else early[step - 1]
        start = pl.multiple_of((group ^ step) * share, share)
        for which, source in enumerate((x_hbm, m_hbm, v_hbm)):
            copies.append(
                pltpu.make_async_copy(
                    source.at[0, pl.ds(start, share), :], target.at[which], sems.at[step, which]
                )
            )
    for copy in copies:
        copy.start()
    whole_copy.wait()
    turned_ref[...] = x_ref[...].T
    tail_ref[...] = turned_ref[turned_ref.shape[0] - SEASON :, :]
    for copy in copies:
        copy.wait()


def prepare(here, x, m, v, count):
    rank, width = x.shape[1:]
    share = rank // count
    outs = [
        jax.ShapeDtypeStruct((SEASON, rank), F32),
        jax.ShapeDtypeStruct((width, rank), F32),
        jax.ShapeDtypeStruct((rank, width), F32),
    ]
    outs += [jax.ShapeDtypeStruct((3, share, width), F32)] * count
    return pl.pallas_call(
        functools.partial(prepare_kernel, share, count),
        out_shape=tuple(outs),
        in_specs=[scalars()] + [far()] * 3,
        out_specs=tuple([whole()] * len(outs)),
        scratch_shapes=[pltpu.SemaphoreType.DMA(()), pltpu.SemaphoreType.DMA((count, 3))],
        compiler_params=params(),
        cost_estimate=cost(0, 6 * rank * width * 4),
        name="prepare",
    )(here, held(x), held(m), held(v))


def error_kernel(chunks, obs_hbm, bits_hbm, f_hbm, x_ref, err_ref, f_ref, gd_ref, obs_ref, bits_ref, sems):
    words, series = bits_ref.shape
    width = obs_ref.shape[1]
    per = width // words
    rows = series // chunks

    def copies(index):
        part = pl.ds(index * rows, rows)
        return (
            pltpu.make_async_copy(bits_hbm.at[:, part], bits_ref.at[:, part], sems.at[index, 0]),
            pltpu.make_async_copy(f_hbm.at[part, :], f_ref.at[part, :], sems.at[index, 1]),
            pltpu.make_async_copy(obs_hbm.at[part, :], obs_ref.at[part, :], sems.at[index, 2]),
        )

    for index in range(chunks):
        for copy in copies(index):
            copy.start()
    half = x_ref[...].astype(BF16)
    lane = lax.broadcasted_iota(jnp.int32, (words, width), 1)
    word = lax.broadcasted_iota(jnp.int32, (words, width), 0)
    spread = (lane // per == word).astype(BF16)
    flag = jnp.left_shift(1, lax.broadcasted_iota(jnp.int32, (1, width), 1) % per)
    for index in range(chunks):
        for copy in copies(index):
            copy.wait()
        part = pl.ds(index * rows, rows)
        value = lax.dot_general(
            bits_ref[:, part].astype(F32).astype(BF16),
            spread,
            (((0,), (0,)), ((), ())),
            preferred_element_type=F32,
        ).astype(jnp.int32)
        predicted = jnp.dot(f_ref[part, :], half, preferred_element_type=F32)
        error = jnp.where(
            jnp.bitwise_and(value, flag) != 0, predicted - obs_ref[part, :].astype(F32), 0.0
        ).astype(BF16)
        err_ref[part, :] = error
        term = lax.dot_general(
            f_ref[part, :], error, (((0,), (0,)), ((), ())), preferred_element_type=F32
        )
        if index == 0:
            gd_ref[...] = term
        else:
            gd_ref[...] += term


def error_step(obs, bits, factors, x):
    series, width = obs.shape
    rank = factors.shape[1]
    words = bits.shape[0]
    chunks = series // rows_of(series, 1024)
    return pl.pallas_call(
        functools.partial(error_kernel, chunks),
        out_shape=(
            jax.ShapeDtypeStruct((series, width), BF16),
            jax.ShapeDtypeStruct((series, rank), BF16),
            jax.ShapeDtypeStruct((rank, width), F32),
        ),
        in_specs=[far(), far(), far(), whole()],
        out_specs=(whole(), whole(), whole()),
        scratch_shapes=[
            pltpu.VMEM((series, width), BF16),
            pltpu.VMEM((words, series), jnp.int32),
            pltpu.SemaphoreType.DMA((chunks, 3)),
        ],
        compiler_params=params(),
        cost_estimate=cost(6 * series * width * rank, series * (3 * width * 2 + words * 4)),
        name="errors",
    )(held(obs), held(bits), held(factors), x)


def factor_kernel(f_ref, err_ref, x_ref, after, out_ref, half_ref):
    @pl.when(pl.program_id(0) == 0)
    def _():
        half_ref[...] = x_ref[...].astype(BF16)

    gradient = lax.dot_general(
        err_ref[...], half_ref[...], (((1,), (1,)), ((), ())), preferred_element_type=F32
    )
    out_ref[...] = (f_ref[...].astype(F32) - factor_rate * gradient).astype(BF16)


def factor_step(factors, err, x, after):
    series, rank = factors.shape
    width = err.shape[1]
    rows = rows_of(series, 1024)
    return pl.pallas_call(
        factor_kernel,
        out_shape=jax.ShapeDtypeStruct((series, rank), BF16),
        grid=(series // rows,),
        in_specs=[
            pl.BlockSpec((rows, rank), lambda i: (i, 0)),
            pl.BlockSpec((rows, width), lambda i: (i, 0)),
            pl.BlockSpec((rank, width), lambda i: (0, 0)),
            pl.BlockSpec(memory_space=pl.ANY),
        ],
        out_specs=pl.BlockSpec((rows, rank), lambda i: (i, 0)),
        scratch_shapes=[pltpu.VMEM((rank, width), BF16)],
        compiler_params=params(),
        cost_estimate=cost(2 * series * width * rank, series * 3 * width * 2),
        name="factors",
    )(factors, err, x, after)


def gradient_kernel(share, count, lanes, block_index, halo_ref, turned_ref, w_ref, gd_ref, out_ref, z_ref, r_ref):
    width, rank = turned_ref.shape
    lags = list(range(1, w_ref.shape[0])) + [SEASON]
    for part in range(rank // lanes):
        columns = slice(part * lanes, (part + 1) * lanes)
        z_ref[part, :SEASON, :] = jnp.where(block_index[0] == 0, 0.0, halo_ref[:, columns])
        z_ref[part, SEASON:, :] = turned_ref[:, columns]
        resid = turned_ref[:, columns]
        for index, lag in enumerate(lags):
            begin = SEASON - lag
            resid = resid - w_ref[index : index + 1, columns] * z_ref[part, begin : begin + width, :]
        r_ref[part, :width, :] = resid
        r_ref[part, width:, :] = jnp.zeros((SEASON, lanes), F32)
        back = resid
        for index, lag in enumerate(lags):
            back = back - w_ref[index : index + 1, columns] * r_ref[part, lag : lag + width, :]
        back = back.T
        for line in range(0, lanes, share):
            which = (part * lanes + line) // share
            at = which * share
            out_ref[which] = data_scale * gd_ref[at : at + share, :] + back[line : line + share, :]


def gradient_step(block_index, halo, turned, weights, gd, count):
    rank, width = gd.shape
    share = rank // count
    lanes = 128
    return pl.pallas_call(
        functools.partial(gradient_kernel, share, count, lanes),
        out_shape=jax.ShapeDtypeStruct((count, share, width), F32),
        in_specs=[scalars()] + [whole()] * 4,
        out_specs=whole(),
        scratch_shapes=[
            pltpu.VMEM((rank // lanes, SEASON + width, lanes), F32),
            pltpu.VMEM((rank // lanes, SEASON + width, lanes), F32),
        ],
        compiler_params=params(),
        cost_estimate=cost(100 * rank * width, 4 * rank * width * 4),
        name="gradient",
    )(block_index, halo, turned, weights, gd)


def adam_kernel(count, here, grads_ref, *rest):
    early, out_ref = rest[:-1], rest[-1]
    total = [0.0, 0.0, 0.0]
    for step in range(count):
        block, first, second = [early[step][which] for which in range(3)]
        gradient = grads_ref[here[0] ^ step]
        first = beta_one * first + (1.0 - beta_one) * gradient
        second = beta_two * second + (1.0 - beta_two) * gradient * gradient
        block = block - step_rate * first / (jnp.sqrt(second) + adam_eps)
        total = [total[0] + block, total[1] + first, total[2] + second]
    for which in range(3):
        out_ref[which] = total[which] / count


def adam_step(here, grads, early):
    count, share, width = grads.shape
    return pl.pallas_call(
        functools.partial(adam_kernel, count),
        out_shape=jax.ShapeDtypeStruct((3, share, width), F32),
        in_specs=[scalars()] + [whole()] * (1 + count),
        out_specs=whole(),
        compiler_params=params(),
        cost_estimate=cost(80 * share * width, 20 * share * width * 4),
        name="adam",
    )(here, grads, *early)


def place_kernel(share, count, here, *rest):
    parts, outs, sems = rest[:count], rest[count : count + 3], rest[count + 3]
    copies = []
    for step, part in enumerate(parts):
        start = pl.multiple_of((here[0] ^ step) * share, share)
        for which in range(3):
            copies.append(
                pltpu.make_async_copy(
                    part.at[which], outs[which].at[0, pl.ds(start, share), :], sems.at[step, which]
                )
            )
    for copy in copies:
        copy.start()
    for copy in copies:
        copy.wait()


def place(here, parts):
    count = len(parts)
    _, share, width = parts[0].shape
    out = jax.ShapeDtypeStruct((1, count * share, width), F32)
    return pl.pallas_call(
        functools.partial(place_kernel, share, count),
        out_shape=(out, out, out),
        in_specs=[scalars()] + [pl.BlockSpec(memory_space=pl.ANY)] * count,
        out_specs=(far(), far(), far()),
        scratch_shapes=[pltpu.SemaphoreType.DMA((count, 3))],
        compiler_params=params(),
        cost_estimate=cost(0, 6 * count * share * width * 4),
        name="place",
    )(here, *parts)


def crossed(value, step):
    count = lax.axis_size("grp")
    return lax.ppermute(value, "grp", [(source, source ^ step) for source in range(count)])


def shifted(value, steps):
    count = lax.axis_size("blk")
    return lax.ppermute(value, "blk", [(source, (source + steps) % count) for source in range(count)])


def body(obs, mask_bits, factors, x_blocks, first_moment, second_moment, ar_weights, stratum):
    cycle = lax.axis_size("blk")
    count = lax.axis_size("grp")
    group = lax.axis_index("grp")
    block_index = (lax.axis_index("blk") + stratum[0]) % cycle
    here = group.astype(jnp.int32).reshape(1)

    tail, turned, x, own, *early = prepare(here, x_blocks, first_moment, second_moment, count)
    halo = shifted(tail, 1)
    early = [own] + [crossed(value, step + 1) for step, value in enumerate(early)]
    err, kept, gd = error_step(obs, mask_bits.T, factors, x)
    grads = gradient_step(block_index.reshape(1), halo, turned, ar_weights, gd, count)
    grads = lax.all_to_all(grads, "grp", 0, 0, tiled=True)
    means = adam_step(here, grads, early)
    moved = shifted(means, -1)
    factor_new = factor_step(kept, err, x, means)
    moved, factor_new = lax.optimization_barrier((moved, factor_new))
    span = 1
    while span < count:
        span *= 2
    level = span // 2
    known = {0: moved}
    while level >= 1:
        for key in list(known):
            known[key ^ level] = crossed(known[key], level)
        level //= 2
    parts = [known[key] for key in range(count)]
    outs = place(here, parts)
    return (factor_new, *outs)


def solution(mesh):
    rows = P(("grp", "blk"), None)
    blocks = P("grp", None, "blk")
    return jax.shard_map(
        body,
        mesh=mesh,
        in_specs=(rows, rows, rows, blocks, blocks, blocks, P(), P()),
        out_specs=(rows, blocks, blocks, blocks),
        check_vma=False,
    )
```

```python
import functools

import jax
import jax.numpy as jnp
from jax import lax
from jax.experimental import pallas as pl
from jax.experimental.pallas import tpu as pltpu
from jax.sharding import PartitionSpec as P

SEASON = 168

beta_one = 0.9
beta_two = 0.999
adam_eps = 1e-08
step_rate = 0.05
factor_rate = 0.002
data_scale = 0.25

LIMIT = 32 * 1024 * 1024
F32 = jnp.float32
BF16 = jnp.bfloat16


def whole():
    return pl.BlockSpec(memory_space=pltpu.VMEM)


def far():
    return pl.BlockSpec(memory_space=pltpu.HBM)


def held(value):
    return pltpu.with_memory_space_constraint(value, pltpu.HBM)


def scalars():
    return pl.BlockSpec(memory_space=pltpu.SMEM)


def params(**more):
    return pltpu.CompilerParams(vmem_limit_bytes=LIMIT, **more)


def cost(flops, moved):
    return pl.CostEstimate(flops=int(flops), bytes_accessed=int(moved), transcendentals=0)


def rows_of(total, most):
    best = total
    for rows in range(128, most + 1, 128):
        if total % rows == 0:
            best = rows
    return best


def prepare_kernel(share, count, x_hbm, m_hbm, v_hbm, tail_ref, turned_ref, x_ref, own_ref, *rest):
    early, (x_sem, sems) = rest[:-2], rest[-2:]
    group = lax.axis_index("grp")
    whole_copy = pltpu.make_async_copy(x_hbm.at[0], x_ref, x_sem)
    whole_copy.start()
    copies = []
    for step in range(count):
        target = own_ref if step == 0 else early[step - 1]
        start = pl.multiple_of((group ^ step) * share, share)
        for which, source in enumerate((x_hbm, m_hbm, v_hbm)):
            copies.append(
                pltpu.make_async_copy(
                    source.at[0, pl.ds(start, share), :], target.at[which], sems.at[step, which]
                )
            )
    for copy in copies:
        copy.start()
    whole_copy.wait()
    turned_ref[...] = x_ref[...].T
    tail_ref[...] = turned_ref[turned_ref.shape[0] - SEASON :, :]
    for copy in copies:
        copy.wait()


def prepare(x, m, v, count):
    rank, width = x.shape[1:]
    share = rank // count
    outs = [
        jax.ShapeDtypeStruct((SEASON, rank), F32),
        jax.ShapeDtypeStruct((width, rank), F32),
        jax.ShapeDtypeStruct((rank, width), F32),
    ]
    outs += [jax.ShapeDtypeStruct((3, share, width), F32)] * count
    return pl.pallas_call(
        functools.partial(prepare_kernel, share, count),
        out_shape=tuple(outs),
        in_specs=[far()] * 3,
        out_specs=tuple([whole()] * len(outs)),
        scratch_shapes=[pltpu.SemaphoreType.DMA(()), pltpu.SemaphoreType.DMA((count, 3))],
        compiler_params=params(),
        cost_estimate=cost(0, 6 * rank * width * 4),
        name="prepare",
    )(held(x), held(m), held(v))


def error_kernel(chunks, obs_hbm, bits_hbm, f_hbm, x_ref, err_ref, f_ref, gd_ref, obs_ref, bits_ref, sems):
    words, series = bits_ref.shape
    width = obs_ref.shape[1]
    per = width // words
    rows = series // chunks

    def copies(index):
        part = pl.ds(index * rows, rows)
        return (
            pltpu.make_async_copy(bits_hbm.at[:, part], bits_ref.at[:, part], sems.at[index, 0]),
            pltpu.make_async_copy(f_hbm.at[part, :], f_ref.at[part, :], sems.at[index, 1]),
            pltpu.make_async_copy(obs_hbm.at[part, :], obs_ref.at[part, :], sems.at[index, 2]),
        )

    for index in range(chunks):
        for copy in copies(index):
            copy.start()
    half = x_ref[...].astype(BF16)
    lane = lax.broadcasted_iota(jnp.int32, (words, width), 1)
    word = lax.broadcasted_iota(jnp.int32, (words, width), 0)
    spread = (lane // per == word).astype(BF16)
    flag = jnp.left_shift(1, lax.broadcasted_iota(jnp.int32, (1, width), 1) % per)

    def arrive(index):
        for copy in copies(index):
            copy.wait()

    def predict(index):
        part = pl.ds(index * rows, rows)
        value = lax.dot_general(
            bits_ref[:, part].astype(F32).astype(BF16),
            spread,
            (((0,), (0,)), ((), ())),
            preferred_element_type=F32,
        )
        return value, jnp.dot(f_ref[part, :], half, preferred_element_type=F32)

    def settle(index, value, predicted):
        part = pl.ds(index * rows, rows)
        error = jnp.where(
            jnp.bitwise_and(value.astype(jnp.int32), flag) != 0,
            predicted - obs_ref[part, :].astype(F32),
            0.0,
        ).astype(BF16)
        err_ref[part, :] = error
        term = lax.dot_general(
            f_ref[part, :], error, (((0,), (0,)), ((), ())), preferred_element_type=F32
        )
        if index == 0:
            gd_ref[...] = term
        else:
            gd_ref[...] += term

    arrive(0)
    ready = predict(0)
    for index in range(chunks):
        if index + 1 < chunks:
            arrive(index + 1)
            later = predict(index + 1)
        settle(index, *ready)
        ready = later


def error_step(obs, bits, factors, x):
    series, width = obs.shape
    rank = factors.shape[1]
    words = bits.shape[0]
    chunks = series // rows_of(series, 1024)
    return pl.pallas_call(
        functools.partial(error_kernel, chunks),
        out_shape=(
            jax.ShapeDtypeStruct((series, width), BF16),
            jax.ShapeDtypeStruct((series, rank), BF16),
            jax.ShapeDtypeStruct((rank, width), F32),
        ),
        in_specs=[far(), far(), far(), whole()],
        out_specs=(whole(), whole(), whole()),
        scratch_shapes=[
            pltpu.VMEM((series, width), BF16),
            pltpu.VMEM((words, series), jnp.int32),
            pltpu.SemaphoreType.DMA((chunks, 3)),
        ],
        compiler_params=params(),
        cost_estimate=cost(6 * series * width * rank, series * (3 * width * 2 + words * 4)),
        name="errors",
    )(held(obs), held(bits), held(factors), x)


def factor_kernel(begin, rows, chunks, f_ref, err_ref, turned_ref, *rest):
    out_hbm, out_ref, sems = rest[-3:]
    half = turned_ref[...].astype(BF16)
    size = rows // chunks

    def copy(index):
        return pltpu.make_async_copy(
            out_ref.at[pl.ds(index * size, size), :],
            out_hbm.at[pl.ds(begin + index * size, size), :],
            sems.at[index],
        )

    for index in range(chunks):
        part = pl.ds(begin + index * size, size)
        gradient = jnp.dot(err_ref[part, :], half, preferred_element_type=F32)
        out_ref[pl.ds(index * size, size), :] = (
            f_ref[part, :].astype(F32) - factor_rate * gradient
        ).astype(BF16)
        copy(index).start()
    for index in range(chunks):
        copy(index).wait()


def factor_step(factors, err, turned, after, sofar, begin, rows):
    series, rank = factors.shape
    width = err.shape[1]
    chunks = rows // rows_of(rows, 1024)
    rest = (after,) if sofar is None else (after, sofar)
    return pl.pallas_call(
        functools.partial(factor_kernel, begin, rows, chunks),
        out_shape=jax.ShapeDtypeStruct((series, rank), BF16),
        in_specs=[whole()] * 3 + [pl.BlockSpec(memory_space=pl.ANY)] * len(rest),
        out_specs=far(),
        input_output_aliases={} if sofar is None else {4: 0},
        scratch_shapes=[pltpu.VMEM((rows, rank), BF16), pltpu.SemaphoreType.DMA((chunks,))],
        compiler_params=params(),
        cost_estimate=cost(2 * rows * width * rank, rows * 3 * width * 2),
        name="factors",
    )(factors, err, turned, *rest)


def gradient_kernel(share, count, parts, lanes, stratum, halo_ref, turned_ref, w_ref, gd_ref, *rest):
    outs, (z_ref, r_ref) = rest[: count * parts], rest[count * parts :]
    width, rank = turned_ref.shape
    group = lax.axis_index("grp")
    block_index = lax.rem(lax.axis_index("blk") + stratum[0], lax.axis_size("blk"))
    lags = list(range(1, w_ref.shape[0])) + [SEASON]
    for part in range(rank // lanes):
        columns = slice(part * lanes, (part + 1) * lanes)
        z_ref[part, :SEASON, :] = jnp.where(block_index == 0, 0.0, halo_ref[:, columns])
        z_ref[part, SEASON:, :] = turned_ref[:, columns]
        resid = turned_ref[:, columns]
        for index, lag in enumerate(lags):
            begin = SEASON - lag
            resid = resid - w_ref[index : index + 1, columns] * z_ref[part, begin : begin + width, :]
        r_ref[part, :width, :] = resid
        r_ref[part, width:, :] = jnp.zeros((SEASON, lanes), F32)
        back = resid
        for index, lag in enumerate(lags):
            back = back - w_ref[index : index + 1, columns] * r_ref[part, lag : lag + width, :]
        rows = slice(part * lanes, (part + 1) * lanes)
        gd_ref[rows, :] = data_scale * gd_ref[rows, :] + back.T
    size = share // parts
    for step in range(count):
        start = (group ^ step) * share
        for part in range(parts):
            at = pl.multiple_of(start + part * size, size)
            outs[step * parts + part][...] = gd_ref[pl.ds(at, size), :]


def gradient_step(stratum, halo, turned, weights, gd, count, parts):
    rank, width = gd.shape
    share = rank // count
    lanes = 128
    size = share // parts

    def kernel(stratum, halo_ref, turned_ref, w_ref, gd_ref, *rest):
        work = rest[-1]
        work[...] = gd_ref[...]
        gradient_kernel(share, count, parts, lanes, stratum, halo_ref, turned_ref, w_ref, work, *rest[:-1])

    outs = pl.pallas_call(
        kernel,
        out_shape=tuple([jax.ShapeDtypeStruct((size, width), F32)] * (count * parts)),
        in_specs=[scalars()] + [whole()] * 4,
        out_specs=tuple([whole()] * (count * parts)),
        scratch_shapes=[
            pltpu.VMEM((rank // lanes, SEASON + width, lanes), F32),
            pltpu.VMEM((rank // lanes, SEASON + width, lanes), F32),
            pltpu.VMEM((rank, width), F32),
        ],
        compiler_params=params(),
        cost_estimate=cost(100 * rank * width, 4 * rank * width * 4),
        name="gradient",
    )(stratum, halo, turned, weights, gd)
    return [[outs[step * parts + part] for step in range(count)] for part in range(parts)]


def adam_kernel(part, count, *rest):
    grads, early, out_ref = rest[:count], rest[count : 2 * count], rest[2 * count]
    size = out_ref.shape[1]
    rows = slice(part * size, (part + 1) * size)
    total = [0.0, 0.0, 0.0]
    for step in range(count):
        block, first, second = [early[step][which, rows, :] for which in range(3)]
        gradient = grads[step][...]
        first = beta_one * first + (1.0 - beta_one) * gradient
        second = beta_two * second + (1.0 - beta_two) * gradient * gradient
        block = block - step_rate * first / (jnp.sqrt(second) + adam_eps)
        total = [total[0] + block, total[1] + first, total[2] + second]
    for which in range(3):
        out_ref[which] = total[which] / count


def adam_step(grads, early, part):
    count = len(grads)
    size, width = grads[0].shape
    return pl.pallas_call(
        functools.partial(adam_kernel, part, count),
        out_shape=jax.ShapeDtypeStruct((3, size, width), F32),
        in_specs=[whole()] * (2 * count),
        out_specs=whole(),
        compiler_params=params(),
        cost_estimate=cost(80 * size * width, 20 * size * width * 4),
        name="adam",
    )(*grads, *early)


def place_kernel(base, share, *rest):
    outs, sems = rest[-4:-1], rest[-1]
    count, size = sems.shape[0], rest[0].shape[1]
    group = lax.axis_index("grp")
    copies = []
    for step, part in enumerate(rest[:count]):
        start = pl.multiple_of((group ^ step) * share + base, size)
        for which in range(3):
            copies.append(
                pltpu.make_async_copy(
                    part.at[which], outs[which].at[0, pl.ds(start, size), :], sems.at[step, which]
                )
            )
    for copy in copies:
        copy.start()
    for copy in copies:
        copy.wait()


def place(parts, base, share, sofar):
    count = len(parts)
    width = parts[0].shape[2]
    out = jax.ShapeDtypeStruct((1, count * share, width), F32)
    return pl.pallas_call(
        functools.partial(place_kernel, base, share),
        out_shape=(out, out, out),
        in_specs=[pl.BlockSpec(memory_space=pl.ANY)] * (count + len(sofar)),
        out_specs=(far(), far(), far()),
        input_output_aliases={count + which: which for which in range(len(sofar))},
        scratch_shapes=[pltpu.SemaphoreType.DMA((count, 3))],
        compiler_params=params(),
        cost_estimate=cost(0, 6 * count * parts[0].size * 4),
        name="place",
    )(*parts, *sofar)


def crossed(value, step):
    count = lax.axis_size("grp")
    return lax.ppermute(value, "grp", [(source, source ^ step) for source in range(count)])


def shifted(value, steps):
    count = lax.axis_size("blk")
    return lax.ppermute(value, "blk", [(source, (source + steps) % count) for source in range(count)])


def delivered(value, step):
    groups, slots = lax.axis_size("grp"), lax.axis_size("blk")
    pairs = [
        (group * slots + slot, (group ^ step) * slots + (slot - 1) % slots)
        for group in range(groups)
        for slot in range(slots)
    ]
    return lax.ppermute(value, ("grp", "blk"), pairs)


def body(obs, mask_bits, factors, x_blocks, first_moment, second_moment, ar_weights, stratum):
    count = lax.axis_size("grp")
    pieces = 2

    tail, turned, x, own, *early = prepare(x_blocks, first_moment, second_moment, count)
    halo = shifted(tail, 1)
    early = [own] + [crossed(value, step + 1) for step, value in enumerate(early)]
    err, kept, gd = error_step(obs, mask_bits.T, factors, x)
    grads = gradient_step(stratum, halo, turned, ar_weights, gd, count, pieces)
    grads = [
        [part if step == 0 else crossed(part, step) for step, part in enumerate(row)]
        for row in grads
    ]
    series = obs.shape[0]
    third = series // 3 // 128 * 128

    factor_new = factor_step(kept, err, turned, grads[0][0], None, 0, third)
    grads[0][-1], factor_new = lax.optimization_barrier((grads[0][-1], factor_new))
    means = [adam_step(row, early, index) for index, row in enumerate(grads)]
    direct = [step for step in range(count) if step % 2 == 0]
    moved = [{step: delivered(part, step) for step in direct} for part in means]
    factor_new = factor_step(
        kept, err, turned, means[-1], factor_new, third, series - third
    )
    moved[0], factor_new = lax.optimization_barrier((moved[0], factor_new))
    share = own.shape[1]
    outs = ()
    for index, known in enumerate(moved):
        for step in direct:
            if step + 1 < count:
                known[step + 1] = crossed(known[step], 1)
        parts = [known[step] for step in range(count)]
        outs = place(parts, index * parts[0].shape[1], share, outs)
    return (factor_new, *outs)


def solution(mesh):
    rows = P(("grp", "blk"), None)
    blocks = P("grp", None, "blk")
    return jax.shard_map(
        body,
        mesh=mesh,
        in_specs=(rows, rows, rows, blocks, blocks, blocks, P(), P()),
        out_specs=(rows, blocks, blocks, blocks),
        check_vma=False,
    )
```

```python
import functools

import jax
import jax.numpy as jnp
from jax import lax
from jax.experimental import pallas as pl
from jax.experimental.pallas import tpu as pltpu
from jax.sharding import PartitionSpec as P

SEASON = 168

beta_one = 0.9
beta_two = 0.999
adam_eps = 1e-08
step_rate = 0.05
factor_rate = 0.002
data_scale = 0.25

LIMIT = 32 * 1024 * 1024
F32 = jnp.float32
BF16 = jnp.bfloat16


def whole():
    return pl.BlockSpec(memory_space=pltpu.VMEM)


def far():
    return pl.BlockSpec(memory_space=pltpu.HBM)


def held(value):
    return pltpu.with_memory_space_constraint(value, pltpu.HBM)


def scalars():
    return pl.BlockSpec(memory_space=pltpu.SMEM)


def params(**more):
    return pltpu.CompilerParams(vmem_limit_bytes=LIMIT, **more)


def cost(flops, moved):
    return pl.CostEstimate(flops=int(flops), bytes_accessed=int(moved), transcendentals=0)


def rows_of(total, most):
    best = total
    for rows in range(128, most + 1, 128):
        if total % rows == 0:
            best = rows
    return best


def prepare_kernel(x_hbm, tail_ref, turned_ref, x_ref, sem):
    copy = pltpu.make_async_copy(x_hbm.at[0], x_ref, sem)
    copy.start()
    copy.wait()
    turned_ref[...] = x_ref[...].T
    tail_ref[...] = turned_ref[turned_ref.shape[0] - SEASON :, :]


def prepare(x):
    rank, width = x.shape[1:]
    return pl.pallas_call(
        prepare_kernel,
        out_shape=(
            jax.ShapeDtypeStruct((SEASON, rank), F32),
            jax.ShapeDtypeStruct((width, rank), F32),
            jax.ShapeDtypeStruct((rank, width), F32),
        ),
        in_specs=[far()],
        out_specs=(whole(), whole(), whole()),
        scratch_shapes=[pltpu.SemaphoreType.DMA(())],
        compiler_params=params(),
        cost_estimate=cost(0, 4 * rank * width * 4),
        name="prepare",
    )(held(x))


def error_kernel(rows, obs_hbm, bits_hbm, f_hbm, x_ref, err_ref, f_ref, gd_ref, obs_ref, bits_ref, *rest):
    (value_a, value_b, predicted_a, predicted_b), sems = rest[:4], rest[4]
    words, series = bits_ref.shape
    width = obs_ref.shape[1]
    per = width // words
    chunks = series // rows

    def lines(index):
        return pl.ds(pl.multiple_of(index * rows, rows), rows)

    def copies(index):
        part = lines(index)
        return (
            pltpu.make_async_copy(bits_hbm.at[:, part], bits_ref.at[:, part], sems.at[index, 0]),
            pltpu.make_async_copy(f_hbm.at[part, :], f_ref.at[part, :], sems.at[index, 1]),
            pltpu.make_async_copy(obs_hbm.at[part, :], obs_ref.at[part, :], sems.at[index, 2]),
        )

    @pl.loop(0, chunks)
    def _(index):
        for copy in copies(index):
            copy.start()

    half = x_ref[...].astype(BF16)
    lane = lax.broadcasted_iota(jnp.int32, (words, width), 1)
    word = lax.broadcasted_iota(jnp.int32, (words, width), 0)
    spread = (lane // per == word).astype(BF16)
    flag = jnp.left_shift(1, lax.broadcasted_iota(jnp.int32, (1, width), 1) % per)
    gd_ref[...] = jnp.zeros_like(gd_ref)

    def predict(index, value_ref, predicted_ref):
        for copy in copies(index):
            copy.wait()
        part = lines(index)
        value_ref[...] = lax.dot_general(
            bits_ref[:, part].astype(F32).astype(BF16),
            spread,
            (((0,), (0,)), ((), ())),
            preferred_element_type=F32,
        )
        predicted_ref[...] = jnp.dot(f_ref[part, :], half, preferred_element_type=F32)

    def settle(index, value_ref, predicted_ref):
        part = lines(index)
        error = jnp.where(
            jnp.bitwise_and(value_ref[...].astype(jnp.int32), flag) != 0,
            predicted_ref[...] - obs_ref[part, :].astype(F32),
            0.0,
        ).astype(BF16)
        err_ref[part, :] = error
        gd_ref[...] += lax.dot_general(
            f_ref[part, :], error, (((0,), (0,)), ((), ())), preferred_element_type=F32
        )

    predict(0, value_a, predicted_a)

    @pl.loop(0, (chunks - 1) // 2)
    def _(pair):
        predict(2 * pair + 1, value_b, predicted_b)
        settle(2 * pair, value_a, predicted_a)
        predict(2 * pair + 2, value_a, predicted_a)
        settle(2 * pair + 1, value_b, predicted_b)

    if chunks % 2 == 0:
        predict(chunks - 1, value_b, predicted_b)
        settle(chunks - 2, value_a, predicted_a)
        settle(chunks - 1, value_b, predicted_b)
    else:
        settle(chunks - 1, value_a, predicted_a)


def error_step(obs, bits, factors, x):
    series, width = obs.shape
    rank = factors.shape[1]
    words = bits.shape[0]
    rows = rows_of(series, 512)
    return pl.pallas_call(
        functools.partial(error_kernel, rows),
        out_shape=(
            jax.ShapeDtypeStruct((series, width), BF16),
            jax.ShapeDtypeStruct((series, rank), BF16),
            jax.ShapeDtypeStruct((rank, width), F32),
        ),
        in_specs=[far(), far(), far(), whole()],
        out_specs=(whole(), whole(), whole()),
        scratch_shapes=[
            pltpu.VMEM((series, width), BF16),
            pltpu.VMEM((words, series), jnp.int32),
            pltpu.VMEM((rows, width), F32),
            pltpu.VMEM((rows, width), F32),
            pltpu.VMEM((rows, width), F32),
            pltpu.VMEM((rows, width), F32),
            pltpu.SemaphoreType.DMA((series // rows, 3)),
        ],
        compiler_params=params(),
        cost_estimate=cost(6 * series * width * rank, series * (3 * width * 2 + words * 4)),
        name="errors",
    )(held(obs), held(bits), held(factors), x)


def factor_kernel(begin, rows, chunks, f_ref, err_ref, turned_ref, *rest):
    out_hbm, out_ref, sems = rest[-3:]
    half = turned_ref[...].astype(BF16)
    size = rows // chunks

    def copy(index):
        return pltpu.make_async_copy(
            out_ref.at[pl.ds(index * size, size), :],
            out_hbm.at[pl.ds(begin + index * size, size), :],
            sems.at[index],
        )

    for index in range(chunks):
        part = pl.ds(begin + index * size, size)
        gradient = jnp.dot(err_ref[part, :], half, preferred_element_type=F32)
        out_ref[pl.ds(index * size, size), :] = (
            f_ref[part, :].astype(F32) - factor_rate * gradient
        ).astype(BF16)
        copy(index).start()
    for index in range(chunks):
        copy(index).wait()


def factor_step(factors, err, turned, after, sofar, begin, rows):
    series, rank = factors.shape
    width = err.shape[1]
    chunks = rows // rows_of(rows, 1024)
    rest = (after,) if sofar is None else (after, sofar)
    return pl.pallas_call(
        functools.partial(factor_kernel, begin, rows, chunks),
        out_shape=jax.ShapeDtypeStruct((series, rank), BF16),
        in_specs=[whole()] * 3 + [pl.BlockSpec(memory_space=pl.ANY)] * len(rest),
        out_specs=far(),
        input_output_aliases={} if sofar is None else {4: 0},
        scratch_shapes=[pltpu.VMEM((rows, rank), BF16), pltpu.SemaphoreType.DMA((chunks,))],
        compiler_params=params(),
        cost_estimate=cost(2 * rows * width * rank, rows * 3 * width * 2),
        name="factors",
    )(factors, err, turned, *rest)


def update_kernel(
    count, pieces, lanes, stratum, halo_ref, turned_ref, w_ref, gd_ref, x_ref, m_hbm, v_hbm, *rest
):
    outs, (z_ref, r_ref, m_ref, v_ref, new_ref, sems) = rest[: 2 * pieces], rest[2 * pieces :]
    m_copy = pltpu.make_async_copy(m_hbm.at[0], m_ref, sems.at[0])
    v_copy = pltpu.make_async_copy(v_hbm.at[0], v_ref, sems.at[1])
    m_copy.start()
    v_copy.start()
    width, rank = turned_ref.shape
    share = rank // count
    block_index = lax.rem(lax.axis_index("blk") + stratum[0], lax.axis_size("blk"))
    lags = list(range(1, w_ref.shape[0])) + [SEASON]
    for part in range(rank // lanes):
        columns = slice(part * lanes, (part + 1) * lanes)
        z_ref[part, :SEASON, :] = jnp.where(block_index == 0, 0.0, halo_ref[:, columns])
        z_ref[part, SEASON:, :] = turned_ref[:, columns]
        resid = turned_ref[:, columns]
        for index, lag in enumerate(lags):
            begin = SEASON - lag
            resid = resid - w_ref[index : index + 1, columns] * z_ref[part, begin : begin + width, :]
        r_ref[part, :width, :] = resid
        r_ref[part, width:, :] = jnp.zeros((SEASON, lanes), F32)
        back = resid
        for index, lag in enumerate(lags):
            back = back - w_ref[index : index + 1, columns] * r_ref[part, lag : lag + width, :]
        z_ref[part, :width, :] = back
    m_copy.wait()
    v_copy.wait()
    for part in range(rank // lanes):
        rows = slice(part * lanes, (part + 1) * lanes)
        gradient = data_scale * gd_ref[rows, :] + z_ref[part, :width, :].T
        first = beta_one * m_ref[rows, :] + (1.0 - beta_one) * gradient
        second = beta_two * v_ref[rows, :] + (1.0 - beta_two) * gradient * gradient
        new_ref[0, rows, :] = x_ref[rows, :] - step_rate * first / (jnp.sqrt(second) + adam_eps)
        new_ref[1, rows, :] = first
        new_ref[2, rows, :] = second
    size = share // pieces
    odd = lax.axis_index("grp") % 2
    for piece in range(pieces):
        for line in range(count // 2):
            for side in range(2):
                one = 2 * line + (odd if side == 0 else 1 - odd)
                start = pl.multiple_of(one * share + piece * size, size)
                for which in range(3):
                    outs[2 * piece + side][which, line] = new_ref[which, pl.ds(start, size), :]


def update_step(stratum, halo, turned, weights, gd, x, m, v, count, pieces):
    rank, width = gd.shape
    lanes = 128
    size = rank // count // pieces
    out = jax.ShapeDtypeStruct((3, count // 2, size, width), F32)
    outs = pl.pallas_call(
        functools.partial(update_kernel, count, pieces, lanes),
        out_shape=(out,) * (2 * pieces),
        in_specs=[scalars()] + [whole()] * 5 + [far()] * 2,
        out_specs=(whole(),) * (2 * pieces),
        scratch_shapes=[
            pltpu.VMEM((rank // lanes, SEASON + width, lanes), F32),
            pltpu.VMEM((rank // lanes, SEASON + width, lanes), F32),
            pltpu.VMEM((rank, width), F32),
            pltpu.VMEM((rank, width), F32),
            pltpu.VMEM((3, rank, width), F32),
            pltpu.SemaphoreType.DMA((2,)),
        ],
        compiler_params=params(),
        cost_estimate=cost(120 * rank * width, 10 * rank * width * 4),
        name="update",
    )(stratum, halo, turned, weights, gd, x, held(m), held(v))
    return [(outs[2 * piece], outs[2 * piece + 1]) for piece in range(pieces)]


def halve_kernel(level, kept_ref, got_ref, keep_ref, send_ref):
    mine = (lax.axis_index("grp") // level) % 2
    for line in range(keep_ref.shape[1]):
        for out, side in ((keep_ref, mine), (send_ref, 1 - mine)):
            for which in range(3):
                out[which, line] = kept_ref[which, 2 * line + side] + got_ref[which, 2 * line + side]


def halve(kept, got, level):
    _, lines, size, width = kept.shape
    out = jax.ShapeDtypeStruct((3, lines // 2, size, width), F32)
    return pl.pallas_call(
        functools.partial(halve_kernel, level),
        out_shape=(out, out),
        in_specs=[whole(), whole()],
        out_specs=(whole(), whole()),
        compiler_params=params(),
        cost_estimate=cost(kept.size, 3 * kept.size * 4),
        name="halve",
    )(kept, got)


def mean_kernel(count, kept_ref, got_ref, out_ref):
    for which in range(3):
        out_ref[which] = (kept_ref[which, 0] + got_ref[which, 0]) / count


def mean(kept, got, count):
    _, _, size, width = kept.shape
    return pl.pallas_call(
        functools.partial(mean_kernel, count),
        out_shape=jax.ShapeDtypeStruct((3, size, width), F32),
        in_specs=[whole(), whole()],
        out_specs=whole(),
        compiler_params=params(),
        cost_estimate=cost(2 * kept.size, 3 * kept.size * 4),
        name="mean",
    )(kept, got)


def place_kernel(count, share, *rest):
    parts, outs, sems = rest[:-4], rest[-4:-1], rest[-1]
    size = parts[0].shape[1]
    group = lax.axis_index("grp")
    copies = []
    for index, part in enumerate(parts):
        piece, step = divmod(index, count)
        start = pl.multiple_of((group ^ step) * share + piece * size, size)
        for which in range(3):
            copies.append(
                pltpu.make_async_copy(
                    part.at[which], outs[which].at[0, pl.ds(start, size), :], sems.at[index, which]
                )
            )
    for copy in copies:
        copy.start()
    for copy in copies:
        copy.wait()


def place(pieces):
    parts = [part for piece in pieces for part in piece]
    count = len(pieces[0])
    _, size, width = parts[0].shape
    share = size * len(pieces)
    out = jax.ShapeDtypeStruct((1, count * share, width), F32)
    return pl.pallas_call(
        functools.partial(place_kernel, count, share),
        out_shape=(out, out, out),
        in_specs=[pl.BlockSpec(memory_space=pl.ANY)] * len(parts),
        out_specs=(far(), far(), far()),
        scratch_shapes=[pltpu.SemaphoreType.DMA((len(parts), 3))],
        compiler_params=params(),
        cost_estimate=cost(0, 6 * count * share * width * 4),
        name="place",
    )(*parts)


def crossed(value, step):
    count = lax.axis_size("grp")
    return lax.ppermute(value, "grp", [(source, source ^ step) for source in range(count)])


def shifted(value, steps):
    count = lax.axis_size("blk")
    return lax.ppermute(value, "blk", [(source, (source + steps) % count) for source in range(count)])


def delivered(value, step):
    groups, slots = lax.axis_size("grp"), lax.axis_size("blk")
    pairs = [
        (group * slots + slot, (group ^ step) * slots + (slot - 1) % slots)
        for group in range(groups)
        for slot in range(slots)
    ]
    return lax.ppermute(value, ("grp", "blk"), pairs)


def body(obs, mask_bits, factors, x_blocks, first_moment, second_moment, ar_weights, stratum):
    count = lax.axis_size("grp")
    series = obs.shape[0]
    third = series // 3 // 128 * 128

    tail, turned, x = prepare(x_blocks)
    halo = shifted(tail, 1)
    err, kept, gd = error_step(obs, mask_bits.T, factors, x)
    (keep0, send0), (keep1, send1) = update_step(
        stratum, halo, turned, ar_weights, gd, x, first_moment, second_moment, count, 2
    )

    got0 = crossed(send0, 1)
    got1 = crossed(send1, 1)
    keep0, send0 = halve(keep0, got0, 2)
    far0 = crossed(send0, 2)
    factor_new = factor_step(kept, err, turned, send0, None, 0, third)
    got1, factor_new = lax.optimization_barrier((got1, factor_new))
    keep1, send1 = halve(keep1, got1, 2)
    far1 = crossed(send1, 2)
    mean0 = mean(keep0, far0, count)

    near0 = delivered(mean0, 0)
    mean1 = mean(keep1, far1, count)
    near1 = delivered(mean1, 0)
    side1 = delivered(mean1, 2)
    side0 = crossed(near0, 2)
    factor_new = factor_step(kept, err, turned, near0, factor_new, third, series - third)
    near1, side0, side1, factor_new = lax.optimization_barrier((near1, side0, side1, factor_new))
    pieces = [
        [near0, crossed(near0, 1), side0, crossed(side0, 1)],
        [near1, crossed(near1, 1), side1, crossed(side1, 1)],
    ]
    return (factor_new, *place(pieces))


def solution(mesh):
    rows = P(("grp", "blk"), None)
    blocks = P("grp", None, "blk")
    return jax.shard_map(
        body,
        mesh=mesh,
        in_specs=(rows, rows, rows, blocks, blocks, blocks, P(), P()),
        out_specs=(rows, blocks, blocks, blocks),
        check_vma=False,
    )
```

```python
import functools

import jax
import jax.numpy as jnp
from jax import lax
from jax.experimental import pallas as pl
from jax.experimental.pallas import tpu as pltpu
from jax.sharding import PartitionSpec as P

SEASON = 168

beta_one = 0.9
beta_two = 0.999
adam_eps = 1e-08
step_rate = 0.05
factor_rate = 0.002
data_scale = 0.25

LIMIT = 32 * 1024 * 1024
F32 = jnp.float32
BF16 = jnp.bfloat16


def whole():
    return pl.BlockSpec(memory_space=pltpu.VMEM)


def far():
    return pl.BlockSpec(memory_space=pltpu.HBM)


def held(value):
    return pltpu.with_memory_space_constraint(value, pltpu.HBM)


def scalars():
    return pl.BlockSpec(memory_space=pltpu.SMEM)


def params(**more):
    return pltpu.CompilerParams(vmem_limit_bytes=LIMIT, **more)


def cost(flops, moved):
    return pl.CostEstimate(flops=int(flops), bytes_accessed=int(moved), transcendentals=0)


def rows_of(total, most):
    best = total
    for rows in range(128, most + 1, 128):
        if total % rows == 0:
            best = rows
    return best


def prepare_kernel(x_hbm, tail_ref, turned_ref, x_ref, sem):
    copy = pltpu.make_async_copy(x_hbm.at[0], x_ref, sem)
    copy.start()
    copy.wait()
    turned_ref[...] = x_ref[...].T
    tail_ref[...] = turned_ref[turned_ref.shape[0] - SEASON :, :]


def prepare(x):
    rank, width = x.shape[1:]
    return pl.pallas_call(
        prepare_kernel,
        out_shape=(
            jax.ShapeDtypeStruct((SEASON, rank), F32),
            jax.ShapeDtypeStruct((width, rank), F32),
            jax.ShapeDtypeStruct((rank, width), F32),
        ),
        in_specs=[far()],
        out_specs=(whole(), whole(), whole()),
        scratch_shapes=[pltpu.SemaphoreType.DMA(())],
        compiler_params=params(),
        cost_estimate=cost(0, 4 * rank * width * 4),
        name="prepare",
    )(held(x))


def error_kernel(rows, obs_hbm, bits_hbm, f_hbm, turned_ref, err_ref, both_ref, gd_ref, bits_ref, sems):
    width, series = err_ref.shape
    rank = turned_ref.shape[1]
    words = bits_ref.shape[0]
    per = width // words
    chunks = series // rows

    def copies(index):
        part = pl.ds(index * rows, rows)
        return (
            pltpu.make_async_copy(bits_hbm.at[:, part], bits_ref.at[:, part], sems.at[index, 0]),
            pltpu.make_async_copy(
                f_hbm.at[part, :], both_ref.at[part, pl.ds(0, rank)], sems.at[index, 1]
            ),
            pltpu.make_async_copy(
                obs_hbm.at[part, :], both_ref.at[part, pl.ds(rank, width)], sems.at[index, 2]
            ),
        )

    for index in range(chunks):
        for copy in copies(index):
            copy.start()
    row = lax.broadcasted_iota(jnp.int32, (width, width), 0)
    column = lax.broadcasted_iota(jnp.int32, (width, width), 1)
    weights = jnp.concatenate(
        [turned_ref[...].astype(BF16), jnp.where(row == column, -1.0, 0.0).astype(BF16)], axis=1
    )
    flag = jnp.left_shift(1, lax.broadcasted_iota(jnp.int32, (1, per, 1), 1))

    def compare(index):
        for copy in copies(index):
            copy.wait()
        part = pl.ds(index * rows, rows)
        return lax.dot_general(
            weights, both_ref[part, :], (((1,), (1,)), ((), ())), preferred_element_type=F32
        )

    def settle(index, gap):
        part = pl.ds(index * rows, rows)
        seen = jnp.bitwise_and(bits_ref[:, part][:, None, :], flag) != 0
        error = jnp.where(seen, gap.reshape(words, per, rows), 0.0).reshape(width, rows)
        error = error.astype(BF16)
        err_ref[:, part] = error
        term = jnp.dot(error, both_ref[part, pl.ds(0, rank)], preferred_element_type=F32)
        if index == 0:
            gd_ref[...] = term
        else:
            gd_ref[...] += term

    gap = compare(0)
    for index in range(chunks):
        later = compare(index + 1) if index + 1 < chunks else None
        settle(index, gap)
        gap = later


def error_step(obs, bits, factors, turned):
    series, width = obs.shape
    rank = factors.shape[1]
    words = bits.shape[0]
    rows = rows_of(series, 1024)
    return pl.pallas_call(
        functools.partial(error_kernel, rows),
        out_shape=(
            jax.ShapeDtypeStruct((width, series), BF16),
            jax.ShapeDtypeStruct((series, rank + width), BF16),
            jax.ShapeDtypeStruct((width, rank), F32),
        ),
        in_specs=[far(), far(), far(), whole()],
        out_specs=(whole(), whole(), whole()),
        scratch_shapes=[
            pltpu.VMEM((words, series), jnp.int32),
            pltpu.SemaphoreType.DMA((series // rows, 3)),
        ],
        compiler_params=params(),
        cost_estimate=cost(8 * series * width * rank, series * (3 * width * 2 + words * 4)),
        name="errors",
    )(held(obs), held(bits), held(factors), turned)


def factor_kernel(begin, rows, chunks, both_ref, err_ref, turned_ref, *rest):
    out_hbm, out_ref, sems = rest[-3:]
    half = turned_ref[...].astype(BF16)
    size = rows // chunks

    def copy(index):
        return pltpu.make_async_copy(
            out_ref.at[pl.ds(index * size, size), :],
            out_hbm.at[pl.ds(begin + index * size, size), :],
            sems.at[index],
        )

    for index in range(chunks):
        part = pl.ds(begin + index * size, size)
        gradient = lax.dot_general(
            err_ref[:, part], half, (((0,), (0,)), ((), ())), preferred_element_type=F32
        )
        out_ref[pl.ds(index * size, size), :] = (
            both_ref[part, pl.ds(0, half.shape[1])].astype(F32) - factor_rate * gradient
        ).astype(BF16)
        copy(index).start()
    for index in range(chunks):
        copy(index).wait()


def factor_step(both, err, turned, after, sofar, begin, rows):
    width, series = err.shape
    rank = turned.shape[1]
    chunks = rows // rows_of(rows, 1024)
    rest = (after,) if sofar is None else (after, sofar)
    return pl.pallas_call(
        functools.partial(factor_kernel, begin, rows, chunks),
        out_shape=jax.ShapeDtypeStruct((series, rank), BF16),
        in_specs=[whole()] * 3 + [pl.BlockSpec(memory_space=pl.ANY)] * len(rest),
        out_specs=far(),
        input_output_aliases={} if sofar is None else {4: 0},
        scratch_shapes=[pltpu.VMEM((rows, rank), BF16), pltpu.SemaphoreType.DMA((chunks,))],
        compiler_params=params(),
        cost_estimate=cost(2 * rows * width * rank, rows * 3 * width * 2),
        name="factors",
    )(both, err, turned, *rest)


def update_kernel(
    count, pieces, lanes, stratum_ref, halo_ref, turned_ref, w_ref, gd_ref, x_ref, m_hbm, v_hbm, *rest
):
    outs, scratch = rest[: 2 * pieces], rest[2 * pieces :]
    z_ref, r_ref, m_ref, v_ref, new_ref, sems = scratch
    m_copy = pltpu.make_async_copy(m_hbm.at[0], m_ref, sems.at[0])
    v_copy = pltpu.make_async_copy(v_hbm.at[0], v_ref, sems.at[1])
    m_copy.start()
    v_copy.start()
    width, rank = turned_ref.shape
    share = rank // count
    block_index = lax.rem(lax.axis_index("blk") + stratum_ref[...], lax.axis_size("blk"))
    lags = list(range(1, w_ref.shape[0])) + [SEASON]
    for part in range(rank // lanes):
        columns = slice(part * lanes, (part + 1) * lanes)
        z_ref[part, :SEASON, :] = jnp.where(block_index == 0, 0.0, halo_ref[:, columns])
        z_ref[part, SEASON:, :] = turned_ref[:, columns]
        resid = turned_ref[:, columns]
        for index, lag in enumerate(lags):
            begin = SEASON - lag
            resid = resid - w_ref[index : index + 1, columns] * z_ref[part, begin : begin + width, :]
        r_ref[part, :width, :] = resid
        r_ref[part, width:, :] = jnp.zeros((SEASON, lanes), F32)
        back = resid
        for index, lag in enumerate(lags):
            back = back - w_ref[index : index + 1, columns] * r_ref[part, lag : lag + width, :]
        z_ref[part, :width, :] = data_scale * gd_ref[:, columns] + back
    m_copy.wait()
    v_copy.wait()
    for part in range(rank // lanes):
        rows = slice(part * lanes, (part + 1) * lanes)
        gradient = z_ref[part, :width, :].T
        first = beta_one * m_ref[rows, :] + (1.0 - beta_one) * gradient
        second = beta_two * v_ref[rows, :] + (1.0 - beta_two) * gradient * gradient
        new_ref[0, rows, :] = x_ref[rows, :] - step_rate * first / (jnp.sqrt(second) + adam_eps)
        new_ref[1, rows, :] = first
        new_ref[2, rows, :] = second
    size = share // pieces
    odd = lax.axis_index("grp") % 2
    for piece in range(pieces):
        for line in range(count // 2):
            for side in range(2):
                one = 2 * line + (odd if side == 0 else 1 - odd)
                start = pl.multiple_of(one * share + piece * size, size)
                for which in range(3):
                    outs[2 * piece + side][which, line] = new_ref[which, pl.ds(start, size), :]


def update_step(stratum, halo, turned, weights, gd, x, m, v, count, pieces):
    width, rank = gd.shape
    lanes = 128
    size = rank // count // pieces
    out = jax.ShapeDtypeStruct((3, count // 2, size, width), F32)
    outs = pl.pallas_call(
        functools.partial(update_kernel, count, pieces, lanes),
        out_shape=(out,) * (2 * pieces),
        in_specs=[whole()] * 6 + [far()] * 2,
        out_specs=(whole(),) * (2 * pieces),
        scratch_shapes=[
            pltpu.VMEM((rank // lanes, SEASON + width, lanes), F32),
            pltpu.VMEM((rank // lanes, SEASON + width, lanes), F32),
            pltpu.VMEM((rank, width), F32),
            pltpu.VMEM((rank, width), F32),
            pltpu.VMEM((3, rank, width), F32),
            pltpu.SemaphoreType.DMA((2,)),
        ],
        compiler_params=params(),
        cost_estimate=cost(120 * rank * width, 10 * rank * width * 4),
        name="update",
    )(stratum.reshape(1, 1), halo, turned, weights, gd, x, held(m), held(v))
    return [(outs[2 * piece], outs[2 * piece + 1]) for piece in range(pieces)]


def halve_kernel(level, kept_ref, got_ref, keep_ref, send_ref):
    mine = (lax.axis_index("grp") // level) % 2
    for line in range(keep_ref.shape[1]):
        for out, side in ((keep_ref, mine), (send_ref, 1 - mine)):
            for which in range(3):
                out[which, line] = kept_ref[which, 2 * line + side] + got_ref[which, 2 * line + side]


def halve(kept, got, level):
    _, lines, size, width = kept.shape
    out = jax.ShapeDtypeStruct((3, lines // 2, size, width), F32)
    return pl.pallas_call(
        functools.partial(halve_kernel, level),
        out_shape=(out, out),
        in_specs=[whole(), whole()],
        out_specs=(whole(), whole()),
        compiler_params=params(),
        cost_estimate=cost(kept.size, 3 * kept.size * 4),
        name="halve",
    )(kept, got)


def mean_kernel(count, kept_ref, got_ref, out_ref):
    for which in range(3):
        out_ref[which] = (kept_ref[which, 0] + got_ref[which, 0]) / count


def mean(kept, got, count):
    _, _, size, width = kept.shape
    return pl.pallas_call(
        functools.partial(mean_kernel, count),
        out_shape=jax.ShapeDtypeStruct((3, size, width), F32),
        in_specs=[whole(), whole()],
        out_specs=whole(),
        compiler_params=params(),
        cost_estimate=cost(2 * kept.size, 3 * kept.size * 4),
        name="mean",
    )(kept, got)


def place_kernel(count, share, *rest):
    parts, outs, sems = rest[:-4], rest[-4:-1], rest[-1]
    size = parts[0].shape[1]
    group = lax.axis_index("grp")
    copies = []
    for index, part in enumerate(parts):
        piece, step = divmod(index, count)
        start = pl.multiple_of((group ^ step) * share + piece * size, size)
        for which in range(3):
            copies.append(
                pltpu.make_async_copy(
                    part.at[which], outs[which].at[0, pl.ds(start, size), :], sems.at[index, which]
                )
            )
    for copy in copies:
        copy.start()
    for copy in copies:
        copy.wait()


def place(pieces):
    parts = [part for piece in pieces for part in piece]
    count = len(pieces[0])
    _, size, width = parts[0].shape
    share = size * len(pieces)
    out = jax.ShapeDtypeStruct((1, count * share, width), F32)
    return pl.pallas_call(
        functools.partial(place_kernel, count, share),
        out_shape=(out, out, out),
        in_specs=[pl.BlockSpec(memory_space=pl.ANY)] * len(parts),
        out_specs=(far(), far(), far()),
        scratch_shapes=[pltpu.SemaphoreType.DMA((len(parts), 3))],
        compiler_params=params(),
        cost_estimate=cost(0, 6 * count * share * width * 4),
        name="place",
    )(*parts)


def crossed(value, step):
    count = lax.axis_size("grp")
    return lax.ppermute(value, "grp", [(source, source ^ step) for source in range(count)])


def shifted(value, steps):
    count = lax.axis_size("blk")
    return lax.ppermute(value, "blk", [(source, (source + steps) % count) for source in range(count)])


def delivered(value, step):
    groups, slots = lax.axis_size("grp"), lax.axis_size("blk")
    pairs = [
        (group * slots + slot, (group ^ step) * slots + (slot - 1) % slots)
        for group in range(groups)
        for slot in range(slots)
    ]
    return lax.ppermute(value, ("grp", "blk"), pairs)


def body(obs, mask_bits, factors, x_blocks, first_moment, second_moment, ar_weights, stratum):
    count = lax.axis_size("grp")
    series = obs.shape[0]
    third = series // 3 // 128 * 128

    tail, turned, x = prepare(x_blocks)
    halo = shifted(tail, 1)
    err, kept, gd = error_step(obs, mask_bits.T, factors, turned)
    (keep0, send0), (keep1, send1) = update_step(
        stratum, halo, turned, ar_weights, gd, x, first_moment, second_moment, count, 2
    )

    got0 = crossed(send0, 1)
    got1 = crossed(send1, 1)
    keep0, send0 = halve(keep0, got0, 2)
    far0 = crossed(send0, 2)
    factor_new = factor_step(kept, err, turned, send0, None, 0, third)
    got1, factor_new = lax.optimization_barrier((got1, factor_new))
    keep1, send1 = halve(keep1, got1, 2)
    far1 = crossed(send1, 2)
    mean0 = mean(keep0, far0, count)

    near0 = delivered(mean0, 0)
    mean1 = mean(keep1, far1, count)
    near1 = delivered(mean1, 0)
    side0 = crossed(near0, 2)
    mean1, _ = lax.optimization_barrier((mean1, near0))
    side1 = delivered(mean1, 2)
    factor_new = factor_step(kept, err, turned, near0, factor_new, third, series - third)
    near1, factor_new = lax.optimization_barrier((near1, factor_new))
    pieces = [
        [near0, crossed(near0, 1), side0, crossed(side0, 1)],
        [near1, crossed(near1, 1), side1, crossed(side1, 1)],
    ]
    return (factor_new, *place(pieces))


def solution(mesh):
    rows = P(("grp", "blk"), None)
    blocks = P("grp", None, "blk")
    return jax.shard_map(
        body,
        mesh=mesh,
        in_specs=(rows, rows, rows, blocks, blocks, blocks, P(), P()),
        out_specs=(rows, blocks, blocks, blocks),
        check_vma=False,
    )
```

```python
import functools

import jax
import jax.numpy as jnp
from jax import lax
from jax.experimental import pallas as pl
from jax.experimental.pallas import tpu as pltpu
from jax.sharding import PartitionSpec as P

SEASON = 168

beta_one = 0.9
beta_two = 0.999
adam_eps = 1e-08
step_rate = 0.05
factor_rate = 0.002
data_scale = 0.25

LIMIT = 32 * 1024 * 1024
F32 = jnp.float32
BF16 = jnp.bfloat16


def whole():
    return pl.BlockSpec(memory_space=pltpu.VMEM)


def far():
    return pl.BlockSpec(memory_space=pltpu.HBM)


def held(value):
    return pltpu.with_memory_space_constraint(value, pltpu.HBM)


def scalars():
    return pl.BlockSpec(memory_space=pltpu.SMEM)


def params(**more):
    return pltpu.CompilerParams(vmem_limit_bytes=LIMIT, **more)


def cost(flops, moved):
    return pl.CostEstimate(flops=int(flops), bytes_accessed=int(moved), transcendentals=0)


def rows_of(total, most):
    best = total
    for rows in range(128, most + 1, 128):
        if total % rows == 0:
            best = rows
    return best


def prepare_kernel(x_hbm, tail_ref, turned_ref, x_ref, sem):
    copy = pltpu.make_async_copy(x_hbm.at[0], x_ref, sem)
    copy.start()
    copy.wait()
    turned_ref[...] = x_ref[...].T
    tail_ref[...] = turned_ref[turned_ref.shape[0] - SEASON :, :]


def prepare(x):
    rank, width = x.shape[1:]
    return pl.pallas_call(
        prepare_kernel,
        out_shape=(
            jax.ShapeDtypeStruct((SEASON, rank), F32),
            jax.ShapeDtypeStruct((width, rank), F32),
            jax.ShapeDtypeStruct((rank, width), F32),
        ),
        in_specs=[far()],
        out_specs=(whole(), whole(), whole()),
        scratch_shapes=[pltpu.SemaphoreType.DMA(())],
        compiler_params=params(),
        cost_estimate=cost(0, 4 * rank * width * 4),
        name="prepare",
    )(held(x))


def error_kernel(rows, obs_hbm, bits_hbm, f_hbm, turned_ref, err_ref, both_ref, gd_ref, bits_ref, sems):
    width, series = err_ref.shape
    rank = turned_ref.shape[1]
    words = bits_ref.shape[0]
    per = width // words
    chunks = series // rows

    def copies(index):
        part = pl.ds(index * rows, rows)
        return (
            pltpu.make_async_copy(bits_hbm.at[:, part], bits_ref.at[:, part], sems.at[index, 0]),
            pltpu.make_async_copy(
                f_hbm.at[part, :], both_ref.at[part, pl.ds(0, rank)], sems.at[index, 1]
            ),
            pltpu.make_async_copy(
                obs_hbm.at[part, :], both_ref.at[part, pl.ds(rank, width)], sems.at[index, 2]
            ),
        )

    ahead = 3
    for index in range(min(ahead, chunks)):
        for copy in copies(index):
            copy.start()
    row = lax.broadcasted_iota(jnp.int32, (width, width), 0)
    column = lax.broadcasted_iota(jnp.int32, (width, width), 1)
    weights = jnp.concatenate(
        [turned_ref[...].astype(BF16), jnp.where(row == column, -1.0, 0.0).astype(BF16)], axis=1
    )
    flag = jnp.left_shift(1, lax.broadcasted_iota(jnp.int32, (1, per, 1), 1))

    def compare(index):
        for copy in copies(index):
            copy.wait()
        if index + ahead < chunks:
            for copy in copies(index + ahead):
                copy.start()
        part = pl.ds(index * rows, rows)
        return lax.dot_general(
            weights, both_ref[part, :], (((1,), (1,)), ((), ())), preferred_element_type=F32
        )

    def settle(index, gap):
        part = pl.ds(index * rows, rows)
        seen = jnp.bitwise_and(bits_ref[:, part][:, None, :], flag) != 0
        error = jnp.where(seen, gap.reshape(words, per, rows), 0.0).reshape(width, rows)
        error = error.astype(BF16)
        err_ref[:, part] = error
        term = jnp.dot(error, both_ref[part, pl.ds(0, rank)], preferred_element_type=F32)
        if index == 0:
            gd_ref[...] = term
        else:
            gd_ref[...] += term

    gap = compare(0)
    for index in range(chunks):
        later = compare(index + 1) if index + 1 < chunks else None
        settle(index, gap)
        gap = later


def error_step(obs, bits, factors, turned):
    series, width = obs.shape
    rank = factors.shape[1]
    words = bits.shape[0]
    rows = rows_of(series, 1024)
    return pl.pallas_call(
        functools.partial(error_kernel, rows),
        out_shape=(
            jax.ShapeDtypeStruct((width, series), BF16),
            jax.ShapeDtypeStruct((series, rank + width), BF16),
            jax.ShapeDtypeStruct((width, rank), F32),
        ),
        in_specs=[far(), far(), far(), whole()],
        out_specs=(whole(), whole(), whole()),
        scratch_shapes=[
            pltpu.VMEM((words, series), jnp.int32),
            pltpu.SemaphoreType.DMA((series // rows, 3)),
        ],
        compiler_params=params(),
        cost_estimate=cost(8 * series * width * rank, series * (3 * width * 2 + words * 4)),
        name="errors",
    )(held(obs), held(bits), held(factors), turned)


def factor_kernel(begin, rows, chunks, both_ref, err_ref, turned_ref, *rest):
    out_hbm, out_ref, sems = rest[-3:]
    half = turned_ref[...].astype(BF16)
    size = rows // chunks

    def copy(index):
        return pltpu.make_async_copy(
            out_ref.at[pl.ds(index * size, size), :],
            out_hbm.at[pl.ds(begin + index * size, size), :],
            sems.at[index],
        )

    for index in range(chunks):
        part = pl.ds(begin + index * size, size)
        gradient = lax.dot_general(
            err_ref[:, part], half, (((0,), (0,)), ((), ())), preferred_element_type=F32
        )
        out_ref[pl.ds(index * size, size), :] = (
            both_ref[part, pl.ds(0, half.shape[1])].astype(F32) - factor_rate * gradient
        ).astype(BF16)
        copy(index).start()
    for index in range(chunks):
        copy(index).wait()


def factor_step(both, err, turned, after, sofar, begin, rows):
    width, series = err.shape
    rank = turned.shape[1]
    chunks = rows // rows_of(rows, 1024)
    rest = (after,) if sofar is None else (after, sofar)
    return pl.pallas_call(
        functools.partial(factor_kernel, begin, rows, chunks),
        out_shape=jax.ShapeDtypeStruct((series, rank), BF16),
        in_specs=[whole()] * 3 + [pl.BlockSpec(memory_space=pl.ANY)] * len(rest),
        out_specs=far(),
        input_output_aliases={} if sofar is None else {4: 0},
        scratch_shapes=[pltpu.VMEM((rows, rank), BF16), pltpu.SemaphoreType.DMA((chunks,))],
        compiler_params=params(),
        cost_estimate=cost(2 * rows * width * rank, rows * 3 * width * 2),
        name="factors",
    )(both, err, turned, *rest)


def update_kernel(
    count, pieces, lanes, stratum_ref, halo_ref, turned_ref, w_ref, gd_ref, x_ref, m_hbm, v_hbm, *rest
):
    outs, scratch = rest[: 2 * pieces], rest[2 * pieces :]
    z_ref, r_ref, m_ref, v_ref, new_ref, sems = scratch
    m_copy = pltpu.make_async_copy(m_hbm.at[0], m_ref, sems.at[0])
    v_copy = pltpu.make_async_copy(v_hbm.at[0], v_ref, sems.at[1])
    m_copy.start()
    v_copy.start()
    width, rank = turned_ref.shape
    share = rank // count
    block_index = lax.rem(lax.axis_index("blk") + stratum_ref[...], lax.axis_size("blk"))
    lags = list(range(1, w_ref.shape[0])) + [SEASON]
    for part in range(rank // lanes):
        columns = slice(part * lanes, (part + 1) * lanes)
        z_ref[part, :SEASON, :] = jnp.where(block_index == 0, 0.0, halo_ref[:, columns])
        z_ref[part, SEASON:, :] = turned_ref[:, columns]
        resid = turned_ref[:, columns]
        for index, lag in enumerate(lags):
            begin = SEASON - lag
            resid = resid - w_ref[index : index + 1, columns] * z_ref[part, begin : begin + width, :]
        r_ref[part, :width, :] = resid
        r_ref[part, width:, :] = jnp.zeros((SEASON, lanes), F32)
        back = resid
        for index, lag in enumerate(lags):
            back = back - w_ref[index : index + 1, columns] * r_ref[part, lag : lag + width, :]
        z_ref[part, :width, :] = data_scale * gd_ref[:, columns] + back
    m_copy.wait()
    v_copy.wait()
    for part in range(rank // lanes):
        rows = slice(part * lanes, (part + 1) * lanes)
        gradient = z_ref[part, :width, :].T
        first = beta_one * m_ref[rows, :] + (1.0 - beta_one) * gradient
        second = beta_two * v_ref[rows, :] + (1.0 - beta_two) * gradient * gradient
        new_ref[0, rows, :] = x_ref[rows, :] - step_rate * first / (jnp.sqrt(second) + adam_eps)
        new_ref[1, rows, :] = first
        new_ref[2, rows, :] = second
    size = share // pieces
    odd = lax.axis_index("grp") % 2
    for piece in range(pieces):
        for line in range(count // 2):
            for side in range(2):
                one = 2 * line + (odd if side == 0 else 1 - odd)
                start = pl.multiple_of(one * share + piece * size, size)
                for which in range(3):
                    outs[2 * piece + side][which, line] = new_ref[which, pl.ds(start, size), :]


def update_step(stratum, halo, turned, weights, gd, x, m, v, count, pieces):
    width, rank = gd.shape
    lanes = 128
    size = rank // count // pieces
    out = jax.ShapeDtypeStruct((3, count // 2, size, width), F32)
    outs = pl.pallas_call(
        functools.partial(update_kernel, count, pieces, lanes),
        out_shape=(out,) * (2 * pieces),
        in_specs=[whole()] * 6 + [far()] * 2,
        out_specs=(whole(),) * (2 * pieces),
        scratch_shapes=[
            pltpu.VMEM((rank // lanes, SEASON + width, lanes), F32),
            pltpu.VMEM((rank // lanes, SEASON + width, lanes), F32),
            pltpu.VMEM((rank, width), F32),
            pltpu.VMEM((rank, width), F32),
            pltpu.VMEM((3, rank, width), F32),
            pltpu.SemaphoreType.DMA((2,)),
        ],
        compiler_params=params(),
        cost_estimate=cost(120 * rank * width, 10 * rank * width * 4),
        name="update",
    )(stratum.reshape(1, 1), halo, turned, weights, gd, x, held(m), held(v))
    return [(outs[2 * piece], outs[2 * piece + 1]) for piece in range(pieces)]


def halve_kernel(level, kept_ref, got_ref, keep_ref, send_ref):
    mine = (lax.axis_index("grp") // level) % 2
    for line in range(keep_ref.shape[1]):
        for out, side in ((keep_ref, mine), (send_ref, 1 - mine)):
            for which in range(3):
                out[which, line] = kept_ref[which, 2 * line + side] + got_ref[which, 2 * line + side]


def halve(kept, got, level):
    _, lines, size, width = kept.shape
    out = jax.ShapeDtypeStruct((3, lines // 2, size, width), F32)
    return pl.pallas_call(
        functools.partial(halve_kernel, level),
        out_shape=(out, out),
        in_specs=[whole(), whole()],
        out_specs=(whole(), whole()),
        compiler_params=params(),
        cost_estimate=cost(kept.size, 3 * kept.size * 4),
        name="halve",
    )(kept, got)


def mean_kernel(count, kept_ref, got_ref, out_ref):
    for which in range(3):
        out_ref[which] = (kept_ref[which, 0] + got_ref[which, 0]) / count


def mean(kept, got, count):
    _, _, size, width = kept.shape
    return pl.pallas_call(
        functools.partial(mean_kernel, count),
        out_shape=jax.ShapeDtypeStruct((3, size, width), F32),
        in_specs=[whole(), whole()],
        out_specs=whole(),
        compiler_params=params(),
        cost_estimate=cost(2 * kept.size, 3 * kept.size * 4),
        name="mean",
    )(kept, got)


def place_kernel(count, share, *rest):
    parts, outs, sems = rest[:-4], rest[-4:-1], rest[-1]
    size = parts[0].shape[1]
    group = lax.axis_index("grp")
    copies = []
    for index, part in enumerate(parts):
        piece, step = divmod(index, count)
        start = pl.multiple_of((group ^ step) * share + piece * size, size)
        for which in range(3):
            copies.append(
                pltpu.make_async_copy(
                    part.at[which], outs[which].at[0, pl.ds(start, size), :], sems.at[index, which]
                )
            )
    for copy in copies:
        copy.start()
    for copy in copies:
        copy.wait()


def place(pieces):
    parts = [part for piece in pieces for part in piece]
    count = len(pieces[0])
    _, size, width = parts[0].shape
    share = size * len(pieces)
    out = jax.ShapeDtypeStruct((1, count * share, width), F32)
    return pl.pallas_call(
        functools.partial(place_kernel, count, share),
        out_shape=(out, out, out),
        in_specs=[pl.BlockSpec(memory_space=pl.ANY)] * len(parts),
        out_specs=(far(), far(), far()),
        scratch_shapes=[pltpu.SemaphoreType.DMA((len(parts), 3))],
        compiler_params=params(),
        cost_estimate=cost(0, 6 * count * share * width * 4),
        name="place",
    )(*parts)


def crossed(value, step):
    count = lax.axis_size("grp")
    return lax.ppermute(value, "grp", [(source, source ^ step) for source in range(count)])


def shifted(value, steps):
    count = lax.axis_size("blk")
    return lax.ppermute(value, "blk", [(source, (source + steps) % count) for source in range(count)])


def delivered(value, step):
    groups, slots = lax.axis_size("grp"), lax.axis_size("blk")
    pairs = [
        (group * slots + slot, (group ^ step) * slots + (slot - 1) % slots)
        for group in range(groups)
        for slot in range(slots)
    ]
    return lax.ppermute(value, ("grp", "blk"), pairs)


def body(obs, mask_bits, factors, x_blocks, first_moment, second_moment, ar_weights, stratum):
    count = lax.axis_size("grp")
    series = obs.shape[0]
    third = series // 3 // 128 * 128

    tail, turned, x = prepare(x_blocks)
    halo = shifted(tail, 1)
    err, kept, gd = error_step(obs, mask_bits.T, factors, turned)
    (keep0, send0), (keep1, send1) = update_step(
        stratum, halo, turned, ar_weights, gd, x, first_moment, second_moment, count, 2
    )

    got0 = crossed(send0, 1)
    got1 = crossed(send1, 1)
    keep0, send0 = halve(keep0, got0, 2)
    far0 = crossed(send0, 2)
    factor_new = factor_step(kept, err, turned, send0, None, 0, third)
    got1, factor_new = lax.optimization_barrier((got1, factor_new))
    keep1, send1 = halve(keep1, got1, 2)
    far1 = crossed(send1, 2)
    mean0 = mean(keep0, far0, count)

    near0 = delivered(mean0, 0)
    mean1 = mean(keep1, far1, count)
    near1 = delivered(mean1, 0)
    side0 = crossed(near0, 2)
    factor_new = factor_step(kept, err, turned, near0, factor_new, third, series - third)
    near1, side0, factor_new = lax.optimization_barrier((near1, side0, factor_new))
    side1 = crossed(near1, 2)
    pieces = [
        [near0, crossed(near0, 1), side0, crossed(side0, 1)],
        [near1, crossed(near1, 1), side1, crossed(side1, 1)],
    ]
    return (factor_new, *place(pieces))


def solution(mesh):
    rows = P(("grp", "blk"), None)
    blocks = P("grp", None, "blk")
    return jax.shard_map(
        body,
        mesh=mesh,
        in_specs=(rows, rows, rows, blocks, blocks, blocks, P(), P()),
        out_specs=(rows, blocks, blocks, blocks),
        check_vma=False,
    )
```

```python
import functools

import jax
import jax.numpy as jnp
from jax import lax
from jax.experimental import pallas as pl
from jax.experimental.pallas import tpu as pltpu
from jax.sharding import PartitionSpec as P

SEASON = 168

beta_one = 0.9
beta_two = 0.999
adam_eps = 1e-08
step_rate = 0.05
factor_rate = 0.002
data_scale = 0.25

LIMIT = 32 * 1024 * 1024
F32 = jnp.float32
BF16 = jnp.bfloat16


def whole():
    return pl.BlockSpec(memory_space=pltpu.VMEM)


def far():
    return pl.BlockSpec(memory_space=pltpu.HBM)


def held(value):
    return pltpu.with_memory_space_constraint(value, pltpu.HBM)


def scalars():
    return pl.BlockSpec(memory_space=pltpu.SMEM)


def params(**more):
    return pltpu.CompilerParams(vmem_limit_bytes=LIMIT, **more)


def cost(flops, moved):
    return pl.CostEstimate(flops=int(flops), bytes_accessed=int(moved), transcendentals=0)


def rows_of(total, most):
    best = total
    for rows in range(128, most + 1, 128):
        if total % rows == 0:
            best = rows
    return best


def prepare_kernel(x_hbm, tail_ref, turned_ref, x_ref, sem):
    copy = pltpu.make_async_copy(x_hbm.at[0], x_ref, sem)
    copy.start()
    copy.wait()
    turned_ref[...] = x_ref[...].T
    tail_ref[...] = turned_ref[turned_ref.shape[0] - SEASON :, :]


def prepare(x):
    rank, width = x.shape[1:]
    return pl.pallas_call(
        prepare_kernel,
        out_shape=(
            jax.ShapeDtypeStruct((SEASON, rank), F32),
            jax.ShapeDtypeStruct((width, rank), F32),
            jax.ShapeDtypeStruct((rank, width), F32),
        ),
        in_specs=[far()],
        out_specs=(whole(), whole(), whole()),
        scratch_shapes=[pltpu.SemaphoreType.DMA(())],
        compiler_params=params(),
        cost_estimate=cost(0, 4 * rank * width * 4),
        name="prepare",
    )(held(x))


def error_kernel(rows, obs_hbm, bits_hbm, f_hbm, turned_ref, err_ref, both_ref, gd_ref, bits_ref, sems):
    width, series = err_ref.shape
    rank = turned_ref.shape[1]
    words = bits_ref.shape[0]
    per = width // words
    chunks = series // rows

    def copies(index):
        part = pl.ds(index * rows, rows)
        return (
            pltpu.make_async_copy(bits_hbm.at[:, part], bits_ref.at[:, part], sems.at[index, 0]),
            pltpu.make_async_copy(
                f_hbm.at[part, :], both_ref.at[part, pl.ds(0, rank)], sems.at[index, 1]
            ),
            pltpu.make_async_copy(
                obs_hbm.at[part, :], both_ref.at[part, pl.ds(rank, width)], sems.at[index, 2]
            ),
        )

    for index in range(chunks):
        for copy in copies(index):
            copy.start()
    row = lax.broadcasted_iota(jnp.int32, (width, width), 0)
    column = lax.broadcasted_iota(jnp.int32, (width, width), 1)
    weights = jnp.concatenate(
        [turned_ref[...].astype(BF16), jnp.where(row == column, -1.0, 0.0).astype(BF16)], axis=1
    )
    flag = jnp.left_shift(1, lax.broadcasted_iota(jnp.int32, (1, per, 1), 1))

    def compare(index):
        for copy in copies(index):
            copy.wait()
        part = pl.ds(index * rows, rows)
        return lax.dot_general(
            weights, both_ref[part, :], (((1,), (1,)), ((), ())), preferred_element_type=F32
        )

    def settle(index, gap):
        part = pl.ds(index * rows, rows)
        seen = jnp.bitwise_and(bits_ref[:, part][:, None, :], flag) != 0
        error = jnp.where(seen, gap.reshape(words, per, rows), 0.0).reshape(width, rows)
        error = error.astype(BF16)
        err_ref[:, part] = error
        term = jnp.dot(error, both_ref[part, pl.ds(0, rank)], preferred_element_type=F32)
        if index == 0:
            gd_ref[...] = term
        else:
            gd_ref[...] += term

    gap = compare(0)
    for index in range(chunks):
        later = compare(index + 1) if index + 1 < chunks else None
        settle(index, gap)
        gap = later


def error_step(obs, bits, factors, turned):
    series, width = obs.shape
    rank = factors.shape[1]
    words = bits.shape[0]
    rows = rows_of(series, 1024)
    return pl.pallas_call(
        functools.partial(error_kernel, rows),
        out_shape=(
            jax.ShapeDtypeStruct((width, series), BF16),
            jax.ShapeDtypeStruct((series, rank + width), BF16),
            jax.ShapeDtypeStruct((width, rank), F32),
        ),
        in_specs=[far(), far(), far(), whole()],
        out_specs=(whole(), whole(), whole()),
        scratch_shapes=[
            pltpu.VMEM((words, series), jnp.int32),
            pltpu.SemaphoreType.DMA((series // rows, 3)),
        ],
        compiler_params=params(),
        cost_estimate=cost(8 * series * width * rank, series * (3 * width * 2 + words * 4)),
        name="errors",
    )(held(obs), held(bits), held(factors), turned)


def factor_kernel(begin, rows, chunks, both_ref, err_ref, turned_ref, *rest):
    out_hbm, out_ref, sems = rest[-3:]
    half = turned_ref[...].astype(BF16)
    size = rows // chunks

    def copy(index):
        return pltpu.make_async_copy(
            out_ref.at[pl.ds(index * size, size), :],
            out_hbm.at[pl.ds(begin + index * size, size), :],
            sems.at[index],
        )

    for index in range(chunks):
        part = pl.ds(begin + index * size, size)
        gradient = lax.dot_general(
            err_ref[:, part], half, (((0,), (0,)), ((), ())), preferred_element_type=F32
        )
        out_ref[pl.ds(index * size, size), :] = (
            both_ref[part, pl.ds(0, half.shape[1])].astype(F32) - factor_rate * gradient
        ).astype(BF16)
        copy(index).start()
    for index in range(chunks):
        copy(index).wait()


def factor_step(both, err, turned, after, sofar, begin, rows):
    width, series = err.shape
    rank = turned.shape[1]
    chunks = rows // rows_of(rows, 1024)
    rest = (after,) if sofar is None else (after, sofar)
    return pl.pallas_call(
        functools.partial(factor_kernel, begin, rows, chunks),
        out_shape=jax.ShapeDtypeStruct((series, rank), BF16),
        in_specs=[whole()] * 3 + [pl.BlockSpec(memory_space=pl.ANY)] * len(rest),
        out_specs=far(),
        input_output_aliases={} if sofar is None else {4: 0},
        scratch_shapes=[pltpu.VMEM((rows, rank), BF16), pltpu.SemaphoreType.DMA((chunks,))],
        compiler_params=params(),
        cost_estimate=cost(2 * rows * width * rank, rows * 3 * width * 2),
        name="factors",
    )(both, err, turned, *rest)


def regress_kernel(lanes, turned_ref, w_ref, gd_ref, m_hbm, v_hbm, base_ref, m_ref, v_ref, z_ref, r_ref, sems):
    m_copy = pltpu.make_async_copy(m_hbm.at[0], m_ref, sems.at[0])
    v_copy = pltpu.make_async_copy(v_hbm.at[0], v_ref, sems.at[1])
    m_copy.start()
    v_copy.start()
    width, rank = turned_ref.shape
    lags = list(range(1, w_ref.shape[0])) + [SEASON]
    for part in range(rank // lanes):
        columns = slice(part * lanes, (part + 1) * lanes)
        z_ref[part, :SEASON, :] = jnp.zeros((SEASON, lanes), F32)
        z_ref[part, SEASON:, :] = turned_ref[:, columns]
        r_ref[part, width:, :] = jnp.zeros((SEASON, lanes), F32)
        resid = turned_ref[:, columns]
        for index, lag in enumerate(lags):
            begin = SEASON - lag
            resid = resid - w_ref[index : index + 1, columns] * z_ref[part, begin : begin + width, :]
        r_ref[part, :width, :] = resid
        back = data_scale * gd_ref[:, columns] + resid
        for index, lag in enumerate(lags):
            back = back - w_ref[index : index + 1, columns] * r_ref[part, lag : lag + width, :]
        base_ref[:, columns] = back
    m_copy.wait()
    v_copy.wait()


def regress_step(turned, weights, gd, m, v):
    width, rank = gd.shape
    lanes = 128
    return pl.pallas_call(
        functools.partial(regress_kernel, lanes),
        out_shape=(
            jax.ShapeDtypeStruct((width, rank), F32),
            jax.ShapeDtypeStruct((rank, width), F32),
            jax.ShapeDtypeStruct((rank, width), F32),
        ),
        in_specs=[whole()] * 3 + [far()] * 2,
        out_specs=(whole(),) * 3,
        scratch_shapes=[
            pltpu.VMEM((rank // lanes, SEASON + width, lanes), F32),
            pltpu.VMEM((rank // lanes, SEASON + width, lanes), F32),
            pltpu.SemaphoreType.DMA((2,)),
        ],
        compiler_params=params(),
        cost_estimate=cost(100 * rank * width, 6 * rank * width * 4),
        name="regress",
    )(turned, weights, gd, held(m), held(v))


def update_kernel(
    count, sizes, lanes, stratum_ref, halo_ref, w_ref, base_ref, x_ref, m_ref, v_ref, *rest
):
    outs, (z_ref, r_ref, new_ref) = rest[: 2 * len(sizes)], rest[2 * len(sizes) :]
    width, rank = base_ref.shape
    share = rank // count
    short = w_ref.shape[0] - 1
    reach = -(-short // 8) * 8
    block_index = lax.rem(lax.axis_index("blk") + stratum_ref[...], lax.axis_size("blk"))
    for part in range(rank // lanes):
        columns = slice(part * lanes, (part + 1) * lanes)
        halo = jnp.where(block_index == 0, 0.0, halo_ref[:, columns])
        z_ref[part, :SEASON, :] = halo
        z_ref[part, SEASON:, :] = jnp.zeros((reach, lanes), F32)
        r_ref[part, :SEASON, :] = -w_ref[short : short + 1, columns] * halo
        r_ref[part, SEASON:, :] = jnp.zeros((reach, lanes), F32)
        first_rows = r_ref[part, :reach, :]
        for lag in range(1, short + 1):
            begin = SEASON - lag
            first_rows = first_rows - w_ref[lag - 1 : lag, columns] * z_ref[part, begin : begin + reach, :]
        r_ref[part, :reach, :] = first_rows
        back = r_ref[part, :SEASON, :]
        for lag in range(1, short + 1):
            back = back - w_ref[lag - 1 : lag, columns] * r_ref[part, lag : lag + SEASON, :]
        base_ref[:SEASON, columns] += back
    for part in range(rank // lanes):
        rows = slice(part * lanes, (part + 1) * lanes)
        gradient = base_ref[:, rows].T
        first = beta_one * m_ref[rows, :] + (1.0 - beta_one) * gradient
        second = beta_two * v_ref[rows, :] + (1.0 - beta_two) * gradient * gradient
        new_ref[0, rows, :] = x_ref[rows, :] - step_rate * first / (jnp.sqrt(second) + adam_eps)
        new_ref[1, rows, :] = first
        new_ref[2, rows, :] = second
    odd = lax.axis_index("grp") % 2
    begin = 0
    for piece, size in enumerate(sizes):
        for line in range(count // 2):
            for side in range(2):
                one = 2 * line + (odd if side == 0 else 1 - odd)
                start = pl.multiple_of(one * share + begin, 8)
                for which in range(3):
                    outs[2 * piece + side][which, line] = new_ref[which, pl.ds(start, size), :]
        begin += size


def update_step(stratum, halo, weights, base, x, m, v, count, sizes):
    width, rank = base.shape
    lanes = 128
    reach = -(-(weights.shape[0] - 1) // 8) * 8
    kinds = []
    for size in sizes:
        kinds += [jax.ShapeDtypeStruct((3, count // 2, size, width), F32)] * 2

    def kernel(stratum_ref, halo_ref, w_ref, base_ref, x_ref, m_ref, v_ref, *rest):
        work = rest[-1]
        work[...] = base_ref[...]
        update_kernel(
            count, sizes, lanes, stratum_ref, halo_ref, w_ref, work, x_ref, m_ref, v_ref, *rest[:-1]
        )

    outs = pl.pallas_call(
        kernel,
        out_shape=tuple(kinds),
        in_specs=[whole()] * 7,
        out_specs=(whole(),) * len(kinds),
        scratch_shapes=[
            pltpu.VMEM((rank // lanes, SEASON + reach, lanes), F32),
            pltpu.VMEM((rank // lanes, SEASON + reach, lanes), F32),
            pltpu.VMEM((3, rank, width), F32),
            pltpu.VMEM((width, rank), F32),
        ],
        compiler_params=params(),
        cost_estimate=cost(60 * rank * width, 10 * rank * width * 4),
        name="update",
    )(stratum.reshape(1, 1), halo, weights, base, x, m, v)
    return [(outs[2 * piece], outs[2 * piece + 1]) for piece in range(len(sizes))]


def halve_kernel(level, kept_ref, got_ref, keep_ref, send_ref):
    mine = (lax.axis_index("grp") // level) % 2
    for line in range(keep_ref.shape[1]):
        for out, side in ((keep_ref, mine), (send_ref, 1 - mine)):
            for which in range(3):
                out[which, line] = kept_ref[which, 2 * line + side] + got_ref[which, 2 * line + side]


def halve(kept, got, level):
    _, lines, size, width = kept.shape
    out = jax.ShapeDtypeStruct((3, lines // 2, size, width), F32)
    return pl.pallas_call(
        functools.partial(halve_kernel, level),
        out_shape=(out, out),
        in_specs=[whole(), whole()],
        out_specs=(whole(), whole()),
        compiler_params=params(),
        cost_estimate=cost(kept.size, 3 * kept.size * 4),
        name="halve",
    )(kept, got)


def mean_kernel(count, kept_ref, got_ref, out_ref):
    for which in range(3):
        out_ref[which] = (kept_ref[which, 0] + got_ref[which, 0]) / count


def mean(kept, got, count):
    _, _, size, width = kept.shape
    return pl.pallas_call(
        functools.partial(mean_kernel, count),
        out_shape=jax.ShapeDtypeStruct((3, size, width), F32),
        in_specs=[whole(), whole()],
        out_specs=whole(),
        compiler_params=params(),
        cost_estimate=cost(2 * kept.size, 3 * kept.size * 4),
        name="mean",
    )(kept, got)


def place_kernel(count, share, *rest):
    parts, outs, sems = rest[:-4], rest[-4:-1], rest[-1]
    group = lax.axis_index("grp")
    copies = []
    for index, part in enumerate(parts):
        begin = sum(before.shape[1] for before in parts[: index // count * count : count])
        size = part.shape[1]
        start = pl.multiple_of((group ^ (index % count)) * share + begin, 8)
        for which in range(3):
            copies.append(
                pltpu.make_async_copy(
                    part.at[which], outs[which].at[0, pl.ds(start, size), :], sems.at[index, which]
                )
            )
    for copy in copies:
        copy.start()
    for copy in copies:
        copy.wait()


def place(pieces):
    parts = [part for piece in pieces for part in piece]
    count = len(pieces[0])
    width = parts[0].shape[2]
    share = sum(piece[0].shape[1] for piece in pieces)
    out = jax.ShapeDtypeStruct((1, count * share, width), F32)
    return pl.pallas_call(
        functools.partial(place_kernel, count, share),
        out_shape=(out, out, out),
        in_specs=[pl.BlockSpec(memory_space=pl.ANY)] * len(parts),
        out_specs=(far(), far(), far()),
        scratch_shapes=[pltpu.SemaphoreType.DMA((len(parts), 3))],
        compiler_params=params(),
        cost_estimate=cost(0, 6 * count * share * width * 4),
        name="place",
    )(*parts)


def crossed(value, step):
    count = lax.axis_size("grp")
    return lax.ppermute(value, "grp", [(source, source ^ step) for source in range(count)])


def shifted(value, steps):
    count = lax.axis_size("blk")
    return lax.ppermute(value, "blk", [(source, (source + steps) % count) for source in range(count)])


def delivered(value, step):
    groups, slots = lax.axis_size("grp"), lax.axis_size("blk")
    pairs = [
        (group * slots + slot, (group ^ step) * slots + (slot - 1) % slots)
        for group in range(groups)
        for slot in range(slots)
    ]
    return lax.ppermute(value, ("grp", "blk"), pairs)


def body(obs, mask_bits, factors, x_blocks, first_moment, second_moment, ar_weights, stratum):
    count = lax.axis_size("grp")
    series = obs.shape[0]
    third = series // 3 // 128 * 128

    tail, turned, x = prepare(x_blocks)
    halo = shifted(tail, 1)
    err, kept, gd = error_step(obs, mask_bits.T, factors, turned)
    base, first, second = regress_step(turned, ar_weights, gd, first_moment, second_moment)
    share = x.shape[0] // count
    lead = share // 2
    (keep0, send0), (keep1, send1) = update_step(
        stratum, halo, ar_weights, base, x, first, second, count, (lead, share - lead)
    )

    got0 = crossed(send0, 1)
    got1 = crossed(send1, 1)
    keep0, send0 = halve(keep0, got0, 2)
    far0 = crossed(send0, 2)
    factor_new = factor_step(kept, err, turned, send0, None, 0, third)
    got1, factor_new = lax.optimization_barrier((got1, factor_new))
    keep1, send1 = halve(keep1, got1, 2)
    far1 = crossed(send1, 2)
    mean0 = mean(keep0, far0, count)

    near0 = delivered(mean0, 0)
    mean1 = mean(keep1, far1, count)
    near1 = delivered(mean1, 0)
    side1 = delivered(mean1, 2)
    side0 = crossed(near0, 2)
    factor_new = factor_step(kept, err, turned, near0, factor_new, third, series - third)
    near1, factor_new = lax.optimization_barrier((near1, factor_new))
    pieces = [
        [near0, crossed(near0, 1), side0, crossed(side0, 1)],
        [near1, crossed(near1, 1), side1, crossed(side1, 1)],
    ]
    return (factor_new, *place(pieces))


def solution(mesh):
    rows = P(("grp", "blk"), None)
    blocks = P("grp", None, "blk")
    return jax.shard_map(
        body,
        mesh=mesh,
        in_specs=(rows, rows, rows, blocks, blocks, blocks, P(), P()),
        out_specs=(rows, blocks, blocks, blocks),
        check_vma=False,
    )
```

```python
import functools
import math

import jax
import jax.numpy as jnp
from jax import lax
from jax.experimental import pallas as pl
from jax.experimental.pallas import tpu as pltpu
from jax.sharding import PartitionSpec as P

SEASON = 168

beta_one = 0.9
beta_two = 0.999
adam_eps = 1e-08
step_rate = 0.05
factor_rate = 0.002
data_scale = 0.25

LIMIT = 32 * 1024 * 1024
F32 = jnp.float32
BF16 = jnp.bfloat16


def whole():
    return pl.BlockSpec(memory_space=pltpu.VMEM)


def far():
    return pl.BlockSpec(memory_space=pltpu.HBM)


def held(value):
    return pltpu.with_memory_space_constraint(value, pltpu.HBM)


def scalars():
    return pl.BlockSpec(memory_space=pltpu.SMEM)


def params(**more):
    return pltpu.CompilerParams(vmem_limit_bytes=LIMIT, **more)


def cost(flops, moved):
    return pl.CostEstimate(flops=int(flops), bytes_accessed=int(moved), transcendentals=0)


def rows_of(total, most):
    best = total
    for rows in range(128, most + 1, 128):
        if total % rows == 0:
            best = rows
    return best


def chunk_copies(rows, index, rank, hbm, both_ref, bits_ref, at, sems):
    obs_hbm, bits_hbm, f_hbm = hbm
    width = both_ref.shape[1] - rank
    source, target = pl.ds(index * rows, rows), pl.ds(at, rows)
    return (
        pltpu.make_async_copy(bits_hbm.at[:, source], bits_ref.at[:, target], sems.at[0]),
        pltpu.make_async_copy(
            f_hbm.at[source, :], both_ref.at[target, pl.ds(0, rank)], sems.at[1]
        ),
        pltpu.make_async_copy(
            obs_hbm.at[source, :], both_ref.at[target, pl.ds(rank, width)], sems.at[2]
        ),
    )


def prepare_kernel(
    rows, x_hbm, obs_hbm, bits_hbm, f_hbm, tail_ref, turned_ref, x_ref, both_ref, bits_ref, sem, sems
):
    copy = pltpu.make_async_copy(x_hbm.at[0], x_ref, sem)
    copy.start()
    rank = x_ref.shape[0]
    first = chunk_copies(rows, 0, rank, (obs_hbm, bits_hbm, f_hbm), both_ref, bits_ref, 0, sems)
    for other in first:
        other.start()
    copy.wait()
    turned_ref[...] = x_ref[...].T
    tail_ref[...] = turned_ref[turned_ref.shape[0] - SEASON :, :]
    for other in first:
        other.wait()


def prepare(x, obs, bits, factors, rows):
    rank, width = x.shape[1:]
    return pl.pallas_call(
        functools.partial(prepare_kernel, rows),
        out_shape=(
            jax.ShapeDtypeStruct((SEASON, rank), F32),
            jax.ShapeDtypeStruct((width, rank), F32),
            jax.ShapeDtypeStruct((rank, width), F32),
            jax.ShapeDtypeStruct((rows, rank + width), BF16),
            jax.ShapeDtypeStruct((bits.shape[0], rows), jnp.int32),
        ),
        in_specs=[far()] * 4,
        out_specs=(whole(),) * 5,
        scratch_shapes=[pltpu.SemaphoreType.DMA(()), pltpu.SemaphoreType.DMA((3,))],
        compiler_params=params(),
        cost_estimate=cost(0, 4 * rank * width * 4 + rows * (rank + width) * 4),
        name="prepare",
    )(held(x), held(obs), held(bits), held(factors))


def error_kernel(
    rows,
    obs_hbm,
    bits_hbm,
    f_hbm,
    turned_ref,
    first_ref,
    first_bits_ref,
    err_ref,
    both_ref,
    gd_ref,
    bits_ref,
    sems,
):
    width, series = err_ref.shape
    rank = turned_ref.shape[1]
    words = bits_ref.shape[0]
    per = width // words
    chunks = series // rows

    def copies(index):
        return chunk_copies(
            rows, index, rank, (obs_hbm, bits_hbm, f_hbm),
            both_ref, bits_ref, (index - 1) * rows, sems.at[index - 1],
        )

    def pair(index):
        if index == 0:
            return first_ref[...], first_bits_ref[...]
        part = pl.ds((index - 1) * rows, rows)
        return both_ref[part, :], bits_ref[:, part]

    for index in range(1, chunks):
        for copy in copies(index):
            copy.start()
    row = lax.broadcasted_iota(jnp.int32, (width, width), 0)
    column = lax.broadcasted_iota(jnp.int32, (width, width), 1)
    weights = jnp.concatenate(
        [turned_ref[...].astype(BF16), jnp.where(row == column, -1.0, 0.0).astype(BF16)], axis=1
    )
    flag = jnp.left_shift(1, lax.broadcasted_iota(jnp.int32, (1, per, 1), 1))

    def compare(index):
        if index > 0:
            for copy in copies(index):
                copy.wait()
        return lax.dot_general(
            weights, pair(index)[0], (((1,), (1,)), ((), ())), preferred_element_type=F32
        )

    def settle(index, gap):
        part = pl.ds(index * rows, rows)
        both, bits = pair(index)
        seen = jnp.bitwise_and(bits[:, None, :], flag) != 0
        error = jnp.where(seen, gap.reshape(words, per, rows), 0.0).reshape(width, rows)
        error = error.astype(BF16)
        err_ref[:, part] = error
        term = jnp.dot(error, both[:, :rank], preferred_element_type=F32)
        if index == 0:
            gd_ref[...] = term
        else:
            gd_ref[...] += term

    gap = compare(0)
    for index in range(chunks):
        later = compare(index + 1) if index + 1 < chunks else None
        settle(index, gap)
        gap = later


def error_step(obs, bits, factors, turned, first, first_bits):
    series, width = obs.shape
    rank = factors.shape[1]
    words = bits.shape[0]
    rows = first.shape[0]
    others = max(series - rows, rows)
    return pl.pallas_call(
        functools.partial(error_kernel, rows),
        out_shape=(
            jax.ShapeDtypeStruct((width, series), BF16),
            jax.ShapeDtypeStruct((others, rank + width), BF16),
            jax.ShapeDtypeStruct((width, rank), F32),
        ),
        in_specs=[far(), far(), far(), whole(), whole(), whole()],
        out_specs=(whole(), whole(), whole()),
        scratch_shapes=[
            pltpu.VMEM((words, others), jnp.int32),
            pltpu.SemaphoreType.DMA((others // rows, 3)),
        ],
        compiler_params=params(),
        cost_estimate=cost(8 * series * width * rank, series * (3 * width * 2 + words * 4)),
        name="errors",
    )(held(obs), held(bits), held(factors), turned, first, first_bits)


def factor_kernel(begin, rows, chunks, first_ref, both_ref, err_ref, turned_ref, *rest):
    out_hbm, out_ref, sems = rest[-3:]
    half = turned_ref[...].astype(BF16)
    size = rows // chunks

    def copy(index):
        return pltpu.make_async_copy(
            out_ref.at[pl.ds(index * size, size), :],
            out_hbm.at[pl.ds(begin + index * size, size), :],
            sems.at[index],
        )

    for index in range(chunks):
        part = pl.ds(begin + index * size, size)
        split = first_ref.shape[0]
        if begin + index * size < split:
            old = first_ref[part, pl.ds(0, half.shape[1])]
        else:
            old = both_ref[pl.ds(begin + index * size - split, size), pl.ds(0, half.shape[1])]
        gradient = lax.dot_general(
            err_ref[:, part], half, (((0,), (0,)), ((), ())), preferred_element_type=F32
        )
        out_ref[pl.ds(index * size, size), :] = (
            old.astype(F32) - factor_rate * gradient
        ).astype(BF16)
        copy(index).start()
    for index in range(chunks):
        copy(index).wait()


def factor_step(first, both, err, turned, after, sofar, begin, rows):
    width, series = err.shape
    rank = turned.shape[1]
    chunks = rows // math.gcd(first.shape[0], rows, begin)
    rest = (after,) if sofar is None else (after, sofar)
    return pl.pallas_call(
        functools.partial(factor_kernel, begin, rows, chunks),
        out_shape=jax.ShapeDtypeStruct((series, rank), BF16),
        in_specs=[whole()] * 4 + [pl.BlockSpec(memory_space=pl.ANY)] * len(rest),
        out_specs=far(),
        input_output_aliases={} if sofar is None else {5: 0},
        scratch_shapes=[pltpu.VMEM((rows, rank), BF16), pltpu.SemaphoreType.DMA((chunks,))],
        compiler_params=params(),
        cost_estimate=cost(2 * rows * width * rank, rows * 3 * width * 2),
        name="factors",
    )(first, both, err, turned, *rest)


def regress_kernel(
    lanes, turned_ref, w_ref, gd_ref, m_hbm, v_hbm, base_ref, m_ref, v_ref, z_ref, r_ref, sems
):
    m_copy = pltpu.make_async_copy(m_hbm.at[0], m_ref, sems.at[0])
    v_copy = pltpu.make_async_copy(v_hbm.at[0], v_ref, sems.at[1])
    m_copy.start()
    v_copy.start()
    width, rank = turned_ref.shape
    lags = list(range(1, w_ref.shape[0])) + [SEASON]
    for part in range(rank // lanes):
        columns = slice(part * lanes, (part + 1) * lanes)
        z_ref[part, :SEASON, :] = jnp.zeros((SEASON, lanes), F32)
        z_ref[part, SEASON:, :] = turned_ref[:, columns]
        r_ref[part, width:, :] = jnp.zeros((SEASON, lanes), F32)
        resid = turned_ref[:, columns]
        for index, lag in enumerate(lags):
            begin = SEASON - lag
            resid = resid - w_ref[index : index + 1, columns] * z_ref[part, begin : begin + width, :]
        r_ref[part, :width, :] = resid
        back = data_scale * gd_ref[:, columns] + resid
        for index, lag in enumerate(lags):
            back = back - w_ref[index : index + 1, columns] * r_ref[part, lag : lag + width, :]
        base_ref[:, columns] = back
    m_copy.wait()
    v_copy.wait()


def regress_step(turned, weights, gd, m, v):
    width, rank = gd.shape
    lanes = 128
    return pl.pallas_call(
        functools.partial(regress_kernel, lanes),
        out_shape=(
            jax.ShapeDtypeStruct((width, rank), F32),
            jax.ShapeDtypeStruct((rank, width), F32),
            jax.ShapeDtypeStruct((rank, width), F32),
        ),
        in_specs=[whole()] * 3 + [far()] * 2,
        out_specs=(whole(),) * 3,
        scratch_shapes=[
            pltpu.VMEM((rank // lanes, SEASON + width, lanes), F32),
            pltpu.VMEM((rank // lanes, SEASON + width, lanes), F32),
            pltpu.SemaphoreType.DMA((2,)),
        ],
        compiler_params=params(),
        cost_estimate=cost(100 * rank * width, 6 * rank * width * 4),
        name="regress",
    )(turned, weights, gd, held(m), held(v))


def update_kernel(
    count, sizes, lanes, stratum_ref, halo_ref, w_ref, base_ref, x_ref, m_ref, v_ref, *rest
):
    outs, (z_ref, r_ref, new_ref) = rest[: 2 * len(sizes)], rest[2 * len(sizes) :]
    width, rank = base_ref.shape
    share = rank // count
    short = w_ref.shape[0] - 1
    reach = -(-short // 8) * 8
    block_index = lax.rem(lax.axis_index("blk") + stratum_ref[...], lax.axis_size("blk"))
    for part in range(rank // lanes):
        columns = slice(part * lanes, (part + 1) * lanes)
        halo = jnp.where(block_index == 0, 0.0, halo_ref[:, columns])
        z_ref[part, :SEASON, :] = halo
        z_ref[part, SEASON:, :] = jnp.zeros((reach, lanes), F32)
        r_ref[part, :SEASON, :] = -w_ref[short : short + 1, columns] * halo
        r_ref[part, SEASON:, :] = jnp.zeros((reach, lanes), F32)
        first_rows = r_ref[part, :reach, :]
        for lag in range(1, short + 1):
            begin = SEASON - lag
            first_rows = first_rows - w_ref[lag - 1 : lag, columns] * z_ref[part, begin : begin + reach, :]
        r_ref[part, :reach, :] = first_rows
        back = r_ref[part, :SEASON, :]
        for lag in range(1, short + 1):
            back = back - w_ref[lag - 1 : lag, columns] * r_ref[part, lag : lag + SEASON, :]
        base_ref[:SEASON, columns] += back
    for part in range(rank // lanes):
        rows = slice(part * lanes, (part + 1) * lanes)
        gradient = base_ref[:, rows].T
        first = beta_one * m_ref[rows, :] + (1.0 - beta_one) * gradient
        second = beta_two * v_ref[rows, :] + (1.0 - beta_two) * gradient * gradient
        new_ref[0, rows, :] = x_ref[rows, :] - step_rate * first / (jnp.sqrt(second) + adam_eps)
        new_ref[1, rows, :] = first
        new_ref[2, rows, :] = second
    odd = lax.axis_index("grp") % 2
    begin = 0
    for piece, size in enumerate(sizes):
        for line in range(count // 2):
            for side in range(2):
                one = 2 * line + (odd if side == 0 else 1 - odd)
                start = pl.multiple_of(one * share + begin, 8)
                for which in range(3):
                    outs[2 * piece + side][which, line] = new_ref[which, pl.ds(start, size), :]
        begin += size


def update_step(stratum, halo, weights, base, x, m, v, count, sizes):
    width, rank = base.shape
    lanes = 128
    reach = -(-(weights.shape[0] - 1) // 8) * 8
    kinds = []
    for size in sizes:
        kinds += [jax.ShapeDtypeStruct((3, count // 2, size, width), F32)] * 2

    def kernel(stratum_ref, halo_ref, w_ref, base_ref, x_ref, m_ref, v_ref, *rest):
        work = rest[-1]
        work[...] = base_ref[...]
        update_kernel(
            count, sizes, lanes, stratum_ref, halo_ref, w_ref, work, x_ref, m_ref, v_ref, *rest[:-1]
        )

    outs = pl.pallas_call(
        kernel,
        out_shape=tuple(kinds),
        in_specs=[whole()] * 7,
        out_specs=(whole(),) * len(kinds),
        scratch_shapes=[
            pltpu.VMEM((rank // lanes, SEASON + reach, lanes), F32),
            pltpu.VMEM((rank // lanes, SEASON + reach, lanes), F32),
            pltpu.VMEM((3, rank, width), F32),
            pltpu.VMEM((width, rank), F32),
        ],
        compiler_params=params(),
        cost_estimate=cost(60 * rank * width, 10 * rank * width * 4),
        name="update",
    )(stratum.reshape(1, 1), halo, weights, base, x, m, v)
    return [(outs[2 * piece], outs[2 * piece + 1]) for piece in range(len(sizes))]


def halve_kernel(level, kept_ref, got_ref, keep_ref, send_ref):
    mine = (lax.axis_index("grp") // level) % 2
    for line in range(keep_ref.shape[1]):
        for out, side in ((keep_ref, mine), (send_ref, 1 - mine)):
            for which in range(3):
                out[which, line] = kept_ref[which, 2 * line + side] + got_ref[which, 2 * line + side]


def halve(kept, got, level):
    _, lines, size, width = kept.shape
    out = jax.ShapeDtypeStruct((3, lines // 2, size, width), F32)
    return pl.pallas_call(
        functools.partial(halve_kernel, level),
        out_shape=(out, out),
        in_specs=[whole(), whole()],
        out_specs=(whole(), whole()),
        compiler_params=params(),
        cost_estimate=cost(kept.size, 3 * kept.size * 4),
        name="halve",
    )(kept, got)


def mean_kernel(count, kept_ref, got_ref, out_ref):
    for which in range(3):
        out_ref[which] = (kept_ref[which, 0] + got_ref[which, 0]) / count


def mean(kept, got, count):
    _, _, size, width = kept.shape
    return pl.pallas_call(
        functools.partial(mean_kernel, count),
        out_shape=jax.ShapeDtypeStruct((3, size, width), F32),
        in_specs=[whole(), whole()],
        out_specs=whole(),
        compiler_params=params(),
        cost_estimate=cost(2 * kept.size, 3 * kept.size * 4),
        name="mean",
    )(kept, got)


def place_kernel(count, share, *rest):
    parts, outs, sems = rest[:-4], rest[-4:-1], rest[-1]
    group = lax.axis_index("grp")
    copies = []
    for index, part in enumerate(parts):
        begin = sum(before.shape[1] for before in parts[: index // count * count : count])
        size = part.shape[1]
        start = pl.multiple_of((group ^ (index % count)) * share + begin, 8)
        for which in range(3):
            copies.append(
                pltpu.make_async_copy(
                    part.at[which], outs[which].at[0, pl.ds(start, size), :], sems.at[index, which]
                )
            )
    for copy in copies:
        copy.start()
    for copy in copies:
        copy.wait()


def place(pieces):
    parts = [part for piece in pieces for part in piece]
    count = len(pieces[0])
    width = parts[0].shape[2]
    share = sum(piece[0].shape[1] for piece in pieces)
    out = jax.ShapeDtypeStruct((1, count * share, width), F32)
    return pl.pallas_call(
        functools.partial(place_kernel, count, share),
        out_shape=(out, out, out),
        in_specs=[pl.BlockSpec(memory_space=pl.ANY)] * len(parts),
        out_specs=(far(), far(), far()),
        scratch_shapes=[pltpu.SemaphoreType.DMA((len(parts), 3))],
        compiler_params=params(),
        cost_estimate=cost(0, 6 * count * share * width * 4),
        name="place",
    )(*parts)


def crossed(value, step):
    count = lax.axis_size("grp")
    return lax.ppermute(value, "grp", [(source, source ^ step) for source in range(count)])


def shifted(value, steps):
    count = lax.axis_size("blk")
    return lax.ppermute(value, "blk", [(source, (source + steps) % count) for source in range(count)])


def delivered(value, step):
    groups, slots = lax.axis_size("grp"), lax.axis_size("blk")
    pairs = [
        (group * slots + slot, (group ^ step) * slots + (slot - 1) % slots)
        for group in range(groups)
        for slot in range(slots)
    ]
    return lax.ppermute(value, ("grp", "blk"), pairs)


def body(obs, mask_bits, factors, x_blocks, first_moment, second_moment, ar_weights, stratum):
    count = lax.axis_size("grp")
    series = obs.shape[0]
    rows = rows_of(series, 1024)
    third = max(series // rows // 3, 1) * rows
    bits = mask_bits.T

    tail, turned, x, lead, lead_bits = prepare(x_blocks, obs, bits, factors, rows)
    halo = shifted(tail, 1)
    err, kept, gd = error_step(obs, bits, factors, turned, lead, lead_bits)
    base, first, second = regress_step(turned, ar_weights, gd, first_moment, second_moment)
    share = x.shape[0] // count
    half = share // 2
    (keep0, send0), (keep1, send1) = update_step(
        stratum, halo, ar_weights, base, x, first, second, count, (half, share - half)
    )

    got0 = crossed(send0, 1)
    got1 = crossed(send1, 1)
    keep0, send0 = halve(keep0, got0, 2)
    far0 = crossed(send0, 2)
    factor_new = factor_step(lead, kept, err, turned, send0, None, 0, third)
    got1, factor_new = lax.optimization_barrier((got1, factor_new))
    keep1, send1 = halve(keep1, got1, 2)
    far1 = crossed(send1, 2)
    mean0 = mean(keep0, far0, count)

    near0 = delivered(mean0, 0)
    mean1 = mean(keep1, far1, count)
    near1 = delivered(mean1, 0)
    side1 = delivered(mean1, 2)
    side0 = crossed(near0, 2)
    factor_new = factor_step(lead, kept, err, turned, near0, factor_new, third, series - third)
    near1, factor_new = lax.optimization_barrier((near1, factor_new))
    pieces = [
        [near0, crossed(near0, 1), side0, crossed(side0, 1)],
        [near1, crossed(near1, 1), side1, crossed(side1, 1)],
    ]
    return (factor_new, *place(pieces))


def solution(mesh):
    rows = P(("grp", "blk"), None)
    blocks = P("grp", None, "blk")
    return jax.shard_map(
        body,
        mesh=mesh,
        in_specs=(rows, rows, rows, blocks, blocks, blocks, P(), P()),
        out_specs=(rows, blocks, blocks, blocks),
        check_vma=False,
    )
```

```python
import functools
import math

import jax
import jax.numpy as jnp
from jax import lax
from jax.experimental import pallas as pl
from jax.experimental.pallas import tpu as pltpu
from jax.sharding import PartitionSpec as P

SEASON = 168

beta_one = 0.9
beta_two = 0.999
adam_eps = 1e-08
step_rate = 0.05
factor_rate = 0.002
data_scale = 0.25

LIMIT = 32 * 1024 * 1024
F32 = jnp.float32
BF16 = jnp.bfloat16


def whole():
    return pl.BlockSpec(memory_space=pltpu.VMEM)


def far():
    return pl.BlockSpec(memory_space=pltpu.HBM)


def held(value):
    return pltpu.with_memory_space_constraint(value, pltpu.HBM)


def scalars():
    return pl.BlockSpec(memory_space=pltpu.SMEM)


def params(**more):
    return pltpu.CompilerParams(vmem_limit_bytes=LIMIT, **more)


def cost(flops, moved):
    return pl.CostEstimate(flops=int(flops), bytes_accessed=int(moved), transcendentals=0)


def rows_of(total, most):
    best = total
    for rows in range(128, most + 1, 128):
        if total % rows == 0:
            best = rows
    return best


def chunk_copies(rows, index, rank, hbm, both_ref, bits_ref, at, sems):
    obs_hbm, bits_hbm, f_hbm = hbm
    width = both_ref.shape[1] - rank
    source, target = pl.ds(index * rows, rows), pl.ds(at, rows)
    return (
        pltpu.make_async_copy(bits_hbm.at[:, source], bits_ref.at[:, target], sems.at[0]),
        pltpu.make_async_copy(
            f_hbm.at[source, :], both_ref.at[target, pl.ds(0, rank)], sems.at[1]
        ),
        pltpu.make_async_copy(
            obs_hbm.at[source, :], both_ref.at[target, pl.ds(rank, width)], sems.at[2]
        ),
    )


def prepare_kernel(
    rows, x_hbm, obs_hbm, bits_hbm, f_hbm, tail_ref, turned_ref, x_ref, both_ref, bits_ref, sem, sems
):
    copy = pltpu.make_async_copy(x_hbm.at[0], x_ref, sem)
    copy.start()
    rank = x_ref.shape[0]
    first = chunk_copies(rows, 0, rank, (obs_hbm, bits_hbm, f_hbm), both_ref, bits_ref, 0, sems)
    for other in first:
        other.start()
    copy.wait()
    turned_ref[...] = x_ref[...].T
    tail_ref[...] = turned_ref[turned_ref.shape[0] - SEASON :, :]
    for other in first:
        other.wait()


def prepare(x, obs, bits, factors, rows):
    rank, width = x.shape[1:]
    return pl.pallas_call(
        functools.partial(prepare_kernel, rows),
        out_shape=(
            jax.ShapeDtypeStruct((SEASON, rank), F32),
            jax.ShapeDtypeStruct((width, rank), F32),
            jax.ShapeDtypeStruct((rank, width), F32),
            jax.ShapeDtypeStruct((rows, rank + width), BF16),
            jax.ShapeDtypeStruct((bits.shape[0], rows), jnp.int32),
        ),
        in_specs=[far()] * 4,
        out_specs=(whole(),) * 5,
        scratch_shapes=[pltpu.SemaphoreType.DMA(()), pltpu.SemaphoreType.DMA((3,))],
        compiler_params=params(),
        cost_estimate=cost(0, 4 * rank * width * 4 + rows * (rank + width) * 4),
        name="prepare",
    )(held(x), held(obs), held(bits), held(factors))


def error_kernel(
    rows,
    obs_hbm,
    bits_hbm,
    f_hbm,
    turned_ref,
    first_ref,
    first_bits_ref,
    err_ref,
    both_ref,
    gd_ref,
    bits_ref,
    sems,
):
    width, series = err_ref.shape
    rank = turned_ref.shape[1]
    words = bits_ref.shape[0]
    per = width // words
    chunks = series // rows

    def copies(index):
        return chunk_copies(
            rows, index, rank, (obs_hbm, bits_hbm, f_hbm),
            both_ref, bits_ref, (index - 1) * rows, sems.at[index - 1],
        )

    def pair(index):
        if index == 0:
            return first_ref[...], first_bits_ref[...]
        part = pl.ds((index - 1) * rows, rows)
        return both_ref[part, :], bits_ref[:, part]

    for index in range(1, chunks):
        for copy in copies(index):
            copy.start()
    row = lax.broadcasted_iota(jnp.int32, (width, width), 0)
    column = lax.broadcasted_iota(jnp.int32, (width, width), 1)
    weights = jnp.concatenate(
        [turned_ref[...].astype(BF16), jnp.where(row == column, -1.0, 0.0).astype(BF16)], axis=1
    )
    flag = jnp.left_shift(1, lax.broadcasted_iota(jnp.int32, (1, per, 1), 1))

    def compare(index):
        if index > 0:
            for copy in copies(index):
                copy.wait()
        return lax.dot_general(
            weights, pair(index)[0], (((1,), (1,)), ((), ())), preferred_element_type=F32
        )

    def settle(index, gap):
        part = pl.ds(index * rows, rows)
        both, bits = pair(index)
        seen = jnp.bitwise_and(bits[:, None, :], flag) != 0
        error = jnp.where(seen, gap.reshape(words, per, rows), 0.0).reshape(width, rows)
        error = error.astype(BF16)
        err_ref[:, part] = error
        term = jnp.dot(error, both[:, :rank], preferred_element_type=F32)
        if index == 0:
            gd_ref[...] = term
        else:
            gd_ref[...] += term

    gap = compare(0)
    for index in range(chunks):
        later = compare(index + 1) if index + 1 < chunks else None
        settle(index, gap)
        gap = later


def error_step(obs, bits, factors, turned, first, first_bits):
    series, width = obs.shape
    rank = factors.shape[1]
    words = bits.shape[0]
    rows = first.shape[0]
    others = max(series - rows, rows)
    return pl.pallas_call(
        functools.partial(error_kernel, rows),
        out_shape=(
            jax.ShapeDtypeStruct((width, series), BF16),
            jax.ShapeDtypeStruct((others, rank + width), BF16),
            jax.ShapeDtypeStruct((width, rank), F32),
        ),
        in_specs=[far(), far(), far(), whole(), whole(), whole()],
        out_specs=(whole(), whole(), whole()),
        scratch_shapes=[
            pltpu.VMEM((words, others), jnp.int32),
            pltpu.SemaphoreType.DMA((others // rows, 3)),
        ],
        compiler_params=params(),
        cost_estimate=cost(8 * series * width * rank, series * (3 * width * 2 + words * 4)),
        name="errors",
    )(held(obs), held(bits), held(factors), turned, first, first_bits)


def factor_kernel(begin, rows, chunks, first_ref, both_ref, err_ref, turned_ref, *rest):
    out_hbm, out_ref, sems = rest[-3:]
    half = turned_ref[...].astype(BF16)
    size = rows // chunks

    def copy(index):
        return pltpu.make_async_copy(
            out_ref.at[pl.ds(index * size, size), :],
            out_hbm.at[pl.ds(begin + index * size, size), :],
            sems.at[index],
        )

    for index in range(chunks):
        part = pl.ds(begin + index * size, size)
        split = first_ref.shape[0]
        if begin + index * size < split:
            old = first_ref[part, pl.ds(0, half.shape[1])]
        else:
            old = both_ref[pl.ds(begin + index * size - split, size), pl.ds(0, half.shape[1])]
        gradient = lax.dot_general(
            err_ref[:, part], half, (((0,), (0,)), ((), ())), preferred_element_type=F32
        )
        out_ref[pl.ds(index * size, size), :] = (
            old.astype(F32) - factor_rate * gradient
        ).astype(BF16)
        copy(index).start()
    for index in range(chunks):
        copy(index).wait()


def factor_step(first, both, err, turned, after, sofar, begin, rows):
    width, series = err.shape
    rank = turned.shape[1]
    chunks = rows // math.gcd(first.shape[0], rows, begin)
    rest = (after,) if sofar is None else (after, sofar)
    return pl.pallas_call(
        functools.partial(factor_kernel, begin, rows, chunks),
        out_shape=jax.ShapeDtypeStruct((series, rank), BF16),
        in_specs=[whole()] * 4 + [pl.BlockSpec(memory_space=pl.ANY)] * len(rest),
        out_specs=far(),
        input_output_aliases={} if sofar is None else {5: 0},
        scratch_shapes=[pltpu.VMEM((rows, rank), BF16), pltpu.SemaphoreType.DMA((chunks,))],
        compiler_params=params(),
        cost_estimate=cost(2 * rows * width * rank, rows * 3 * width * 2),
        name="factors",
    )(first, both, err, turned, *rest)


def regress_kernel(
    lanes, turned_ref, w_ref, gd_ref, m_hbm, v_hbm, base_ref, m_ref, v_ref, z_ref, r_ref, sems
):
    m_copy = pltpu.make_async_copy(m_hbm.at[0], m_ref, sems.at[0])
    v_copy = pltpu.make_async_copy(v_hbm.at[0], v_ref, sems.at[1])
    m_copy.start()
    v_copy.start()
    width, rank = turned_ref.shape
    lags = list(range(1, w_ref.shape[0])) + [SEASON]
    for part in range(rank // lanes):
        columns = slice(part * lanes, (part + 1) * lanes)
        z_ref[part, :SEASON, :] = jnp.zeros((SEASON, lanes), F32)
        z_ref[part, SEASON:, :] = turned_ref[:, columns]
        r_ref[part, width:, :] = jnp.zeros((SEASON, lanes), F32)
        resid = turned_ref[:, columns]
        for index, lag in enumerate(lags):
            begin = SEASON - lag
            resid = resid - w_ref[index : index + 1, columns] * z_ref[part, begin : begin + width, :]
        r_ref[part, :width, :] = resid
        back = data_scale * gd_ref[:, columns] + resid
        for index, lag in enumerate(lags):
            back = back - w_ref[index : index + 1, columns] * r_ref[part, lag : lag + width, :]
        base_ref[:, columns] = back
    m_copy.wait()
    v_copy.wait()


def regress_step(turned, weights, gd, m, v):
    width, rank = gd.shape
    lanes = 128
    return pl.pallas_call(
        functools.partial(regress_kernel, lanes),
        out_shape=(
            jax.ShapeDtypeStruct((width, rank), F32),
            jax.ShapeDtypeStruct((rank, width), F32),
            jax.ShapeDtypeStruct((rank, width), F32),
        ),
        in_specs=[whole()] * 3 + [far()] * 2,
        out_specs=(whole(),) * 3,
        scratch_shapes=[
            pltpu.VMEM((rank // lanes, SEASON + width, lanes), F32),
            pltpu.VMEM((rank // lanes, SEASON + width, lanes), F32),
            pltpu.SemaphoreType.DMA((2,)),
        ],
        compiler_params=params(),
        cost_estimate=cost(100 * rank * width, 6 * rank * width * 4),
        name="regress",
    )(turned, weights, gd, held(m), held(v))


def update_kernel(
    count, sizes, lanes, stratum_ref, halo_ref, w_ref, base_ref, x_ref, m_ref, v_ref, *rest
):
    outs, (z_ref, r_ref, new_ref) = rest[: 2 * len(sizes)], rest[2 * len(sizes) :]
    width, rank = base_ref.shape
    share = rank // count
    short = w_ref.shape[0] - 1
    reach = -(-short // 8) * 8
    block_index = lax.rem(lax.axis_index("blk") + stratum_ref[...], lax.axis_size("blk"))
    for part in range(rank // lanes):
        columns = slice(part * lanes, (part + 1) * lanes)
        halo = jnp.where(block_index == 0, 0.0, halo_ref[:, columns])
        z_ref[part, :SEASON, :] = halo
        z_ref[part, SEASON:, :] = jnp.zeros((reach, lanes), F32)
        r_ref[part, :SEASON, :] = -w_ref[short : short + 1, columns] * halo
        r_ref[part, SEASON:, :] = jnp.zeros((reach, lanes), F32)
        first_rows = r_ref[part, :reach, :]
        for lag in range(1, short + 1):
            begin = SEASON - lag
            first_rows = first_rows - w_ref[lag - 1 : lag, columns] * z_ref[part, begin : begin + reach, :]
        r_ref[part, :reach, :] = first_rows
        back = r_ref[part, :SEASON, :]
        for lag in range(1, short + 1):
            back = back - w_ref[lag - 1 : lag, columns] * r_ref[part, lag : lag + SEASON, :]
        base_ref[:SEASON, columns] += back
    for part in range(rank // lanes):
        rows = slice(part * lanes, (part + 1) * lanes)
        gradient = base_ref[:, rows].T
        first = beta_one * m_ref[rows, :] + (1.0 - beta_one) * gradient
        second = beta_two * v_ref[rows, :] + (1.0 - beta_two) * gradient * gradient
        new_ref[0, rows, :] = x_ref[rows, :] - step_rate * first / (jnp.sqrt(second) + adam_eps)
        new_ref[1, rows, :] = first
        new_ref[2, rows, :] = second
    odd = lax.axis_index("grp") % 2
    begin = 0
    for piece, size in enumerate(sizes):
        for line in range(count // 2):
            for side in range(2):
                one = 2 * line + (odd if side == 0 else 1 - odd)
                start = pl.multiple_of(one * share + begin, 8)
                for which in range(3):
                    outs[2 * piece + side][which, line] = new_ref[which, pl.ds(start, size), :]
        begin += size


def update_step(stratum, halo, weights, base, x, m, v, count, sizes):
    width, rank = base.shape
    lanes = 128
    reach = -(-(weights.shape[0] - 1) // 8) * 8
    kinds = []
    for size in sizes:
        kinds += [jax.ShapeDtypeStruct((3, count // 2, size, width), F32)] * 2

    def kernel(stratum_ref, halo_ref, w_ref, base_ref, x_ref, m_ref, v_ref, *rest):
        work = rest[-1]
        work[...] = base_ref[...]
        update_kernel(
            count, sizes, lanes, stratum_ref, halo_ref, w_ref, work, x_ref, m_ref, v_ref, *rest[:-1]
        )

    outs = pl.pallas_call(
        kernel,
        out_shape=tuple(kinds),
        in_specs=[whole()] * 7,
        out_specs=(whole(),) * len(kinds),
        scratch_shapes=[
            pltpu.VMEM((rank // lanes, SEASON + reach, lanes), F32),
            pltpu.VMEM((rank // lanes, SEASON + reach, lanes), F32),
            pltpu.VMEM((3, rank, width), F32),
            pltpu.VMEM((width, rank), F32),
        ],
        compiler_params=params(),
        cost_estimate=cost(60 * rank * width, 10 * rank * width * 4),
        name="update",
    )(stratum.reshape(1, 1), halo, weights, base, x, m, v)
    return [(outs[2 * piece], outs[2 * piece + 1]) for piece in range(len(sizes))]


def halve_kernel(level, kept_ref, got_ref, keep_ref, send_ref):
    mine = (lax.axis_index("grp") // level) % 2
    for line in range(keep_ref.shape[1]):
        for out, side in ((keep_ref, mine), (send_ref, 1 - mine)):
            for which in range(3):
                out[which, line] = kept_ref[which, 2 * line + side] + got_ref[which, 2 * line + side]


def halve(kept, got, level):
    _, lines, size, width = kept.shape
    out = jax.ShapeDtypeStruct((3, lines // 2, size, width), F32)
    return pl.pallas_call(
        functools.partial(halve_kernel, level),
        out_shape=(out, out),
        in_specs=[whole(), whole()],
        out_specs=(whole(), whole()),
        compiler_params=params(),
        cost_estimate=cost(kept.size, 3 * kept.size * 4),
        name="halve",
    )(kept, got)


def mean_kernel(count, kept_ref, got_ref, out_ref):
    for which in range(3):
        out_ref[which] = (kept_ref[which, 0] + got_ref[which, 0]) / count


def mean(kept, got, count):
    _, _, size, width = kept.shape
    return pl.pallas_call(
        functools.partial(mean_kernel, count),
        out_shape=jax.ShapeDtypeStruct((3, size, width), F32),
        in_specs=[whole(), whole()],
        out_specs=whole(),
        compiler_params=params(),
        cost_estimate=cost(2 * kept.size, 3 * kept.size * 4),
        name="mean",
    )(kept, got)


def place_kernel(count, share, *rest):
    parts, outs, sems = rest[:-4], rest[-4:-1], rest[-1]
    group = lax.axis_index("grp")
    copies = []
    for index, part in enumerate(parts):
        begin = sum(before.shape[1] for before in parts[: index // count * count : count])
        size = part.shape[1]
        start = pl.multiple_of((group ^ (index % count)) * share + begin, 8)
        for which in range(3):
            copies.append(
                pltpu.make_async_copy(
                    part.at[which], outs[which].at[0, pl.ds(start, size), :], sems.at[index, which]
                )
            )
    for copy in copies:
        copy.start()
    for copy in copies:
        copy.wait()


def place(pieces):
    parts = [part for piece in pieces for part in piece]
    count = len(pieces[0])
    width = parts[0].shape[2]
    share = sum(piece[0].shape[1] for piece in pieces)
    out = jax.ShapeDtypeStruct((1, count * share, width), F32)
    return pl.pallas_call(
        functools.partial(place_kernel, count, share),
        out_shape=(out, out, out),
        in_specs=[pl.BlockSpec(memory_space=pl.ANY)] * len(parts),
        out_specs=(far(), far(), far()),
        scratch_shapes=[pltpu.SemaphoreType.DMA((len(parts), 3))],
        compiler_params=params(),
        cost_estimate=cost(0, 6 * count * share * width * 4),
        name="place",
    )(*parts)


def crossed(value, step):
    count = lax.axis_size("grp")
    return lax.ppermute(value, "grp", [(source, source ^ step) for source in range(count)])


def shifted(value, steps):
    count = lax.axis_size("blk")
    return lax.ppermute(value, "blk", [(source, (source + steps) % count) for source in range(count)])


def delivered(value, step, around=True):
    groups, slots = lax.axis_size("grp"), lax.axis_size("blk")
    pairs = [
        (group * slots + slot, (group ^ step) * slots + (slot - 1) % slots)
        for group in range(groups)
        for slot in range(0 if around else 1, slots)
    ]
    return lax.ppermute(value, ("grp", "blk"), pairs)


def crossed_last(value, step):
    groups, slots = lax.axis_size("grp"), lax.axis_size("blk")
    pairs = [
        (group * slots + slots - 1, (group ^ step) * slots + slots - 1) for group in range(groups)
    ]
    return lax.ppermute(value, ("grp", "blk"), pairs)


def choose_kernel(last_ref, other_ref, out_ref):
    last = lax.axis_index("blk") == lax.axis_size("blk") - 1
    out_ref[...] = jnp.where(last, last_ref[...], other_ref[...])


def choose(last, other):
    return pl.pallas_call(
        choose_kernel,
        out_shape=jax.ShapeDtypeStruct(last.shape, F32),
        in_specs=[whole(), whole()],
        out_specs=whole(),
        compiler_params=params(),
        cost_estimate=cost(last.size, 3 * last.size * 4),
        name="choose",
    )(last, other)


def body(obs, mask_bits, factors, x_blocks, first_moment, second_moment, ar_weights, stratum):
    count = lax.axis_size("grp")
    series = obs.shape[0]
    rows = rows_of(series, 1024)
    third = max(series // rows // 3, 1) * rows
    bits = mask_bits.T

    tail, turned, x, lead, lead_bits = prepare(x_blocks, obs, bits, factors, rows)
    halo = shifted(tail, 1)
    err, kept, gd = error_step(obs, bits, factors, turned, lead, lead_bits)
    base, first, second = regress_step(turned, ar_weights, gd, first_moment, second_moment)
    share = x.shape[0] // count
    half = share // 2
    (keep0, send0), (keep1, send1) = update_step(
        stratum, halo, ar_weights, base, x, first, second, count, (half, share - half)
    )

    got0 = crossed(send0, 1)
    got1 = crossed(send1, 1)
    keep0, send0 = halve(keep0, got0, 2)
    far0 = crossed(send0, 2)
    factor_new = factor_step(lead, kept, err, turned, send0, None, 0, third)
    got1, factor_new = lax.optimization_barrier((got1, factor_new))
    keep1, send1 = halve(keep1, got1, 2)
    far1 = crossed(send1, 2)
    mean0 = mean(keep0, far0, count)

    near0 = delivered(mean0, 0)
    far1, mean0 = lax.optimization_barrier((far1, mean0))
    mean1 = mean(keep1, far1, count)
    near1 = delivered(mean1, 0)
    flip1 = delivered(mean1, 2, around=False)
    side0 = crossed(near0, 2)
    last1 = crossed_last(near1, 2)
    factor_new = factor_step(lead, kept, err, turned, near0, factor_new, third, series - third)
    flip1, side0, factor_new = lax.optimization_barrier((flip1, side0, factor_new))
    side1 = choose(last1, flip1)
    pieces = [
        [near0, crossed(near0, 1), side0, crossed(side0, 1)],
        [near1, crossed(near1, 1), side1, crossed(side1, 1)],
    ]
    return (factor_new, *place(pieces))


def solution(mesh):
    rows = P(("grp", "blk"), None)
    blocks = P("grp", None, "blk")
    return jax.shard_map(
        body,
        mesh=mesh,
        in_specs=(rows, rows, rows, blocks, blocks, blocks, P(), P()),
        out_specs=(rows, blocks, blocks, blocks),
        check_vma=False,
    )
```

```python
import functools
import math

import jax
import jax.numpy as jnp
from jax import lax
from jax.experimental import pallas as pl
from jax.experimental.pallas import tpu as pltpu
from jax.sharding import PartitionSpec as P

SEASON = 168

beta_one = 0.9
beta_two = 0.999
adam_eps = 1e-08
step_rate = 0.05
factor_rate = 0.002
data_scale = 0.25

LIMIT = 32 * 1024 * 1024
F32 = jnp.float32
BF16 = jnp.bfloat16


def whole():
    return pl.BlockSpec(memory_space=pltpu.VMEM)


def far():
    return pl.BlockSpec(memory_space=pltpu.HBM)


def held(value):
    return pltpu.with_memory_space_constraint(value, pltpu.HBM)


def scalars():
    return pl.BlockSpec(memory_space=pltpu.SMEM)


def params(**more):
    return pltpu.CompilerParams(vmem_limit_bytes=LIMIT, **more)


def cost(flops, moved):
    return pl.CostEstimate(flops=int(flops), bytes_accessed=int(moved), transcendentals=0)


def rows_of(total, most):
    best = total
    for rows in range(128, most + 1, 128):
        if total % rows == 0:
            best = rows
    return best


def chunk_copies(rows, index, rank, hbm, both_ref, bits_ref, at, sems):
    obs_hbm, bits_hbm, f_hbm = hbm
    width = both_ref.shape[1] - rank
    source, target = pl.ds(index * rows, rows), pl.ds(at, rows)
    return (
        pltpu.make_async_copy(bits_hbm.at[:, source], bits_ref.at[:, target], sems.at[0]),
        pltpu.make_async_copy(
            f_hbm.at[source, :], both_ref.at[target, pl.ds(0, rank)], sems.at[1]
        ),
        pltpu.make_async_copy(
            obs_hbm.at[source, :], both_ref.at[target, pl.ds(rank, width)], sems.at[2]
        ),
    )


def prepare_kernel(
    rows, x_hbm, obs_hbm, bits_hbm, f_hbm, tail_ref, turned_ref, x_ref, both_ref, bits_ref, sem, sems
):
    copy = pltpu.make_async_copy(x_hbm.at[0], x_ref, sem)
    copy.start()
    rank = x_ref.shape[0]
    first = chunk_copies(rows, 0, rank, (obs_hbm, bits_hbm, f_hbm), both_ref, bits_ref, 0, sems)
    for other in first:
        other.start()
    copy.wait()
    turned_ref[...] = x_ref[...].T
    tail_ref[...] = turned_ref[turned_ref.shape[0] - SEASON :, :]
    for other in first:
        other.wait()


def prepare(x, obs, bits, factors, rows):
    rank, width = x.shape[1:]
    return pl.pallas_call(
        functools.partial(prepare_kernel, rows),
        out_shape=(
            jax.ShapeDtypeStruct((SEASON, rank), F32),
            jax.ShapeDtypeStruct((width, rank), F32),
            jax.ShapeDtypeStruct((rank, width), F32),
            jax.ShapeDtypeStruct((rows, rank + width), BF16),
            jax.ShapeDtypeStruct((bits.shape[0], rows), jnp.int32),
        ),
        in_specs=[far()] * 4,
        out_specs=(whole(),) * 5,
        scratch_shapes=[pltpu.SemaphoreType.DMA(()), pltpu.SemaphoreType.DMA((3,))],
        compiler_params=params(),
        cost_estimate=cost(0, 4 * rank * width * 4 + rows * (rank + width) * 4),
        name="prepare",
    )(held(x), held(obs), held(bits), held(factors))


def error_kernel(
    rows,
    obs_hbm,
    bits_hbm,
    f_hbm,
    turned_ref,
    first_ref,
    first_bits_ref,
    err_ref,
    both_ref,
    gd_ref,
    bits_ref,
    sems,
):
    width, series = err_ref.shape
    rank = turned_ref.shape[1]
    words = bits_ref.shape[0]
    per = width // words
    chunks = series // rows

    def copies(index):
        return chunk_copies(
            rows, index, rank, (obs_hbm, bits_hbm, f_hbm),
            both_ref, bits_ref, (index - 1) * rows, sems.at[index - 1],
        )

    def pair(index):
        if index == 0:
            return first_ref[...], first_bits_ref[...]
        part = pl.ds((index - 1) * rows, rows)
        return both_ref[part, :], bits_ref[:, part]

    for index in range(1, chunks):
        for copy in copies(index):
            copy.start()
    row = lax.broadcasted_iota(jnp.int32, (width, width), 0)
    column = lax.broadcasted_iota(jnp.int32, (width, width), 1)
    weights = jnp.concatenate(
        [turned_ref[...].astype(BF16), jnp.where(row == column, -1.0, 0.0).astype(BF16)], axis=1
    )
    flag = jnp.left_shift(1, lax.broadcasted_iota(jnp.int32, (1, per, 1), 1))

    def compare(index):
        if index > 0:
            for copy in copies(index):
                copy.wait()
        return lax.dot_general(
            weights, pair(index)[0], (((1,), (1,)), ((), ())), preferred_element_type=F32
        )

    def settle(index, gap):
        part = pl.ds(index * rows, rows)
        both, bits = pair(index)
        seen = jnp.bitwise_and(bits[:, None, :], flag) != 0
        error = jnp.where(seen, gap.reshape(words, per, rows), 0.0).reshape(width, rows)
        error = error.astype(BF16)
        err_ref[:, part] = error
        term = jnp.dot(error, both[:, :rank], preferred_element_type=F32)
        if index == 0:
            gd_ref[...] = term
        else:
            gd_ref[...] += term

    gap = compare(0)
    for index in range(chunks):
        later = compare(index + 1) if index + 1 < chunks else None
        settle(index, gap)
        gap = later


def error_step(obs, bits, factors, turned, first, first_bits):
    series, width = obs.shape
    rank = factors.shape[1]
    words = bits.shape[0]
    rows = first.shape[0]
    others = max(series - rows, rows)
    return pl.pallas_call(
        functools.partial(error_kernel, rows),
        out_shape=(
            jax.ShapeDtypeStruct((width, series), BF16),
            jax.ShapeDtypeStruct((others, rank + width), BF16),
            jax.ShapeDtypeStruct((width, rank), F32),
        ),
        in_specs=[far(), far(), far(), whole(), whole(), whole()],
        out_specs=(whole(), whole(), whole()),
        scratch_shapes=[
            pltpu.VMEM((words, others), jnp.int32),
            pltpu.SemaphoreType.DMA((others // rows, 3)),
        ],
        compiler_params=params(),
        cost_estimate=cost(8 * series * width * rank, series * (3 * width * 2 + words * 4)),
        name="errors",
    )(held(obs), held(bits), held(factors), turned, first, first_bits)


def factor_kernel(begin, rows, chunks, first_ref, both_ref, err_ref, turned_ref, *rest):
    out_hbm, out_ref, sems = rest[-3:]
    half = turned_ref[...].astype(BF16)
    size = rows // chunks

    def copy(index):
        return pltpu.make_async_copy(
            out_ref.at[pl.ds(index * size, size), :],
            out_hbm.at[pl.ds(begin + index * size, size), :],
            sems.at[index],
        )

    for index in range(chunks):
        part = pl.ds(begin + index * size, size)
        split = first_ref.shape[0]
        if begin + index * size < split:
            old = first_ref[part, pl.ds(0, half.shape[1])]
        else:
            old = both_ref[pl.ds(begin + index * size - split, size), pl.ds(0, half.shape[1])]
        gradient = lax.dot_general(
            err_ref[:, part], half, (((0,), (0,)), ((), ())), preferred_element_type=F32
        )
        out_ref[pl.ds(index * size, size), :] = (
            old.astype(F32) - factor_rate * gradient
        ).astype(BF16)
        copy(index).start()
    for index in range(chunks):
        copy(index).wait()


def factor_step(first, both, err, turned, after, sofar, begin, rows):
    width, series = err.shape
    rank = turned.shape[1]
    chunks = rows // math.gcd(first.shape[0], rows, begin)
    rest = (after,) if sofar is None else (after, sofar)
    return pl.pallas_call(
        functools.partial(factor_kernel, begin, rows, chunks),
        out_shape=jax.ShapeDtypeStruct((series, rank), BF16),
        in_specs=[whole()] * 4 + [pl.BlockSpec(memory_space=pl.ANY)] * len(rest),
        out_specs=far(),
        input_output_aliases={} if sofar is None else {5: 0},
        scratch_shapes=[pltpu.VMEM((rows, rank), BF16), pltpu.SemaphoreType.DMA((chunks,))],
        compiler_params=params(),
        cost_estimate=cost(2 * rows * width * rank, rows * 3 * width * 2),
        name="factors",
    )(first, both, err, turned, *rest)


def regress_kernel(
    lanes, turned_ref, w_ref, gd_ref, m_hbm, v_hbm, base_ref, m_ref, v_ref, z_ref, r_ref, sems
):
    m_copy = pltpu.make_async_copy(m_hbm.at[0], m_ref, sems.at[0])
    v_copy = pltpu.make_async_copy(v_hbm.at[0], v_ref, sems.at[1])
    m_copy.start()
    v_copy.start()
    width, rank = turned_ref.shape
    lags = list(range(1, w_ref.shape[0])) + [SEASON]
    for part in range(rank // lanes):
        columns = slice(part * lanes, (part + 1) * lanes)
        z_ref[part, :SEASON, :] = jnp.zeros((SEASON, lanes), F32)
        z_ref[part, SEASON:, :] = turned_ref[:, columns]
        r_ref[part, width:, :] = jnp.zeros((SEASON, lanes), F32)
        resid = turned_ref[:, columns]
        for index, lag in enumerate(lags):
            begin = SEASON - lag
            resid = resid - w_ref[index : index + 1, columns] * z_ref[part, begin : begin + width, :]
        r_ref[part, :width, :] = resid
        back = data_scale * gd_ref[:, columns] + resid
        for index, lag in enumerate(lags):
            back = back - w_ref[index : index + 1, columns] * r_ref[part, lag : lag + width, :]
        base_ref[:, columns] = back
    m_copy.wait()
    v_copy.wait()


def regress_step(turned, weights, gd, m, v):
    width, rank = gd.shape
    lanes = 128
    return pl.pallas_call(
        functools.partial(regress_kernel, lanes),
        out_shape=(
            jax.ShapeDtypeStruct((width, rank), F32),
            jax.ShapeDtypeStruct((rank, width), F32),
            jax.ShapeDtypeStruct((rank, width), F32),
        ),
        in_specs=[whole()] * 3 + [far()] * 2,
        out_specs=(whole(),) * 3,
        scratch_shapes=[
            pltpu.VMEM((rank // lanes, SEASON + width, lanes), F32),
            pltpu.VMEM((rank // lanes, SEASON + width, lanes), F32),
            pltpu.SemaphoreType.DMA((2,)),
        ],
        compiler_params=params(),
        cost_estimate=cost(100 * rank * width, 6 * rank * width * 4),
        name="regress",
    )(turned, weights, gd, held(m), held(v))


def update_kernel(
    count, sizes, lanes, stratum_ref, halo_ref, w_ref, base_ref, x_ref, m_ref, v_ref, *rest
):
    outs, (z_ref, r_ref, new_ref) = rest[: 2 * len(sizes)], rest[2 * len(sizes) :]
    width, rank = base_ref.shape
    share = rank // count
    short = w_ref.shape[0] - 1
    reach = -(-short // 8) * 8
    block_index = lax.rem(lax.axis_index("blk") + stratum_ref[...], lax.axis_size("blk"))
    for part in range(rank // lanes):
        columns = slice(part * lanes, (part + 1) * lanes)
        halo = jnp.where(block_index == 0, 0.0, halo_ref[:, columns])
        z_ref[part, :SEASON, :] = halo
        z_ref[part, SEASON:, :] = jnp.zeros((reach, lanes), F32)
        r_ref[part, :SEASON, :] = -w_ref[short : short + 1, columns] * halo
        r_ref[part, SEASON:, :] = jnp.zeros((reach, lanes), F32)
        first_rows = r_ref[part, :reach, :]
        for lag in range(1, short + 1):
            begin = SEASON - lag
            first_rows = first_rows - w_ref[lag - 1 : lag, columns] * z_ref[part, begin : begin + reach, :]
        r_ref[part, :reach, :] = first_rows
        back = r_ref[part, :SEASON, :]
        for lag in range(1, short + 1):
            back = back - w_ref[lag - 1 : lag, columns] * r_ref[part, lag : lag + SEASON, :]
        base_ref[:SEASON, columns] += back
    for part in range(rank // lanes):
        rows = slice(part * lanes, (part + 1) * lanes)
        gradient = base_ref[:, rows].T
        first = beta_one * m_ref[rows, :] + (1.0 - beta_one) * gradient
        second = beta_two * v_ref[rows, :] + (1.0 - beta_two) * gradient * gradient
        new_ref[0, rows, :] = x_ref[rows, :] - step_rate * first / (jnp.sqrt(second) + adam_eps)
        new_ref[1, rows, :] = first
        new_ref[2, rows, :] = second
    odd = lax.axis_index("grp") % 2
    begin = 0
    for piece, size in enumerate(sizes):
        for line in range(count // 2):
            for side in range(2):
                one = 2 * line + (odd if side == 0 else 1 - odd)
                start = pl.multiple_of(one * share + begin, 8)
                for which in range(3):
                    outs[2 * piece + side][which, line] = new_ref[which, pl.ds(start, size), :]
        begin += size


def update_step(stratum, halo, weights, base, x, m, v, count, sizes):
    width, rank = base.shape
    lanes = 128
    reach = -(-(weights.shape[0] - 1) // 8) * 8
    kinds = []
    for size in sizes:
        kinds += [jax.ShapeDtypeStruct((3, count // 2, size, width), F32)] * 2

    def kernel(stratum_ref, halo_ref, w_ref, base_ref, x_ref, m_ref, v_ref, *rest):
        work = rest[-1]
        work[...] = base_ref[...]
        update_kernel(
            count, sizes, lanes, stratum_ref, halo_ref, w_ref, work, x_ref, m_ref, v_ref, *rest[:-1]
        )

    outs = pl.pallas_call(
        kernel,
        out_shape=tuple(kinds),
        in_specs=[whole()] * 7,
        out_specs=(whole(),) * len(kinds),
        scratch_shapes=[
            pltpu.VMEM((rank // lanes, SEASON + reach, lanes), F32),
            pltpu.VMEM((rank // lanes, SEASON + reach, lanes), F32),
            pltpu.VMEM((3, rank, width), F32),
            pltpu.VMEM((width, rank), F32),
        ],
        compiler_params=params(),
        cost_estimate=cost(60 * rank * width, 10 * rank * width * 4),
        name="update",
    )(stratum.reshape(1, 1), halo, weights, base, x, m, v)
    return [(outs[2 * piece], outs[2 * piece + 1]) for piece in range(len(sizes))]


def halve_kernel(level, kept_ref, got_ref, keep_ref, send_ref):
    mine = (lax.axis_index("grp") // level) % 2
    for line in range(keep_ref.shape[1]):
        for out, side in ((keep_ref, mine), (send_ref, 1 - mine)):
            for which in range(3):
                out[which, line] = kept_ref[which, 2 * line + side] + got_ref[which, 2 * line + side]


def halve(kept, got, level):
    _, lines, size, width = kept.shape
    out = jax.ShapeDtypeStruct((3, lines // 2, size, width), F32)
    return pl.pallas_call(
        functools.partial(halve_kernel, level),
        out_shape=(out, out),
        in_specs=[whole(), whole()],
        out_specs=(whole(), whole()),
        compiler_params=params(),
        cost_estimate=cost(kept.size, 3 * kept.size * 4),
        name="halve",
    )(kept, got)


def mean_kernel(count, kept_ref, got_ref, out_ref):
    for which in range(3):
        out_ref[which] = (kept_ref[which, 0] + got_ref[which, 0]) / count


def mean(kept, got, count):
    _, _, size, width = kept.shape
    return pl.pallas_call(
        functools.partial(mean_kernel, count),
        out_shape=jax.ShapeDtypeStruct((3, size, width), F32),
        in_specs=[whole(), whole()],
        out_specs=whole(),
        compiler_params=params(),
        cost_estimate=cost(2 * kept.size, 3 * kept.size * 4),
        name="mean",
    )(kept, got)


def place_kernel(share, spots, *rest):
    outs, sems = rest[-4:-1], rest[-1]
    group = lax.axis_index("grp")
    copies = []
    for index, (step, begin) in enumerate(spots):
        part = rest[index]
        start = pl.multiple_of((group ^ step) * share + begin, 8)
        for which in range(3):
            copies.append(
                pltpu.make_async_copy(
                    part.at[which],
                    outs[which].at[0, pl.ds(start, part.shape[1]), :],
                    sems.at[index, which],
                )
            )
    for copy in copies:
        copy.start()
    for copy in copies:
        copy.wait()


def place(parts, spots, share, count, sofar):
    width = parts[0].shape[2]
    out = jax.ShapeDtypeStruct((1, count * share, width), F32)
    return pl.pallas_call(
        functools.partial(place_kernel, share, spots),
        out_shape=(out, out, out),
        in_specs=[pl.BlockSpec(memory_space=pl.ANY)] * (len(parts) + len(sofar)),
        out_specs=(far(), far(), far()),
        input_output_aliases={len(parts) + which: which for which in range(len(sofar))},
        scratch_shapes=[pltpu.SemaphoreType.DMA((len(parts), 3))],
        compiler_params=params(),
        cost_estimate=cost(0, 6 * sum(part.size for part in parts) * 4),
        name="place",
    )(*parts, *sofar)


def crossed(value, step):
    count = lax.axis_size("grp")
    return lax.ppermute(value, "grp", [(source, source ^ step) for source in range(count)])


def shifted(value, steps):
    count = lax.axis_size("blk")
    return lax.ppermute(value, "blk", [(source, (source + steps) % count) for source in range(count)])


def delivered(value, step):
    groups, slots = lax.axis_size("grp"), lax.axis_size("blk")
    pairs = [
        (group * slots + slot, (group ^ step) * slots + (slot - 1) % slots)
        for group in range(groups)
        for slot in range(slots)
    ]
    return lax.ppermute(value, ("grp", "blk"), pairs)


def body(obs, mask_bits, factors, x_blocks, first_moment, second_moment, ar_weights, stratum):
    count = lax.axis_size("grp")
    series = obs.shape[0]
    rows = rows_of(series, 1024)
    third = max(series // rows // 3, 1) * rows
    bits = mask_bits.T

    tail, turned, x, lead, lead_bits = prepare(x_blocks, obs, bits, factors, rows)
    halo = shifted(tail, 1)
    err, kept, gd = error_step(obs, bits, factors, turned, lead, lead_bits)
    base, first, second = regress_step(turned, ar_weights, gd, first_moment, second_moment)
    share = x.shape[0] // count
    half = share // 2
    (keep0, send0), (keep1, send1) = update_step(
        stratum, halo, ar_weights, base, x, first, second, count, (half, share - half)
    )

    got0 = crossed(send0, 1)
    got1 = crossed(send1, 1)
    keep0, send0 = halve(keep0, got0, 2)
    far0 = crossed(send0, 2)
    factor_new = factor_step(lead, kept, err, turned, send0, None, 0, third)
    got1, factor_new = lax.optimization_barrier((got1, factor_new))
    keep1, send1 = halve(keep1, got1, 2)
    far1 = crossed(send1, 2)
    mean0 = mean(keep0, far0, count)

    near0 = delivered(mean0, 0)
    mean1 = mean(keep1, far1, count)
    near1 = delivered(mean1, 0)
    side1 = delivered(mean1, 2)
    side0 = crossed(near0, 2)
    factor_new = factor_step(lead, kept, err, turned, near0, factor_new, third, series - third)
    near1, factor_new = lax.optimization_barrier((near1, factor_new))
    parts = [near0, crossed(near0, 1), side0]
    parts += [near1, crossed(near1, 1), side1, crossed(side1, 1)]
    spots = [(0, 0), (1, 0), (2, 0), (0, half), (1, half), (2, half), (3, half)]
    outs = place(parts, spots, share, count, ())
    outs = place([crossed(side0, 1)], [(3, 0)], share, count, outs)
    return (factor_new, *outs)


def solution(mesh):
    rows = P(("grp", "blk"), None)
    blocks = P("grp", None, "blk")
    return jax.shard_map(
        body,
        mesh=mesh,
        in_specs=(rows, rows, rows, blocks, blocks, blocks, P(), P()),
        out_specs=(rows, blocks, blocks, blocks),
        check_vma=False,
    )
```

```python
import functools
import math

import jax
import jax.numpy as jnp
from jax import lax
from jax.experimental import pallas as pl
from jax.experimental.pallas import tpu as pltpu
from jax.sharding import PartitionSpec as P

SEASON = 168

beta_one = 0.9
beta_two = 0.999
adam_eps = 1e-08
step_rate = 0.05
factor_rate = 0.002
data_scale = 0.25

LIMIT = 32 * 1024 * 1024
F32 = jnp.float32
BF16 = jnp.bfloat16


def whole():
    return pl.BlockSpec(memory_space=pltpu.VMEM)


def far():
    return pl.BlockSpec(memory_space=pltpu.HBM)


def held(value):
    return pltpu.with_memory_space_constraint(value, pltpu.HBM)


def scalars():
    return pl.BlockSpec(memory_space=pltpu.SMEM)


def params(**more):
    return pltpu.CompilerParams(vmem_limit_bytes=LIMIT, **more)


def cost(flops, moved):
    return pl.CostEstimate(flops=int(flops), bytes_accessed=int(moved), transcendentals=0)


def rows_of(total, most):
    best = total
    for rows in range(128, most + 1, 128):
        if total % rows == 0:
            best = rows
    return best


def chunk_copies(rows, index, rank, hbm, both_ref, bits_ref, at, sems):
    obs_hbm, bits_hbm, f_hbm = hbm
    width = both_ref.shape[1] - rank
    source, target = pl.ds(index * rows, rows), pl.ds(at, rows)
    return (
        pltpu.make_async_copy(bits_hbm.at[:, source], bits_ref.at[:, target], sems.at[0]),
        pltpu.make_async_copy(
            f_hbm.at[source, :], both_ref.at[target, pl.ds(0, rank)], sems.at[1]
        ),
        pltpu.make_async_copy(
            obs_hbm.at[source, :], both_ref.at[target, pl.ds(rank, width)], sems.at[2]
        ),
    )


def prepare_kernel(
    rows, x_hbm, obs_hbm, bits_hbm, f_hbm, tail_ref, turned_ref, x_ref, both_ref, bits_ref, sem, sems
):
    copy = pltpu.make_async_copy(x_hbm.at[0], x_ref, sem)
    copy.start()
    rank = x_ref.shape[0]
    first = chunk_copies(rows, 0, rank, (obs_hbm, bits_hbm, f_hbm), both_ref, bits_ref, 0, sems)
    for other in first:
        other.start()
    copy.wait()
    turned_ref[...] = x_ref[...].T
    tail_ref[...] = turned_ref[turned_ref.shape[0] - SEASON :, :]
    for other in first:
        other.wait()


def prepare(x, obs, bits, factors, rows):
    rank, width = x.shape[1:]
    return pl.pallas_call(
        functools.partial(prepare_kernel, rows),
        out_shape=(
            jax.ShapeDtypeStruct((SEASON, rank), F32),
            jax.ShapeDtypeStruct((width, rank), F32),
            jax.ShapeDtypeStruct((rank, width), F32),
            jax.ShapeDtypeStruct((rows, rank + width), BF16),
            jax.ShapeDtypeStruct((bits.shape[0], rows), jnp.int32),
        ),
        in_specs=[far()] * 4,
        out_specs=(whole(),) * 5,
        scratch_shapes=[pltpu.SemaphoreType.DMA(()), pltpu.SemaphoreType.DMA((3,))],
        compiler_params=params(),
        cost_estimate=cost(0, 4 * rank * width * 4 + rows * (rank + width) * 4),
        name="prepare",
    )(held(x), held(obs), held(bits), held(factors))


def error_kernel(
    rows,
    obs_hbm,
    bits_hbm,
    f_hbm,
    turned_ref,
    first_ref,
    first_bits_ref,
    err_ref,
    both_ref,
    gd_ref,
    bits_ref,
    sems,
):
    width, series = err_ref.shape
    rank = turned_ref.shape[1]
    words = bits_ref.shape[0]
    per = width // words
    chunks = series // rows

    def copies(index):
        return chunk_copies(
            rows, index, rank, (obs_hbm, bits_hbm, f_hbm),
            both_ref, bits_ref, (index - 1) * rows, sems.at[index - 1],
        )

    def pair(index):
        if index == 0:
            return first_ref[...], first_bits_ref[...]
        part = pl.ds((index - 1) * rows, rows)
        return both_ref[part, :], bits_ref[:, part]

    for index in range(1, chunks):
        for copy in copies(index):
            copy.start()
    row = lax.broadcasted_iota(jnp.int32, (width, width), 0)
    column = lax.broadcasted_iota(jnp.int32, (width, width), 1)
    weights = jnp.concatenate(
        [turned_ref[...].astype(BF16), jnp.where(row == column, -1.0, 0.0).astype(BF16)], axis=1
    )
    flag = jnp.left_shift(1, lax.broadcasted_iota(jnp.int32, (1, per, 1), 1))

    def compare(index):
        if index > 0:
            for copy in copies(index):
                copy.wait()
        return lax.dot_general(
            weights, pair(index)[0], (((1,), (1,)), ((), ())), preferred_element_type=F32
        )

    def settle(index, gap):
        part = pl.ds(index * rows, rows)
        both, bits = pair(index)
        seen = jnp.bitwise_and(bits[:, None, :], flag) != 0
        error = jnp.where(seen, gap.reshape(words, per, rows), 0.0).reshape(width, rows)
        error = error.astype(BF16)
        err_ref[:, part] = error
        term = jnp.dot(error, both[:, :rank], preferred_element_type=F32)
        if index == 0:
            gd_ref[...] = term
        else:
            gd_ref[...] += term

    gap = compare(0)
    for index in range(chunks):
        later = compare(index + 1) if index + 1 < chunks else None
        settle(index, gap)
        gap = later


def error_step(obs, bits, factors, turned, first, first_bits):
    series, width = obs.shape
    rank = factors.shape[1]
    words = bits.shape[0]
    rows = first.shape[0]
    others = max(series - rows, rows)
    return pl.pallas_call(
        functools.partial(error_kernel, rows),
        out_shape=(
            jax.ShapeDtypeStruct((width, series), BF16),
            jax.ShapeDtypeStruct((others, rank + width), BF16),
            jax.ShapeDtypeStruct((width, rank), F32),
        ),
        in_specs=[far(), far(), far(), whole(), whole(), whole()],
        out_specs=(whole(), whole(), whole()),
        scratch_shapes=[
            pltpu.VMEM((words, others), jnp.int32),
            pltpu.SemaphoreType.DMA((others // rows, 3)),
        ],
        compiler_params=params(),
        cost_estimate=cost(8 * series * width * rank, series * (3 * width * 2 + words * 4)),
        name="errors",
    )(held(obs), held(bits), held(factors), turned, first, first_bits)


def factor_kernel(begin, rows, chunks, first_ref, both_ref, err_ref, turned_ref, *rest):
    out_hbm, out_ref, sems = rest[-3:]
    half = turned_ref[...].astype(BF16)
    size = rows // chunks

    def copy(index):
        return pltpu.make_async_copy(
            out_ref.at[pl.ds(index * size, size), :],
            out_hbm.at[pl.ds(begin + index * size, size), :],
            sems.at[index],
        )

    for index in range(chunks):
        part = pl.ds(begin + index * size, size)
        split = first_ref.shape[0]
        if begin + index * size < split:
            old = first_ref[part, pl.ds(0, half.shape[1])]
        else:
            old = both_ref[pl.ds(begin + index * size - split, size), pl.ds(0, half.shape[1])]
        gradient = lax.dot_general(
            err_ref[:, part], half, (((0,), (0,)), ((), ())), preferred_element_type=F32
        )
        out_ref[pl.ds(index * size, size), :] = (
            old.astype(F32) - factor_rate * gradient
        ).astype(BF16)
        copy(index).start()
    for index in range(chunks):
        copy(index).wait()


def factor_step(first, both, err, turned, after, sofar, begin, rows):
    width, series = err.shape
    rank = turned.shape[1]
    chunks = rows // math.gcd(first.shape[0], rows, begin)
    rest = (after,) if sofar is None else (after, sofar)
    return pl.pallas_call(
        functools.partial(factor_kernel, begin, rows, chunks),
        out_shape=jax.ShapeDtypeStruct((series, rank), BF16),
        in_specs=[whole()] * 4 + [pl.BlockSpec(memory_space=pl.ANY)] * len(rest),
        out_specs=far(),
        input_output_aliases={} if sofar is None else {5: 0},
        scratch_shapes=[pltpu.VMEM((rows, rank), BF16), pltpu.SemaphoreType.DMA((chunks,))],
        compiler_params=params(),
        cost_estimate=cost(2 * rows * width * rank, rows * 3 * width * 2),
        name="factors",
    )(first, both, err, turned, *rest)


def regress_kernel(
    lanes, turned_ref, w_ref, gd_ref, m_hbm, v_hbm, base_ref, m_ref, v_ref, z_ref, r_ref, sems
):
    m_copy = pltpu.make_async_copy(m_hbm.at[0], m_ref, sems.at[0])
    v_copy = pltpu.make_async_copy(v_hbm.at[0], v_ref, sems.at[1])
    m_copy.start()
    v_copy.start()
    width, rank = turned_ref.shape
    lags = list(range(1, w_ref.shape[0])) + [SEASON]
    for part in range(rank // lanes):
        columns = slice(part * lanes, (part + 1) * lanes)
        z_ref[part, :SEASON, :] = jnp.zeros((SEASON, lanes), F32)
        z_ref[part, SEASON:, :] = turned_ref[:, columns]
        r_ref[part, width:, :] = jnp.zeros((SEASON, lanes), F32)
        resid = turned_ref[:, columns]
        for index, lag in enumerate(lags):
            begin = SEASON - lag
            resid = resid - w_ref[index : index + 1, columns] * z_ref[part, begin : begin + width, :]
        r_ref[part, :width, :] = resid
        back = data_scale * gd_ref[:, columns] + resid
        for index, lag in enumerate(lags):
            back = back - w_ref[index : index + 1, columns] * r_ref[part, lag : lag + width, :]
        base_ref[:, columns] = back
    m_copy.wait()
    v_copy.wait()


def regress_step(turned, weights, gd, m, v):
    width, rank = gd.shape
    lanes = 128
    return pl.pallas_call(
        functools.partial(regress_kernel, lanes),
        out_shape=(
            jax.ShapeDtypeStruct((width, rank), F32),
            jax.ShapeDtypeStruct((rank, width), F32),
            jax.ShapeDtypeStruct((rank, width), F32),
        ),
        in_specs=[whole()] * 3 + [far()] * 2,
        out_specs=(whole(),) * 3,
        scratch_shapes=[
            pltpu.VMEM((rank // lanes, SEASON + width, lanes), F32),
            pltpu.VMEM((rank // lanes, SEASON + width, lanes), F32),
            pltpu.SemaphoreType.DMA((2,)),
        ],
        compiler_params=params(),
        cost_estimate=cost(100 * rank * width, 6 * rank * width * 4),
        name="regress",
    )(turned, weights, gd, held(m), held(v))


def update_kernel(
    count, sizes, lanes, stratum_ref, halo_ref, w_ref, base_ref, x_ref, m_ref, v_ref, *rest
):
    outs, (z_ref, r_ref, new_ref) = rest[: 2 * len(sizes)], rest[2 * len(sizes) :]
    width, rank = base_ref.shape
    share = rank // count
    short = w_ref.shape[0] - 1
    reach = -(-short // 8) * 8
    block_index = lax.rem(lax.axis_index("blk") + stratum_ref[...], lax.axis_size("blk"))
    for part in range(rank // lanes):
        columns = slice(part * lanes, (part + 1) * lanes)
        halo = jnp.where(block_index == 0, 0.0, halo_ref[:, columns])
        z_ref[part, :SEASON, :] = halo
        z_ref[part, SEASON:, :] = jnp.zeros((reach, lanes), F32)
        r_ref[part, :SEASON, :] = -w_ref[short : short + 1, columns] * halo
        r_ref[part, SEASON:, :] = jnp.zeros((reach, lanes), F32)
        first_rows = r_ref[part, :reach, :]
        for lag in range(1, short + 1):
            begin = SEASON - lag
            first_rows = first_rows - w_ref[lag - 1 : lag, columns] * z_ref[part, begin : begin + reach, :]
        r_ref[part, :reach, :] = first_rows
        back = r_ref[part, :SEASON, :]
        for lag in range(1, short + 1):
            back = back - w_ref[lag - 1 : lag, columns] * r_ref[part, lag : lag + SEASON, :]
        base_ref[:SEASON, columns] += back
    for part in range(rank // lanes):
        rows = slice(part * lanes, (part + 1) * lanes)
        gradient = base_ref[:, rows].T
        first = beta_one * m_ref[rows, :] + (1.0 - beta_one) * gradient
        second = beta_two * v_ref[rows, :] + (1.0 - beta_two) * gradient * gradient
        new_ref[0, rows, :] = x_ref[rows, :] - step_rate * first / (jnp.sqrt(second) + adam_eps)
        new_ref[1, rows, :] = first
        new_ref[2, rows, :] = second
    odd = lax.axis_index("grp") % 2
    begin = 0
    for piece, size in enumerate(sizes):
        for line in range(count // 2):
            for side in range(2):
                one = 2 * line + (odd if side == 0 else 1 - odd)
                start = pl.multiple_of(one * share + begin, 8)
                for which in range(3):
                    outs[2 * piece + side][which, line] = new_ref[which, pl.ds(start, size), :]
        begin += size


def update_step(stratum, halo, weights, base, x, m, v, count, sizes):
    width, rank = base.shape
    lanes = 128
    reach = -(-(weights.shape[0] - 1) // 8) * 8
    kinds = []
    for size in sizes:
        kinds += [jax.ShapeDtypeStruct((3, count // 2, size, width), F32)] * 2

    def kernel(stratum_ref, halo_ref, w_ref, base_ref, x_ref, m_ref, v_ref, *rest):
        work = rest[-1]
        work[...] = base_ref[...]
        update_kernel(
            count, sizes, lanes, stratum_ref, halo_ref, w_ref, work, x_ref, m_ref, v_ref, *rest[:-1]
        )

    outs = pl.pallas_call(
        kernel,
        out_shape=tuple(kinds),
        in_specs=[whole()] * 7,
        out_specs=(whole(),) * len(kinds),
        scratch_shapes=[
            pltpu.VMEM((rank // lanes, SEASON + reach, lanes), F32),
            pltpu.VMEM((rank // lanes, SEASON + reach, lanes), F32),
            pltpu.VMEM((3, rank, width), F32),
            pltpu.VMEM((width, rank), F32),
        ],
        compiler_params=params(),
        cost_estimate=cost(60 * rank * width, 10 * rank * width * 4),
        name="update",
    )(stratum.reshape(1, 1), halo, weights, base, x, m, v)
    return [(outs[2 * piece], outs[2 * piece + 1]) for piece in range(len(sizes))]


def halve_kernel(level, kept_ref, got_ref, keep_ref, send_ref):
    mine = (lax.axis_index("grp") // level) % 2
    for line in range(keep_ref.shape[1]):
        for out, side in ((keep_ref, mine), (send_ref, 1 - mine)):
            for which in range(3):
                out[which, line] = kept_ref[which, 2 * line + side] + got_ref[which, 2 * line + side]


def halve(kept, got, level):
    _, lines, size, width = kept.shape
    out = jax.ShapeDtypeStruct((3, lines // 2, size, width), F32)
    return pl.pallas_call(
        functools.partial(halve_kernel, level),
        out_shape=(out, out),
        in_specs=[whole(), whole()],
        out_specs=(whole(), whole()),
        compiler_params=params(),
        cost_estimate=cost(kept.size, 3 * kept.size * 4),
        name="halve",
    )(kept, got)


def mean_kernel(count, bounds, *rest):
    out_ref = rest[-1]
    at = 0
    for index, (low, high) in enumerate(bounds):
        kept_ref, got_ref = rest[2 * index : 2 * index + 2]
        for which in range(3):
            total = kept_ref[which, 0, low:high, :] + got_ref[which, 0, low:high, :]
            out_ref[which, at : at + high - low, :] = total / count
        at += high - low


def mean(pairs, bounds, count):
    width = pairs[0][0].shape[3]
    size = sum(high - low for low, high in bounds)
    return pl.pallas_call(
        functools.partial(mean_kernel, count, bounds),
        out_shape=jax.ShapeDtypeStruct((3, size, width), F32),
        in_specs=[whole()] * (2 * len(pairs)),
        out_specs=whole(),
        compiler_params=params(),
        cost_estimate=cost(6 * size * width, 36 * size * width),
        name="mean",
    )(*[part for pair in pairs for part in pair])


def place_kernel(share, spots, *rest):
    outs, sems = rest[-4:-1], rest[-1]
    group = lax.axis_index("grp")
    copies = []
    for index, (step, begin) in enumerate(spots):
        part = rest[index]
        start = pl.multiple_of((group ^ step) * share + begin, 8)
        for which in range(3):
            copies.append(
                pltpu.make_async_copy(
                    part.at[which],
                    outs[which].at[0, pl.ds(start, part.shape[1]), :],
                    sems.at[index, which],
                )
            )
    for copy in copies:
        copy.start()
    for copy in copies:
        copy.wait()


def place(parts, spots, share, count, sofar):
    width = parts[0].shape[2]
    out = jax.ShapeDtypeStruct((1, count * share, width), F32)
    return pl.pallas_call(
        functools.partial(place_kernel, share, spots),
        out_shape=(out, out, out),
        in_specs=[pl.BlockSpec(memory_space=pl.ANY)] * (len(parts) + len(sofar)),
        out_specs=(far(), far(), far()),
        input_output_aliases={len(parts) + which: which for which in range(len(sofar))},
        scratch_shapes=[pltpu.SemaphoreType.DMA((len(parts), 3))],
        compiler_params=params(),
        cost_estimate=cost(0, 6 * sum(part.size for part in parts) * 4),
        name="place",
    )(*parts, *sofar)


def crossed(value, step):
    count = lax.axis_size("grp")
    return lax.ppermute(value, "grp", [(source, source ^ step) for source in range(count)])


def shifted(value, steps):
    count = lax.axis_size("blk")
    return lax.ppermute(value, "blk", [(source, (source + steps) % count) for source in range(count)])


def delivered(value, step):
    groups, slots = lax.axis_size("grp"), lax.axis_size("blk")
    pairs = [
        (group * slots + slot, (group ^ step) * slots + (slot - 1) % slots)
        for group in range(groups)
        for slot in range(slots)
    ]
    return lax.ppermute(value, ("grp", "blk"), pairs)


def body(obs, mask_bits, factors, x_blocks, first_moment, second_moment, ar_weights, stratum):
    count = lax.axis_size("grp")
    series = obs.shape[0]
    rows = rows_of(series, 1024)
    third = max(series // rows // 3, 1) * rows
    bits = mask_bits.T

    tail, turned, x, lead, lead_bits = prepare(x_blocks, obs, bits, factors, rows)
    halo = shifted(tail, 1)
    err, kept, gd = error_step(obs, bits, factors, turned, lead, lead_bits)
    base, first, second = regress_step(turned, ar_weights, gd, first_moment, second_moment)
    share = x.shape[0] // count
    half = share // 2
    (keep0, send0), (keep1, send1) = update_step(
        stratum, halo, ar_weights, base, x, first, second, count, (half, share - half)
    )

    got0 = crossed(send0, 1)
    got1 = crossed(send1, 1)
    keep0, send0 = halve(keep0, got0, 2)
    far0 = crossed(send0, 2)
    factor_new = factor_step(lead, kept, err, turned, send0, None, 0, third)
    got1, factor_new = lax.optimization_barrier((got1, factor_new))
    keep1, send1 = halve(keep1, got1, 2)
    far1 = crossed(send1, 2)
    small = max(half * 3 // 4 // 8 * 8, 8)
    mean0 = mean([(keep0, far0)], [(0, small)], count)

    near0 = delivered(mean0, 0)
    mean1 = mean(
        [(keep0, far0), (keep1, far1)], [(small, half), (0, share - half)], count
    )
    near1 = delivered(mean1, 0)
    side1 = delivered(mean1, 2)
    side0 = crossed(near0, 2)
    factor_new = factor_step(lead, kept, err, turned, near0, factor_new, third, series - third)
    near1, factor_new = lax.optimization_barrier((near1, factor_new))
    parts = [near0, crossed(near0, 1), side0]
    parts += [near1, crossed(near1, 1), side1, crossed(side1, 1)]
    spots = [(0, 0), (1, 0), (2, 0), (0, small), (1, small), (2, small), (3, small)]
    outs = place(parts, spots, share, count, ())
    outs = place([crossed(side0, 1)], [(3, 0)], share, count, outs)
    return (factor_new, *outs)


def solution(mesh):
    rows = P(("grp", "blk"), None)
    blocks = P("grp", None, "blk")
    return jax.shard_map(
        body,
        mesh=mesh,
        in_specs=(rows, rows, rows, blocks, blocks, blocks, P(), P()),
        out_specs=(rows, blocks, blocks, blocks),
        check_vma=False,
    )
```

```python
import functools
import math

import jax
import jax.numpy as jnp
from jax import lax
from jax.experimental import pallas as pl
from jax.experimental.pallas import tpu as pltpu
from jax.sharding import PartitionSpec as P

SEASON = 168

beta_one = 0.9
beta_two = 0.999
adam_eps = 1e-08
step_rate = 0.05
factor_rate = 0.002
data_scale = 0.25

LIMIT = 32 * 1024 * 1024
F32 = jnp.float32
BF16 = jnp.bfloat16


def whole():
    return pl.BlockSpec(memory_space=pltpu.VMEM)


def far():
    return pl.BlockSpec(memory_space=pltpu.HBM)


def held(value):
    return pltpu.with_memory_space_constraint(value, pltpu.HBM)


def scalars():
    return pl.BlockSpec(memory_space=pltpu.SMEM)


def params(**more):
    return pltpu.CompilerParams(vmem_limit_bytes=LIMIT, **more)


def cost(flops, moved):
    return pl.CostEstimate(flops=int(flops), bytes_accessed=int(moved), transcendentals=0)


def rows_of(total, most):
    best = total
    for rows in range(128, most + 1, 128):
        if total % rows == 0:
            best = rows
    return best


def chunk_copies(rows, index, rank, hbm, both_ref, bits_ref, at, sems):
    obs_hbm, bits_hbm, f_hbm = hbm
    width = both_ref.shape[1] - rank
    source, target = pl.ds(index * rows, rows), pl.ds(at, rows)
    return (
        pltpu.make_async_copy(bits_hbm.at[:, source], bits_ref.at[:, target], sems.at[0]),
        pltpu.make_async_copy(
            f_hbm.at[source, :], both_ref.at[target, pl.ds(0, rank)], sems.at[1]
        ),
        pltpu.make_async_copy(
            obs_hbm.at[source, :], both_ref.at[target, pl.ds(rank, width)], sems.at[2]
        ),
    )


def prepare_kernel(
    rows, x_hbm, obs_hbm, bits_hbm, f_hbm, tail_ref, turned_ref, x_ref, both_ref, bits_ref, sem, sems
):
    copy = pltpu.make_async_copy(x_hbm.at[0], x_ref, sem)
    copy.start()
    rank = x_ref.shape[0]
    first = chunk_copies(rows, 0, rank, (obs_hbm, bits_hbm, f_hbm), both_ref, bits_ref, 0, sems)
    for other in first:
        other.start()
    copy.wait()
    turned_ref[...] = x_ref[...].T
    tail_ref[...] = turned_ref[turned_ref.shape[0] - SEASON :, :]
    for other in first:
        other.wait()


def prepare(x, obs, bits, factors, rows):
    rank, width = x.shape[1:]
    return pl.pallas_call(
        functools.partial(prepare_kernel, rows),
        out_shape=(
            jax.ShapeDtypeStruct((SEASON, rank), F32),
            jax.ShapeDtypeStruct((width, rank), F32),
            jax.ShapeDtypeStruct((rank, width), F32),
            jax.ShapeDtypeStruct((rows, rank + width), BF16),
            jax.ShapeDtypeStruct((bits.shape[0], rows), jnp.int32),
        ),
        in_specs=[far()] * 4,
        out_specs=(whole(),) * 5,
        scratch_shapes=[pltpu.SemaphoreType.DMA(()), pltpu.SemaphoreType.DMA((3,))],
        compiler_params=params(),
        cost_estimate=cost(0, 4 * rank * width * 4 + rows * (rank + width) * 4),
        name="prepare",
    )(held(x), held(obs), held(bits), held(factors))


def error_kernel(
    rows,
    obs_hbm,
    bits_hbm,
    f_hbm,
    turned_ref,
    first_ref,
    first_bits_ref,
    err_ref,
    both_ref,
    gd_ref,
    bits_ref,
    sems,
):
    width, series = err_ref.shape
    rank = turned_ref.shape[1]
    words = bits_ref.shape[0]
    per = width // words
    chunks = series // rows

    def copies(index):
        return chunk_copies(
            rows, index, rank, (obs_hbm, bits_hbm, f_hbm),
            both_ref, bits_ref, (index - 1) * rows, sems.at[index - 1],
        )

    def pair(index):
        if index == 0:
            return first_ref[...], first_bits_ref[...]
        part = pl.ds((index - 1) * rows, rows)
        return both_ref[part, :], bits_ref[:, part]

    for index in range(1, chunks):
        for copy in copies(index):
            copy.start()
    row = lax.broadcasted_iota(jnp.int32, (width, width), 0)
    column = lax.broadcasted_iota(jnp.int32, (width, width), 1)
    weights = jnp.concatenate(
        [turned_ref[...].astype(BF16), jnp.where(row == column, -1.0, 0.0).astype(BF16)], axis=1
    )
    flag = jnp.left_shift(1, lax.broadcasted_iota(jnp.int32, (1, per, 1), 1))

    def compare(index):
        if index > 0:
            for copy in copies(index):
                copy.wait()
        return lax.dot_general(
            weights, pair(index)[0], (((1,), (1,)), ((), ())), preferred_element_type=F32
        )

    def settle(index, gap):
        part = pl.ds(index * rows, rows)
        both, bits = pair(index)
        seen = jnp.bitwise_and(bits[:, None, :], flag) != 0
        error = jnp.where(seen, gap.reshape(words, per, rows), 0.0).reshape(width, rows)
        error = error.astype(BF16)
        err_ref[:, part] = error
        term = jnp.dot(error, both[:, :rank], preferred_element_type=F32)
        if index == 0:
            gd_ref[...] = term
        else:
            gd_ref[...] += term

    gap = compare(0)
    for index in range(chunks):
        later = compare(index + 1) if index + 1 < chunks else None
        settle(index, gap)
        gap = later


def error_step(obs, bits, factors, turned, first, first_bits):
    series, width = obs.shape
    rank = factors.shape[1]
    words = bits.shape[0]
    rows = first.shape[0]
    others = max(series - rows, rows)
    return pl.pallas_call(
        functools.partial(error_kernel, rows),
        out_shape=(
            jax.ShapeDtypeStruct((width, series), BF16),
            jax.ShapeDtypeStruct((others, rank + width), BF16),
            jax.ShapeDtypeStruct((width, rank), F32),
        ),
        in_specs=[far(), far(), far(), whole(), whole(), whole()],
        out_specs=(whole(), whole(), whole()),
        scratch_shapes=[
            pltpu.VMEM((words, others), jnp.int32),
            pltpu.SemaphoreType.DMA((others // rows, 3)),
        ],
        compiler_params=params(),
        cost_estimate=cost(8 * series * width * rank, series * (3 * width * 2 + words * 4)),
        name="errors",
    )(held(obs), held(bits), held(factors), turned, first, first_bits)


def factor_kernel(begin, rows, chunks, first_ref, both_ref, err_ref, turned_ref, *rest):
    out_hbm, out_ref, sems = rest[-3:]
    half = turned_ref[...].astype(BF16)
    size = rows // chunks

    def copy(index):
        return pltpu.make_async_copy(
            out_ref.at[pl.ds(index * size, size), :],
            out_hbm.at[pl.ds(begin + index * size, size), :],
            sems.at[index],
        )

    for index in range(chunks):
        part = pl.ds(begin + index * size, size)
        split = first_ref.shape[0]
        if begin + index * size < split:
            old = first_ref[part, pl.ds(0, half.shape[1])]
        else:
            old = both_ref[pl.ds(begin + index * size - split, size), pl.ds(0, half.shape[1])]
        gradient = lax.dot_general(
            err_ref[:, part], half, (((0,), (0,)), ((), ())), preferred_element_type=F32
        )
        out_ref[pl.ds(index * size, size), :] = (
            old.astype(F32) - factor_rate * gradient
        ).astype(BF16)
        copy(index).start()
    for index in range(chunks):
        copy(index).wait()


def factor_step(first, both, err, turned, after, sofar, begin, rows):
    width, series = err.shape
    rank = turned.shape[1]
    chunks = rows // math.gcd(first.shape[0], rows, begin)
    rest = (after,) if sofar is None else (after, sofar)
    return pl.pallas_call(
        functools.partial(factor_kernel, begin, rows, chunks),
        out_shape=jax.ShapeDtypeStruct((series, rank), BF16),
        in_specs=[whole()] * 4 + [pl.BlockSpec(memory_space=pl.ANY)] * len(rest),
        out_specs=far(),
        input_output_aliases={} if sofar is None else {5: 0},
        scratch_shapes=[pltpu.VMEM((rows, rank), BF16), pltpu.SemaphoreType.DMA((chunks,))],
        compiler_params=params(),
        cost_estimate=cost(2 * rows * width * rank, rows * 3 * width * 2),
        name="factors",
    )(first, both, err, turned, *rest)


def regress_kernel(
    lanes, turned_ref, w_ref, gd_ref, m_hbm, v_hbm, base_ref, m_ref, v_ref, z_ref, r_ref, sems
):
    m_copy = pltpu.make_async_copy(m_hbm.at[0], m_ref, sems.at[0])
    v_copy = pltpu.make_async_copy(v_hbm.at[0], v_ref, sems.at[1])
    m_copy.start()
    v_copy.start()
    width, rank = turned_ref.shape
    lags = list(range(1, w_ref.shape[0])) + [SEASON]
    for part in range(rank // lanes):
        columns = slice(part * lanes, (part + 1) * lanes)
        z_ref[part, :SEASON, :] = jnp.zeros((SEASON, lanes), F32)
        z_ref[part, SEASON:, :] = turned_ref[:, columns]
        r_ref[part, width:, :] = jnp.zeros((SEASON, lanes), F32)
        resid = turned_ref[:, columns]
        for index, lag in enumerate(lags):
            begin = SEASON - lag
            resid = resid - w_ref[index : index + 1, columns] * z_ref[part, begin : begin + width, :]
        r_ref[part, :width, :] = resid
        back = data_scale * gd_ref[:, columns] + resid
        for index, lag in enumerate(lags):
            back = back - w_ref[index : index + 1, columns] * r_ref[part, lag : lag + width, :]
        base_ref[:, columns] = back
    m_copy.wait()
    v_copy.wait()


def regress_step(turned, weights, gd, m, v):
    width, rank = gd.shape
    lanes = 128
    return pl.pallas_call(
        functools.partial(regress_kernel, lanes),
        out_shape=(
            jax.ShapeDtypeStruct((width, rank), F32),
            jax.ShapeDtypeStruct((rank, width), F32),
            jax.ShapeDtypeStruct((rank, width), F32),
        ),
        in_specs=[whole()] * 3 + [far()] * 2,
        out_specs=(whole(),) * 3,
        scratch_shapes=[
            pltpu.VMEM((rank // lanes, SEASON + width, lanes), F32),
            pltpu.VMEM((rank // lanes, SEASON + width, lanes), F32),
            pltpu.SemaphoreType.DMA((2,)),
        ],
        compiler_params=params(),
        cost_estimate=cost(100 * rank * width, 6 * rank * width * 4),
        name="regress",
    )(turned, weights, gd, held(m), held(v))


def update_kernel(
    count, sizes, lanes, stratum_ref, halo_ref, w_ref, base_ref, x_ref, m_ref, v_ref, *rest
):
    outs, (z_ref, r_ref, new_ref) = rest[: 2 * len(sizes)], rest[2 * len(sizes) :]
    width, rank = base_ref.shape
    share = rank // count
    short = w_ref.shape[0] - 1
    reach = -(-short // 8) * 8
    block_index = lax.rem(lax.axis_index("blk") + stratum_ref[...], lax.axis_size("blk"))
    for part in range(rank // lanes):
        columns = slice(part * lanes, (part + 1) * lanes)
        halo = jnp.where(block_index == 0, 0.0, halo_ref[:, columns])
        z_ref[part, :SEASON, :] = halo
        z_ref[part, SEASON:, :] = jnp.zeros((reach, lanes), F32)
        r_ref[part, :SEASON, :] = -w_ref[short : short + 1, columns] * halo
        r_ref[part, SEASON:, :] = jnp.zeros((reach, lanes), F32)
        first_rows = r_ref[part, :reach, :]
        for lag in range(1, short + 1):
            begin = SEASON - lag
            first_rows = first_rows - w_ref[lag - 1 : lag, columns] * z_ref[part, begin : begin + reach, :]
        r_ref[part, :reach, :] = first_rows
        back = r_ref[part, :SEASON, :]
        for lag in range(1, short + 1):
            back = back - w_ref[lag - 1 : lag, columns] * r_ref[part, lag : lag + SEASON, :]
        base_ref[:SEASON, columns] += back
    for part in range(rank // lanes):
        rows = slice(part * lanes, (part + 1) * lanes)
        gradient = base_ref[:, rows].T
        first = beta_one * m_ref[rows, :] + (1.0 - beta_one) * gradient
        second = beta_two * v_ref[rows, :] + (1.0 - beta_two) * gradient * gradient
        new_ref[0, rows, :] = x_ref[rows, :] - step_rate * first / (jnp.sqrt(second) + adam_eps)
        new_ref[1, rows, :] = first
        new_ref[2, rows, :] = second
    odd = lax.axis_index("grp") % 2
    begin = 0
    for piece, size in enumerate(sizes):
        for line in range(count // 2):
            for side in range(2):
                one = 2 * line + (odd if side == 0 else 1 - odd)
                start = pl.multiple_of(one * share + begin, 8)
                for which in range(3):
                    outs[2 * piece + side][which, line] = new_ref[which, pl.ds(start, size), :]
        begin += size


def update_step(stratum, halo, weights, base, x, m, v, count, sizes):
    width, rank = base.shape
    lanes = 128
    reach = -(-(weights.shape[0] - 1) // 8) * 8
    kinds = []
    for size in sizes:
        kinds += [jax.ShapeDtypeStruct((3, count // 2, size, width), F32)] * 2

    def kernel(stratum_ref, halo_ref, w_ref, base_ref, x_ref, m_ref, v_ref, *rest):
        work = rest[-1]
        work[...] = base_ref[...]
        update_kernel(
            count, sizes, lanes, stratum_ref, halo_ref, w_ref, work, x_ref, m_ref, v_ref, *rest[:-1]
        )

    outs = pl.pallas_call(
        kernel,
        out_shape=tuple(kinds),
        in_specs=[whole()] * 7,
        out_specs=(whole(),) * len(kinds),
        scratch_shapes=[
            pltpu.VMEM((rank // lanes, SEASON + reach, lanes), F32),
            pltpu.VMEM((rank // lanes, SEASON + reach, lanes), F32),
            pltpu.VMEM((3, rank, width), F32),
            pltpu.VMEM((width, rank), F32),
        ],
        compiler_params=params(),
        cost_estimate=cost(60 * rank * width, 10 * rank * width * 4),
        name="update",
    )(stratum.reshape(1, 1), halo, weights, base, x, m, v)
    return [(outs[2 * piece], outs[2 * piece + 1]) for piece in range(len(sizes))]


def halve_kernel(level, kept_ref, got_ref, keep_ref, send_ref):
    mine = (lax.axis_index("grp") // level) % 2
    for line in range(keep_ref.shape[1]):
        for out, side in ((keep_ref, mine), (send_ref, 1 - mine)):
            for which in range(3):
                out[which, line] = kept_ref[which, 2 * line + side] + got_ref[which, 2 * line + side]


def halve(kept, got, level):
    _, lines, size, width = kept.shape
    out = jax.ShapeDtypeStruct((3, lines // 2, size, width), F32)
    return pl.pallas_call(
        functools.partial(halve_kernel, level),
        out_shape=(out, out),
        in_specs=[whole(), whole()],
        out_specs=(whole(), whole()),
        compiler_params=params(),
        cost_estimate=cost(kept.size, 3 * kept.size * 4),
        name="halve",
    )(kept, got)


def mean_kernel(count, kept_ref, got_ref, out_ref):
    for which in range(3):
        out_ref[which] = (kept_ref[which, 0] + got_ref[which, 0]) / count


def mean(kept, got, count):
    _, _, size, width = kept.shape
    return pl.pallas_call(
        functools.partial(mean_kernel, count),
        out_shape=jax.ShapeDtypeStruct((3, size, width), F32),
        in_specs=[whole(), whole()],
        out_specs=whole(),
        compiler_params=params(),
        cost_estimate=cost(2 * kept.size, 3 * kept.size * 4),
        name="mean",
    )(kept, got)


def place_kernel(share, spots, *rest):
    outs, sems = rest[-4:-1], rest[-1]
    group = lax.axis_index("grp")
    copies = []
    for index, (step, begin) in enumerate(spots):
        part = rest[index]
        start = pl.multiple_of((group ^ step) * share + begin, 8)
        for which in range(3):
            copies.append(
                pltpu.make_async_copy(
                    part.at[which],
                    outs[which].at[0, pl.ds(start, part.shape[1]), :],
                    sems.at[index, which],
                )
            )
    for copy in copies:
        copy.start()
    for copy in copies:
        copy.wait()


def place(parts, spots, share, count, sofar):
    width = parts[0].shape[2]
    out = jax.ShapeDtypeStruct((1, count * share, width), F32)
    return pl.pallas_call(
        functools.partial(place_kernel, share, spots),
        out_shape=(out, out, out),
        in_specs=[pl.BlockSpec(memory_space=pl.ANY)] * (len(parts) + len(sofar)),
        out_specs=(far(), far(), far()),
        input_output_aliases={len(parts) + which: which for which in range(len(sofar))},
        scratch_shapes=[pltpu.SemaphoreType.DMA((len(parts), 3))],
        compiler_params=params(),
        cost_estimate=cost(0, 6 * sum(part.size for part in parts) * 4),
        name="place",
    )(*parts, *sofar)


def crossed(value, step):
    count = lax.axis_size("grp")
    return lax.ppermute(value, "grp", [(source, source ^ step) for source in range(count)])


def shifted(value, steps):
    count = lax.axis_size("blk")
    return lax.ppermute(value, "blk", [(source, (source + steps) % count) for source in range(count)])


def delivered(value, step):
    groups, slots = lax.axis_size("grp"), lax.axis_size("blk")
    pairs = [
        (group * slots + slot, (group ^ step) * slots + (slot - 1) % slots)
        for group in range(groups)
        for slot in range(slots)
    ]
    return lax.ppermute(value, ("grp", "blk"), pairs)


def body(obs, mask_bits, factors, x_blocks, first_moment, second_moment, ar_weights, stratum):
    count = lax.axis_size("grp")
    series = obs.shape[0]
    rows = rows_of(series, 1024)
    third = max(series // rows // 3, 1) * rows
    bits = mask_bits.T

    tail, turned, x, lead, lead_bits = prepare(x_blocks, obs, bits, factors, rows)
    halo = shifted(tail, 1)
    err, kept, gd = error_step(obs, bits, factors, turned, lead, lead_bits)
    base, first, second = regress_step(turned, ar_weights, gd, first_moment, second_moment)
    share = x.shape[0] // count
    half = share // 2
    (keep0, send0), (keep1, send1) = update_step(
        stratum, halo, ar_weights, base, x, first, second, count, (half, share - half)
    )

    got0 = crossed(send0, 1)
    keep0, send0 = halve(keep0, got0, 2)
    send1, keep0 = lax.optimization_barrier((send1, keep0))
    got1 = crossed(send1, 1)
    far0 = crossed(send0, 2)
    factor_new = factor_step(lead, kept, err, turned, send0, None, 0, third)
    got1, factor_new = lax.optimization_barrier((got1, factor_new))
    keep1, send1 = halve(keep1, got1, 2)
    far1 = crossed(send1, 2)
    mean0 = mean(keep0, far0, count)

    near0 = delivered(mean0, 0)
    mean1 = mean(keep1, far1, count)
    near1 = delivered(mean1, 0)
    side1 = delivered(mean1, 2)
    side0 = crossed(near0, 2)
    factor_new = factor_step(lead, kept, err, turned, near0, factor_new, third, series - third)
    near1, factor_new = lax.optimization_barrier((near1, factor_new))
    parts = [near0, crossed(near0, 1), side0]
    parts += [near1, crossed(near1, 1), side1, crossed(side1, 1)]
    spots = [(0, 0), (1, 0), (2, 0), (0, half), (1, half), (2, half), (3, half)]
    outs = place(parts, spots, share, count, ())
    outs = place([crossed(side0, 1)], [(3, 0)], share, count, outs)
    return (factor_new, *outs)


def solution(mesh):
    rows = P(("grp", "blk"), None)
    blocks = P("grp", None, "blk")
    return jax.shard_map(
        body,
        mesh=mesh,
        in_specs=(rows, rows, rows, blocks, blocks, blocks, P(), P()),
        out_specs=(rows, blocks, blocks, blocks),
        check_vma=False,
    )
```

```python
import functools
import math

import jax
import jax.numpy as jnp
from jax import lax
from jax.experimental import pallas as pl
from jax.experimental.pallas import tpu as pltpu
from jax.sharding import PartitionSpec as P

SEASON = 168

beta_one = 0.9
beta_two = 0.999
adam_eps = 1e-08
step_rate = 0.05
factor_rate = 0.002
data_scale = 0.25

LIMIT = 32 * 1024 * 1024
F32 = jnp.float32
BF16 = jnp.bfloat16


def whole():
    return pl.BlockSpec(memory_space=pltpu.VMEM)


def far():
    return pl.BlockSpec(memory_space=pltpu.HBM)


def held(value):
    return pltpu.with_memory_space_constraint(value, pltpu.HBM)


def scalars():
    return pl.BlockSpec(memory_space=pltpu.SMEM)


def params(**more):
    return pltpu.CompilerParams(vmem_limit_bytes=LIMIT, **more)


def cost(flops, moved):
    return pl.CostEstimate(flops=int(flops), bytes_accessed=int(moved), transcendentals=0)


def rows_of(total, most):
    best = total
    for rows in range(128, most + 1, 128):
        if total % rows == 0:
            best = rows
    return best


def chunk_copies(rows, index, rank, hbm, both_ref, bits_ref, at, sems):
    obs_hbm, bits_hbm, f_hbm = hbm
    width = both_ref.shape[1] - rank
    source, target = pl.ds(index * rows, rows), pl.ds(at, rows)
    return (
        pltpu.make_async_copy(bits_hbm.at[:, source], bits_ref.at[:, target], sems.at[0]),
        pltpu.make_async_copy(
            f_hbm.at[source, :], both_ref.at[target, pl.ds(0, rank)], sems.at[1]
        ),
        pltpu.make_async_copy(
            obs_hbm.at[source, :], both_ref.at[target, pl.ds(rank, width)], sems.at[2]
        ),
    )


def prepare_kernel(
    rows, x_hbm, obs_hbm, bits_hbm, f_hbm, tail_ref, turned_ref, x_ref, both_ref, bits_ref, sem, sems
):
    copy = pltpu.make_async_copy(x_hbm.at[0], x_ref, sem)
    copy.start()
    rank = x_ref.shape[0]
    first = chunk_copies(rows, 0, rank, (obs_hbm, bits_hbm, f_hbm), both_ref, bits_ref, 0, sems)
    for other in first:
        other.start()
    copy.wait()
    turned_ref[...] = x_ref[...].T
    tail_ref[...] = turned_ref[turned_ref.shape[0] - SEASON :, :]
    for other in first:
        other.wait()


def prepare(x, obs, bits, factors, rows):
    rank, width = x.shape[1:]
    return pl.pallas_call(
        functools.partial(prepare_kernel, rows),
        out_shape=(
            jax.ShapeDtypeStruct((SEASON, rank), F32),
            jax.ShapeDtypeStruct((width, rank), F32),
            jax.ShapeDtypeStruct((rank, width), F32),
            jax.ShapeDtypeStruct((rows, rank + width), BF16),
            jax.ShapeDtypeStruct((bits.shape[0], rows), jnp.int32),
        ),
        in_specs=[far()] * 4,
        out_specs=(whole(),) * 5,
        scratch_shapes=[pltpu.SemaphoreType.DMA(()), pltpu.SemaphoreType.DMA((3,))],
        compiler_params=params(),
        cost_estimate=cost(0, 4 * rank * width * 4 + rows * (rank + width) * 4),
        name="prepare",
    )(held(x), held(obs), held(bits), held(factors))


def error_kernel(
    rows,
    obs_hbm,
    bits_hbm,
    f_hbm,
    turned_ref,
    first_ref,
    first_bits_ref,
    err_ref,
    both_ref,
    gd_ref,
    bits_ref,
    sems,
):
    width, series = err_ref.shape
    rank = turned_ref.shape[1]
    words = bits_ref.shape[0]
    per = width // words
    chunks = series // rows

    def copies(index):
        return chunk_copies(
            rows, index, rank, (obs_hbm, bits_hbm, f_hbm),
            both_ref, bits_ref, (index - 1) * rows, sems.at[index - 1],
        )

    def pair(index):
        if index == 0:
            return first_ref[...], first_bits_ref[...]
        part = pl.ds((index - 1) * rows, rows)
        return both_ref[part, :], bits_ref[:, part]

    for index in range(1, chunks):
        for copy in copies(index):
            copy.start()
    row = lax.broadcasted_iota(jnp.int32, (width, width), 0)
    column = lax.broadcasted_iota(jnp.int32, (width, width), 1)
    weights = jnp.concatenate(
        [turned_ref[...].astype(BF16), jnp.where(row == column, -1.0, 0.0).astype(BF16)], axis=1
    )
    flag = jnp.left_shift(1, lax.broadcasted_iota(jnp.int32, (1, per, 1), 1))

    def compare(index):
        if index > 0:
            for copy in copies(index):
                copy.wait()
        return lax.dot_general(
            weights, pair(index)[0], (((1,), (1,)), ((), ())), preferred_element_type=F32
        )

    def settle(index, gap):
        part = pl.ds(index * rows, rows)
        both, bits = pair(index)
        seen = jnp.bitwise_and(bits[:, None, :], flag) != 0
        error = jnp.where(seen, gap.reshape(words, per, rows), 0.0).reshape(width, rows)
        error = error.astype(BF16)
        err_ref[:, part] = error
        term = jnp.dot(error, both[:, :rank], preferred_element_type=F32)
        if index == 0:
            gd_ref[...] = term
        else:
            gd_ref[...] += term

    gap = compare(0)
    for index in range(chunks):
        later = compare(index + 1) if index + 1 < chunks else None
        settle(index, gap)
        gap = later


def error_step(obs, bits, factors, turned, first, first_bits):
    series, width = obs.shape
    rank = factors.shape[1]
    words = bits.shape[0]
    rows = first.shape[0]
    others = max(series - rows, rows)
    return pl.pallas_call(
        functools.partial(error_kernel, rows),
        out_shape=(
            jax.ShapeDtypeStruct((width, series), BF16),
            jax.ShapeDtypeStruct((others, rank + width), BF16),
            jax.ShapeDtypeStruct((width, rank), F32),
        ),
        in_specs=[far(), far(), far(), whole(), whole(), whole()],
        out_specs=(whole(), whole(), whole()),
        scratch_shapes=[
            pltpu.VMEM((words, others), jnp.int32),
            pltpu.SemaphoreType.DMA((others // rows, 3)),
        ],
        compiler_params=params(),
        cost_estimate=cost(8 * series * width * rank, series * (3 * width * 2 + words * 4)),
        name="errors",
    )(held(obs), held(bits), held(factors), turned, first, first_bits)


def factor_kernel(begin, rows, chunks, first_ref, both_ref, err_ref, turned_ref, *rest):
    out_hbm, out_ref, sems = rest[-3:]
    half = turned_ref[...].astype(BF16)
    size = rows // chunks

    def copy(index):
        return pltpu.make_async_copy(
            out_ref.at[pl.ds(index * size, size), :],
            out_hbm.at[pl.ds(begin + index * size, size), :],
            sems.at[index],
        )

    for index in range(chunks):
        part = pl.ds(begin + index * size, size)
        split = first_ref.shape[0]
        if begin + index * size < split:
            old = first_ref[part, pl.ds(0, half.shape[1])]
        else:
            old = both_ref[pl.ds(begin + index * size - split, size), pl.ds(0, half.shape[1])]
        gradient = lax.dot_general(
            err_ref[:, part], half, (((0,), (0,)), ((), ())), preferred_element_type=F32
        )
        out_ref[pl.ds(index * size, size), :] = (
            old.astype(F32) - factor_rate * gradient
        ).astype(BF16)
        copy(index).start()
    for index in range(chunks):
        copy(index).wait()


def factor_step(first, both, err, turned, after, sofar, begin, rows):
    width, series = err.shape
    rank = turned.shape[1]
    chunks = rows // math.gcd(first.shape[0], rows, begin)
    rest = (after,) if sofar is None else (after, sofar)
    return pl.pallas_call(
        functools.partial(factor_kernel, begin, rows, chunks),
        out_shape=jax.ShapeDtypeStruct((series, rank), BF16),
        in_specs=[whole()] * 4 + [pl.BlockSpec(memory_space=pl.ANY)] * len(rest),
        out_specs=far(),
        input_output_aliases={} if sofar is None else {5: 0},
        scratch_shapes=[pltpu.VMEM((rows, rank), BF16), pltpu.SemaphoreType.DMA((chunks,))],
        compiler_params=params(),
        cost_estimate=cost(2 * rows * width * rank, rows * 3 * width * 2),
        name="factors",
    )(first, both, err, turned, *rest)


def regress_kernel(
    lanes, turned_ref, w_ref, gd_ref, m_hbm, v_hbm, base_ref, m_ref, v_ref, z_ref, r_ref, sems
):
    m_copy = pltpu.make_async_copy(m_hbm.at[0], m_ref, sems.at[0])
    v_copy = pltpu.make_async_copy(v_hbm.at[0], v_ref, sems.at[1])
    m_copy.start()
    v_copy.start()
    width, rank = turned_ref.shape
    lags = list(range(1, w_ref.shape[0])) + [SEASON]
    for part in range(rank // lanes):
        columns = slice(part * lanes, (part + 1) * lanes)
        z_ref[part, :SEASON, :] = jnp.zeros((SEASON, lanes), F32)
        z_ref[part, SEASON:, :] = turned_ref[:, columns]
        r_ref[part, width:, :] = jnp.zeros((SEASON, lanes), F32)
        resid = turned_ref[:, columns]
        for index, lag in enumerate(lags):
            begin = SEASON - lag
            resid = resid - w_ref[index : index + 1, columns] * z_ref[part, begin : begin + width, :]
        r_ref[part, :width, :] = resid
        back = data_scale * gd_ref[:, columns] + resid
        for index, lag in enumerate(lags):
            back = back - w_ref[index : index + 1, columns] * r_ref[part, lag : lag + width, :]
        base_ref[:, columns] = back
    m_copy.wait()
    v_copy.wait()


def regress_step(turned, weights, gd, m, v):
    width, rank = gd.shape
    lanes = 128
    return pl.pallas_call(
        functools.partial(regress_kernel, lanes),
        out_shape=(
            jax.ShapeDtypeStruct((width, rank), F32),
            jax.ShapeDtypeStruct((rank, width), F32),
            jax.ShapeDtypeStruct((rank, width), F32),
        ),
        in_specs=[whole()] * 3 + [far()] * 2,
        out_specs=(whole(),) * 3,
        scratch_shapes=[
            pltpu.VMEM((rank // lanes, SEASON + width, lanes), F32),
            pltpu.VMEM((rank // lanes, SEASON + width, lanes), F32),
            pltpu.SemaphoreType.DMA((2,)),
        ],
        compiler_params=params(),
        cost_estimate=cost(100 * rank * width, 6 * rank * width * 4),
        name="regress",
    )(turned, weights, gd, held(m), held(v))


def update_kernel(
    count, sizes, lanes, stratum_ref, halo_ref, w_ref, base_ref, x_ref, m_ref, v_ref, *rest
):
    outs, (z_ref, r_ref, new_ref) = rest[: 2 * len(sizes)], rest[2 * len(sizes) :]
    width, rank = base_ref.shape
    share = rank // count
    short = w_ref.shape[0] - 1
    reach = -(-short // 8) * 8
    block_index = lax.rem(lax.axis_index("blk") + stratum_ref[...], lax.axis_size("blk"))
    for part in range(rank // lanes):
        columns = slice(part * lanes, (part + 1) * lanes)
        halo = jnp.where(block_index == 0, 0.0, halo_ref[:, columns])
        z_ref[part, :SEASON, :] = halo
        z_ref[part, SEASON:, :] = jnp.zeros((reach, lanes), F32)
        r_ref[part, :SEASON, :] = -w_ref[short : short + 1, columns] * halo
        r_ref[part, SEASON:, :] = jnp.zeros((reach, lanes), F32)
        first_rows = r_ref[part, :reach, :]
        for lag in range(1, short + 1):
            begin = SEASON - lag
            first_rows = first_rows - w_ref[lag - 1 : lag, columns] * z_ref[part, begin : begin + reach, :]
        r_ref[part, :reach, :] = first_rows
        back = r_ref[part, :SEASON, :]
        for lag in range(1, short + 1):
            back = back - w_ref[lag - 1 : lag, columns] * r_ref[part, lag : lag + SEASON, :]
        base_ref[:SEASON, columns] += back
    for part in range(rank // lanes):
        rows = slice(part * lanes, (part + 1) * lanes)
        gradient = base_ref[:, rows].T
        first = beta_one * m_ref[rows, :] + (1.0 - beta_one) * gradient
        second = beta_two * v_ref[rows, :] + (1.0 - beta_two) * gradient * gradient
        new_ref[0, rows, :] = x_ref[rows, :] - step_rate * first / (jnp.sqrt(second) + adam_eps)
        new_ref[1, rows, :] = first
        new_ref[2, rows, :] = second
    odd = lax.axis_index("grp") % 2
    begin = 0
    for piece, size in enumerate(sizes):
        for line in range(count // 2):
            for side in range(2):
                one = 2 * line + (odd if side == 0 else 1 - odd)
                start = pl.multiple_of(one * share + begin, 8)
                for which in range(3):
                    outs[2 * piece + side][which, line] = new_ref[which, pl.ds(start, size), :]
        begin += size


def update_step(stratum, halo, weights, base, x, m, v, count, sizes):
    width, rank = base.shape
    lanes = 128
    reach = -(-(weights.shape[0] - 1) // 8) * 8
    kinds = []
    for size in sizes:
        kinds += [jax.ShapeDtypeStruct((3, count // 2, size, width), F32)] * 2

    def kernel(stratum_ref, halo_ref, w_ref, base_ref, x_ref, m_ref, v_ref, *rest):
        work = rest[-1]
        work[...] = base_ref[...]
        update_kernel(
            count, sizes, lanes, stratum_ref, halo_ref, w_ref, work, x_ref, m_ref, v_ref, *rest[:-1]
        )

    outs = pl.pallas_call(
        kernel,
        out_shape=tuple(kinds),
        in_specs=[whole()] * 7,
        out_specs=(whole(),) * len(kinds),
        scratch_shapes=[
            pltpu.VMEM((rank // lanes, SEASON + reach, lanes), F32),
            pltpu.VMEM((rank // lanes, SEASON + reach, lanes), F32),
            pltpu.VMEM((3, rank, width), F32),
            pltpu.VMEM((width, rank), F32),
        ],
        compiler_params=params(),
        cost_estimate=cost(60 * rank * width, 10 * rank * width * 4),
        name="update",
    )(stratum.reshape(1, 1), halo, weights, base, x, m, v)
    return [(outs[2 * piece], outs[2 * piece + 1]) for piece in range(len(sizes))]


def halve_kernel(level, kept_ref, got_ref, keep_ref, send_ref):
    mine = (lax.axis_index("grp") // level) % 2
    for line in range(keep_ref.shape[1]):
        for out, side in ((keep_ref, mine), (send_ref, 1 - mine)):
            for which in range(3):
                out[which, line] = kept_ref[which, 2 * line + side] + got_ref[which, 2 * line + side]


def halve(kept, got, level):
    _, lines, size, width = kept.shape
    out = jax.ShapeDtypeStruct((3, lines // 2, size, width), F32)
    return pl.pallas_call(
        functools.partial(halve_kernel, level),
        out_shape=(out, out),
        in_specs=[whole(), whole()],
        out_specs=(whole(), whole()),
        compiler_params=params(),
        cost_estimate=cost(kept.size, 3 * kept.size * 4),
        name="halve",
    )(kept, got)


def mean_kernel(count, kept_ref, got_ref, out_ref):
    for which in range(3):
        out_ref[which] = (kept_ref[which, 0] + got_ref[which, 0]) / count


def mean(kept, got, count):
    _, _, size, width = kept.shape
    return pl.pallas_call(
        functools.partial(mean_kernel, count),
        out_shape=jax.ShapeDtypeStruct((3, size, width), F32),
        in_specs=[whole(), whole()],
        out_specs=whole(),
        compiler_params=params(),
        cost_estimate=cost(2 * kept.size, 3 * kept.size * 4),
        name="mean",
    )(kept, got)


def place_kernel(share, spots, *rest):
    outs, sems = rest[-4:-1], rest[-1]
    group = lax.axis_index("grp")
    copies = []
    for index, (step, begin) in enumerate(spots):
        part = rest[index]
        start = pl.multiple_of((group ^ step) * share + begin, 8)
        for which in range(3):
            copies.append(
                pltpu.make_async_copy(
                    part.at[which],
                    outs[which].at[0, pl.ds(start, part.shape[1]), :],
                    sems.at[index, which],
                )
            )
    for copy in copies:
        copy.start()
    for copy in copies:
        copy.wait()


def place(parts, spots, share, count, sofar):
    width = parts[0].shape[2]
    out = jax.ShapeDtypeStruct((1, count * share, width), F32)
    return pl.pallas_call(
        functools.partial(place_kernel, share, spots),
        out_shape=(out, out, out),
        in_specs=[pl.BlockSpec(memory_space=pl.ANY)] * (len(parts) + len(sofar)),
        out_specs=(far(), far(), far()),
        input_output_aliases={len(parts) + which: which for which in range(len(sofar))},
        scratch_shapes=[pltpu.SemaphoreType.DMA((len(parts), 3))],
        compiler_params=params(),
        cost_estimate=cost(0, 6 * sum(part.size for part in parts) * 4),
        name="place",
    )(*parts, *sofar)


def crossed(value, step):
    count = lax.axis_size("grp")
    return lax.ppermute(value, "grp", [(source, source ^ step) for source in range(count)])


def shifted(value, steps):
    count = lax.axis_size("blk")
    return lax.ppermute(value, "blk", [(source, (source + steps) % count) for source in range(count)])


def delivered(value, step):
    groups, slots = lax.axis_size("grp"), lax.axis_size("blk")
    pairs = [
        (group * slots + slot, (group ^ step) * slots + (slot - 1) % slots)
        for group in range(groups)
        for slot in range(slots)
    ]
    return lax.ppermute(value, ("grp", "blk"), pairs)


def body(obs, mask_bits, factors, x_blocks, first_moment, second_moment, ar_weights, stratum):
    count = lax.axis_size("grp")
    series = obs.shape[0]
    rows = rows_of(series, 768)
    third = max(series // rows // 3, 1) * rows
    bits = mask_bits.T

    tail, turned, x, lead, lead_bits = prepare(x_blocks, obs, bits, factors, rows)
    halo = shifted(tail, 1)
    err, kept, gd = error_step(obs, bits, factors, turned, lead, lead_bits)
    base, first, second = regress_step(turned, ar_weights, gd, first_moment, second_moment)
    share = x.shape[0] // count
    half = share // 2
    (keep0, send0), (keep1, send1) = update_step(
        stratum, halo, ar_weights, base, x, first, second, count, (half, share - half)
    )

    got0 = crossed(send0, 1)
    got1 = crossed(send1, 1)
    keep0, send0 = halve(keep0, got0, 2)
    far0 = crossed(send0, 2)
    factor_new = factor_step(lead, kept, err, turned, send0, None, 0, third)
    got1, factor_new = lax.optimization_barrier((got1, factor_new))
    keep1, send1 = halve(keep1, got1, 2)
    far1 = crossed(send1, 2)
    mean0 = mean(keep0, far0, count)

    near0 = delivered(mean0, 0)
    mean1 = mean(keep1, far1, count)
    near1 = delivered(mean1, 0)
    side1 = delivered(mean1, 2)
    side0 = crossed(near0, 2)
    factor_new = factor_step(lead, kept, err, turned, near0, factor_new, third, series - third)
    near1, factor_new = lax.optimization_barrier((near1, factor_new))
    parts = [near0, crossed(near0, 1), side0]
    parts += [near1, crossed(near1, 1), side1, crossed(side1, 1)]
    spots = [(0, 0), (1, 0), (2, 0), (0, half), (1, half), (2, half), (3, half)]
    outs = place(parts, spots, share, count, ())
    outs = place([crossed(side0, 1)], [(3, 0)], share, count, outs)
    return (factor_new, *outs)


def solution(mesh):
    rows = P(("grp", "blk"), None)
    blocks = P("grp", None, "blk")
    return jax.shard_map(
        body,
        mesh=mesh,
        in_specs=(rows, rows, rows, blocks, blocks, blocks, P(), P()),
        out_specs=(rows, blocks, blocks, blocks),
        check_vma=False,
    )
```

```python
import functools
import math

import jax
import jax.numpy as jnp
from jax import lax
from jax.experimental import pallas as pl
from jax.experimental.pallas import tpu as pltpu
from jax.sharding import PartitionSpec as P

SEASON = 168

beta_one = 0.9
beta_two = 0.999
adam_eps = 1e-08
step_rate = 0.05
factor_rate = 0.002
data_scale = 0.25

LIMIT = 32 * 1024 * 1024
F32 = jnp.float32
BF16 = jnp.bfloat16


def whole():
    return pl.BlockSpec(memory_space=pltpu.VMEM)


def far():
    return pl.BlockSpec(memory_space=pltpu.HBM)


def held(value):
    return pltpu.with_memory_space_constraint(value, pltpu.HBM)


def scalars():
    return pl.BlockSpec(memory_space=pltpu.SMEM)


def params(**more):
    return pltpu.CompilerParams(vmem_limit_bytes=LIMIT, **more)


def cost(flops, moved):
    return pl.CostEstimate(flops=int(flops), bytes_accessed=int(moved), transcendentals=0)


def rows_of(total, most):
    best = total
    for rows in range(128, most + 1, 128):
        if total % rows == 0:
            best = rows
    return best


def chunk_copies(rows, index, rank, hbm, both_ref, bits_ref, at, sems):
    obs_hbm, bits_hbm, f_hbm = hbm
    width = both_ref.shape[1] - rank
    source, target = pl.ds(index * rows, rows), pl.ds(at, rows)
    return (
        pltpu.make_async_copy(bits_hbm.at[:, source], bits_ref.at[:, target], sems.at[0]),
        pltpu.make_async_copy(
            f_hbm.at[source, :], both_ref.at[target, pl.ds(0, rank)], sems.at[1]
        ),
        pltpu.make_async_copy(
            obs_hbm.at[source, :], both_ref.at[target, pl.ds(rank, width)], sems.at[2]
        ),
    )


def prepare_kernel(
    rows, x_hbm, obs_hbm, bits_hbm, f_hbm, tail_ref, turned_ref, x_ref, both_ref, bits_ref, sem, sems
):
    copy = pltpu.make_async_copy(x_hbm.at[0], x_ref, sem)
    copy.start()
    rank = x_ref.shape[0]
    first = chunk_copies(rows, 0, rank, (obs_hbm, bits_hbm, f_hbm), both_ref, bits_ref, 0, sems)
    for other in first:
        other.start()
    copy.wait()
    turned_ref[...] = x_ref[...].T
    tail_ref[...] = turned_ref[turned_ref.shape[0] - SEASON :, :]
    for other in first:
        other.wait()


def prepare(x, obs, bits, factors, rows):
    rank, width = x.shape[1:]
    return pl.pallas_call(
        functools.partial(prepare_kernel, rows),
        out_shape=(
            jax.ShapeDtypeStruct((SEASON, rank), F32),
            jax.ShapeDtypeStruct((width, rank), F32),
            jax.ShapeDtypeStruct((rank, width), F32),
            jax.ShapeDtypeStruct((rows, rank + width), BF16),
            jax.ShapeDtypeStruct((bits.shape[0], rows), jnp.int32),
        ),
        in_specs=[far()] * 4,
        out_specs=(whole(),) * 5,
        scratch_shapes=[pltpu.SemaphoreType.DMA(()), pltpu.SemaphoreType.DMA((3,))],
        compiler_params=params(),
        cost_estimate=cost(0, 4 * rank * width * 4 + rows * (rank + width) * 4),
        name="prepare",
    )(held(x), held(obs), held(bits), held(factors))


def error_kernel(
    rows,
    obs_hbm,
    bits_hbm,
    f_hbm,
    turned_ref,
    first_ref,
    first_bits_ref,
    err_ref,
    both_ref,
    gd_ref,
    bits_ref,
    sems,
):
    width, series = err_ref.shape
    rank = turned_ref.shape[1]
    words = bits_ref.shape[0]
    per = width // words
    chunks = series // rows

    def copies(index):
        return chunk_copies(
            rows, index, rank, (obs_hbm, bits_hbm, f_hbm),
            both_ref, bits_ref, (index - 1) * rows, sems.at[index - 1],
        )

    def pair(index):
        if index == 0:
            return first_ref[...], first_bits_ref[...]
        part = pl.ds((index - 1) * rows, rows)
        return both_ref[part, :], bits_ref[:, part]

    for index in range(1, chunks):
        for copy in copies(index):
            copy.start()
    row = lax.broadcasted_iota(jnp.int32, (width, width), 0)
    column = lax.broadcasted_iota(jnp.int32, (width, width), 1)
    weights = jnp.concatenate(
        [turned_ref[...].astype(BF16), jnp.where(row == column, -1.0, 0.0).astype(BF16)], axis=1
    )
    flag = jnp.left_shift(1, lax.broadcasted_iota(jnp.int32, (1, per, 1), 1))

    def compare(index):
        if index > 0:
            for copy in copies(index):
                copy.wait()
        return lax.dot_general(
            weights, pair(index)[0], (((1,), (1,)), ((), ())), preferred_element_type=F32
        )

    def settle(index, gap):
        part = pl.ds(index * rows, rows)
        both, bits = pair(index)
        seen = jnp.bitwise_and(bits[:, None, :], flag) != 0
        error = jnp.where(seen, gap.reshape(words, per, rows), 0.0).reshape(width, rows)
        error = error.astype(BF16)
        err_ref[:, part] = error
        term = jnp.dot(error, both[:, :rank], preferred_element_type=F32)
        if index == 0:
            gd_ref[...] = term
        else:
            gd_ref[...] += term

    gap = compare(0)
    for index in range(chunks):
        later = compare(index + 1) if index + 1 < chunks else None
        settle(index, gap)
        gap = later


def error_step(obs, bits, factors, turned, first, first_bits):
    series, width = obs.shape
    rank = factors.shape[1]
    words = bits.shape[0]
    rows = first.shape[0]
    others = max(series - rows, rows)
    return pl.pallas_call(
        functools.partial(error_kernel, rows),
        out_shape=(
            jax.ShapeDtypeStruct((width, series), BF16),
            jax.ShapeDtypeStruct((others, rank + width), BF16),
            jax.ShapeDtypeStruct((width, rank), F32),
        ),
        in_specs=[far(), far(), far(), whole(), whole(), whole()],
        out_specs=(whole(), whole(), whole()),
        scratch_shapes=[
            pltpu.VMEM((words, others), jnp.int32),
            pltpu.SemaphoreType.DMA((others // rows, 3)),
        ],
        compiler_params=params(),
        cost_estimate=cost(8 * series * width * rank, series * (3 * width * 2 + words * 4)),
        name="errors",
    )(held(obs), held(bits), held(factors), turned, first, first_bits)


def factor_kernel(begin, rows, chunks, first_ref, both_ref, err_ref, turned_ref, *rest):
    out_hbm, out_ref, sems = rest[-3:]
    half = turned_ref[...].astype(BF16)
    size = rows // chunks

    def copy(index):
        return pltpu.make_async_copy(
            out_ref.at[pl.ds(index * size, size), :],
            out_hbm.at[pl.ds(begin + index * size, size), :],
            sems.at[index],
        )

    for index in range(chunks):
        part = pl.ds(begin + index * size, size)
        split = first_ref.shape[0]
        if begin + index * size < split:
            old = first_ref[part, pl.ds(0, half.shape[1])]
        else:
            old = both_ref[pl.ds(begin + index * size - split, size), pl.ds(0, half.shape[1])]
        gradient = lax.dot_general(
            err_ref[:, part], half, (((0,), (0,)), ((), ())), preferred_element_type=F32
        )
        out_ref[pl.ds(index * size, size), :] = (
            old.astype(F32) - factor_rate * gradient
        ).astype(BF16)
        copy(index).start()
    for index in range(chunks):
        copy(index).wait()


def factor_step(first, both, err, turned, after, sofar, begin, rows):
    width, series = err.shape
    rank = turned.shape[1]
    chunks = rows // math.gcd(first.shape[0], rows, begin)
    rest = (after,) if sofar is None else (after, sofar)
    return pl.pallas_call(
        functools.partial(factor_kernel, begin, rows, chunks),
        out_shape=jax.ShapeDtypeStruct((series, rank), BF16),
        in_specs=[whole()] * 4 + [pl.BlockSpec(memory_space=pl.ANY)] * len(rest),
        out_specs=far(),
        input_output_aliases={} if sofar is None else {5: 0},
        scratch_shapes=[pltpu.VMEM((rows, rank), BF16), pltpu.SemaphoreType.DMA((chunks,))],
        compiler_params=params(),
        cost_estimate=cost(2 * rows * width * rank, rows * 3 * width * 2),
        name="factors",
    )(first, both, err, turned, *rest)


def regress_kernel(
    lanes, turned_ref, w_ref, gd_ref, m_hbm, v_hbm, base_ref, m_ref, v_ref, z_ref, r_ref, sems
):
    m_copy = pltpu.make_async_copy(m_hbm.at[0], m_ref, sems.at[0])
    v_copy = pltpu.make_async_copy(v_hbm.at[0], v_ref, sems.at[1])
    m_copy.start()
    v_copy.start()
    width, rank = turned_ref.shape
    lags = list(range(1, w_ref.shape[0])) + [SEASON]
    for part in range(rank // lanes):
        columns = slice(part * lanes, (part + 1) * lanes)
        z_ref[part, :SEASON, :] = jnp.zeros((SEASON, lanes), F32)
        z_ref[part, SEASON:, :] = turned_ref[:, columns]
        r_ref[part, width:, :] = jnp.zeros((SEASON, lanes), F32)
        resid = turned_ref[:, columns]
        for index, lag in enumerate(lags):
            begin = SEASON - lag
            resid = resid - w_ref[index : index + 1, columns] * z_ref[part, begin : begin + width, :]
        r_ref[part, :width, :] = resid
        back = data_scale * gd_ref[:, columns] + resid
        for index, lag in enumerate(lags):
            back = back - w_ref[index : index + 1, columns] * r_ref[part, lag : lag + width, :]
        base_ref[:, columns] = back
    m_copy.wait()
    v_copy.wait()


def regress_step(turned, weights, gd, m, v):
    width, rank = gd.shape
    lanes = 128
    return pl.pallas_call(
        functools.partial(regress_kernel, lanes),
        out_shape=(
            jax.ShapeDtypeStruct((width, rank), F32),
            jax.ShapeDtypeStruct((rank, width), F32),
            jax.ShapeDtypeStruct((rank, width), F32),
        ),
        in_specs=[whole()] * 3 + [far()] * 2,
        out_specs=(whole(),) * 3,
        scratch_shapes=[
            pltpu.VMEM((rank // lanes, SEASON + width, lanes), F32),
            pltpu.VMEM((rank // lanes, SEASON + width, lanes), F32),
            pltpu.SemaphoreType.DMA((2,)),
        ],
        compiler_params=params(),
        cost_estimate=cost(100 * rank * width, 6 * rank * width * 4),
        name="regress",
    )(turned, weights, gd, held(m), held(v))


def update_kernel(
    count, sizes, lanes, stratum_ref, halo_ref, w_ref, base_ref, x_ref, m_ref, v_ref, *rest
):
    outs, (z_ref, r_ref, new_ref) = rest[: 2 * len(sizes)], rest[2 * len(sizes) :]
    width, rank = base_ref.shape
    share = rank // count
    short = w_ref.shape[0] - 1
    reach = -(-short // 8) * 8
    block_index = lax.rem(lax.axis_index("blk") + stratum_ref[...], lax.axis_size("blk"))
    for part in range(rank // lanes):
        columns = slice(part * lanes, (part + 1) * lanes)
        halo = jnp.where(block_index == 0, 0.0, halo_ref[:, columns])
        z_ref[part, :SEASON, :] = halo
        z_ref[part, SEASON:, :] = jnp.zeros((reach, lanes), F32)
        r_ref[part, :SEASON, :] = -w_ref[short : short + 1, columns] * halo
        r_ref[part, SEASON:, :] = jnp.zeros((reach, lanes), F32)
        first_rows = r_ref[part, :reach, :]
        for lag in range(1, short + 1):
            begin = SEASON - lag
            first_rows = first_rows - w_ref[lag - 1 : lag, columns] * z_ref[part, begin : begin + reach, :]
        r_ref[part, :reach, :] = first_rows
        back = r_ref[part, :SEASON, :]
        for lag in range(1, short + 1):
            back = back - w_ref[lag - 1 : lag, columns] * r_ref[part, lag : lag + SEASON, :]
        base_ref[:SEASON, columns] += back
    for part in range(rank // lanes):
        rows = slice(part * lanes, (part + 1) * lanes)
        gradient = base_ref[:, rows].T
        first = beta_one * m_ref[rows, :] + (1.0 - beta_one) * gradient
        second = beta_two * v_ref[rows, :] + (1.0 - beta_two) * gradient * gradient
        new_ref[0, rows, :] = x_ref[rows, :] - step_rate * first / (jnp.sqrt(second) + adam_eps)
        new_ref[1, rows, :] = first
        new_ref[2, rows, :] = second
    odd = lax.axis_index("grp") % 2
    begin = 0
    for piece, size in enumerate(sizes):
        for line in range(count // 2):
            for side in range(2):
                one = 2 * line + (odd if side == 0 else 1 - odd)
                start = pl.multiple_of(one * share + begin, 8)
                for which in range(3):
                    outs[2 * piece + side][which, line] = new_ref[which, pl.ds(start, size), :]
        begin += size


def update_step(stratum, halo, weights, base, x, m, v, count, sizes):
    width, rank = base.shape
    lanes = 128
    reach = -(-(weights.shape[0] - 1) // 8) * 8
    kinds = []
    for size in sizes:
        kinds += [jax.ShapeDtypeStruct((3, count // 2, size, width), F32)] * 2

    def kernel(stratum_ref, halo_ref, w_ref, base_ref, x_ref, m_ref, v_ref, *rest):
        work = rest[-1]
        work[...] = base_ref[...]
        update_kernel(
            count, sizes, lanes, stratum_ref, halo_ref, w_ref, work, x_ref, m_ref, v_ref, *rest[:-1]
        )

    outs = pl.pallas_call(
        kernel,
        out_shape=tuple(kinds),
        in_specs=[whole()] * 7,
        out_specs=(whole(),) * len(kinds),
        scratch_shapes=[
            pltpu.VMEM((rank // lanes, SEASON + reach, lanes), F32),
            pltpu.VMEM((rank // lanes, SEASON + reach, lanes), F32),
            pltpu.VMEM((3, rank, width), F32),
            pltpu.VMEM((width, rank), F32),
        ],
        compiler_params=params(),
        cost_estimate=cost(60 * rank * width, 10 * rank * width * 4),
        name="update",
    )(stratum.reshape(1, 1), halo, weights, base, x, m, v)
    return [(outs[2 * piece], outs[2 * piece + 1]) for piece in range(len(sizes))]


def halve_kernel(level, kept_ref, got_ref, keep_ref, send_ref):
    mine = (lax.axis_index("grp") // level) % 2
    for line in range(keep_ref.shape[1]):
        for out, side in ((keep_ref, mine), (send_ref, 1 - mine)):
            for which in range(3):
                out[which, line] = kept_ref[which, 2 * line + side] + got_ref[which, 2 * line + side]


def halve(kept, got, level):
    _, lines, size, width = kept.shape
    out = jax.ShapeDtypeStruct((3, lines // 2, size, width), F32)
    return pl.pallas_call(
        functools.partial(halve_kernel, level),
        out_shape=(out, out),
        in_specs=[whole(), whole()],
        out_specs=(whole(), whole()),
        compiler_params=params(),
        cost_estimate=cost(kept.size, 3 * kept.size * 4),
        name="halve",
    )(kept, got)


def mean_kernel(count, kept_ref, got_ref, out_ref):
    for which in range(3):
        out_ref[which] = (kept_ref[which, 0] + got_ref[which, 0]) / count


def mean(kept, got, count):
    _, _, size, width = kept.shape
    return pl.pallas_call(
        functools.partial(mean_kernel, count),
        out_shape=jax.ShapeDtypeStruct((3, size, width), F32),
        in_specs=[whole(), whole()],
        out_specs=whole(),
        compiler_params=params(),
        cost_estimate=cost(2 * kept.size, 3 * kept.size * 4),
        name="mean",
    )(kept, got)


def place_kernel(share, spots, *rest):
    outs, sems = rest[-4:-1], rest[-1]
    group = lax.axis_index("grp")
    copies = []
    for index, (step, begin) in enumerate(spots):
        part = rest[index]
        start = pl.multiple_of((group ^ step) * share + begin, 8)
        for which in range(3):
            copies.append(
                pltpu.make_async_copy(
                    part.at[which],
                    outs[which].at[0, pl.ds(start, part.shape[1]), :],
                    sems.at[index, which],
                )
            )
    for copy in copies:
        copy.start()
    for copy in copies:
        copy.wait()


def place(parts, spots, share, count, sofar):
    width = parts[0].shape[2]
    out = jax.ShapeDtypeStruct((1, count * share, width), F32)
    return pl.pallas_call(
        functools.partial(place_kernel, share, spots),
        out_shape=(out, out, out),
        in_specs=[pl.BlockSpec(memory_space=pl.ANY)] * (len(parts) + len(sofar)),
        out_specs=(far(), far(), far()),
        input_output_aliases={len(parts) + which: which for which in range(len(sofar))},
        scratch_shapes=[pltpu.SemaphoreType.DMA((len(parts), 3))],
        compiler_params=params(),
        cost_estimate=cost(0, 6 * sum(part.size for part in parts) * 4),
        name="place",
    )(*parts, *sofar)


def crossed(value, step):
    count = lax.axis_size("grp")
    return lax.ppermute(value, "grp", [(source, source ^ step) for source in range(count)])


def shifted(value, steps):
    count = lax.axis_size("blk")
    return lax.ppermute(value, "blk", [(source, (source + steps) % count) for source in range(count)])


def delivered(value, step):
    groups, slots = lax.axis_size("grp"), lax.axis_size("blk")
    pairs = [
        (group * slots + slot, (group ^ step) * slots + (slot - 1) % slots)
        for group in range(groups)
        for slot in range(slots)
    ]
    return lax.ppermute(value, ("grp", "blk"), pairs)


def body(obs, mask_bits, factors, x_blocks, first_moment, second_moment, ar_weights, stratum):
    count = lax.axis_size("grp")
    series = obs.shape[0]
    rows = rows_of(series, 1024)
    third = max(series // rows // 6, 1) * rows
    bits = mask_bits.T

    tail, turned, x, lead, lead_bits = prepare(x_blocks, obs, bits, factors, rows)
    halo = shifted(tail, 1)
    err, kept, gd = error_step(obs, bits, factors, turned, lead, lead_bits)
    base, first, second = regress_step(turned, ar_weights, gd, first_moment, second_moment)
    share = x.shape[0] // count
    half = share // 2
    (keep0, send0), (keep1, send1) = update_step(
        stratum, halo, ar_weights, base, x, first, second, count, (half, share - half)
    )

    got0 = crossed(send0, 1)
    got1 = crossed(send1, 1)
    keep0, send0 = halve(keep0, got0, 2)
    far0 = crossed(send0, 2)
    factor_new = factor_step(lead, kept, err, turned, send0, None, 0, third)
    got1, factor_new = lax.optimization_barrier((got1, factor_new))
    keep1, send1 = halve(keep1, got1, 2)
    far1 = crossed(send1, 2)
    mean0 = mean(keep0, far0, count)

    near0 = delivered(mean0, 0)
    mean1 = mean(keep1, far1, count)
    near1 = delivered(mean1, 0)
    side1 = delivered(mean1, 2)
    side0 = crossed(near0, 2)
    factor_new = factor_step(lead, kept, err, turned, near0, factor_new, third, series - third)
    near1, factor_new = lax.optimization_barrier((near1, factor_new))
    parts = [near0, crossed(near0, 1), side0]
    parts += [near1, crossed(near1, 1), side1, crossed(side1, 1)]
    spots = [(0, 0), (1, 0), (2, 0), (0, half), (1, half), (2, half), (3, half)]
    outs = place(parts, spots, share, count, ())
    outs = place([crossed(side0, 1)], [(3, 0)], share, count, outs)
    return (factor_new, *outs)


def solution(mesh):
    rows = P(("grp", "blk"), None)
    blocks = P("grp", None, "blk")
    return jax.shard_map(
        body,
        mesh=mesh,
        in_specs=(rows, rows, rows, blocks, blocks, blocks, P(), P()),
        out_specs=(rows, blocks, blocks, blocks),
        check_vma=False,
    )
```

```python
import functools
import math

import jax
import jax.numpy as jnp
from jax import lax
from jax.experimental import pallas as pl
from jax.experimental.pallas import tpu as pltpu
from jax.sharding import PartitionSpec as P

SEASON = 168

beta_one = 0.9
beta_two = 0.999
adam_eps = 1e-08
step_rate = 0.05
factor_rate = 0.002
data_scale = 0.25

LIMIT = 32 * 1024 * 1024
F32 = jnp.float32
BF16 = jnp.bfloat16


def whole():
    return pl.BlockSpec(memory_space=pltpu.VMEM)


def far():
    return pl.BlockSpec(memory_space=pltpu.HBM)


def held(value):
    return pltpu.with_memory_space_constraint(value, pltpu.HBM)


def scalars():
    return pl.BlockSpec(memory_space=pltpu.SMEM)


def params(**more):
    return pltpu.CompilerParams(vmem_limit_bytes=LIMIT, **more)


def cost(flops, moved):
    return pl.CostEstimate(flops=int(flops), bytes_accessed=int(moved), transcendentals=0)


def rows_of(total, most):
    best = total
    for rows in range(128, most + 1, 128):
        if total % rows == 0:
            best = rows
    return best


def chunk_copies(rows, index, rank, hbm, both_ref, bits_ref, at, sems):
    obs_hbm, bits_hbm, f_hbm = hbm
    width = both_ref.shape[1] - rank
    source, target = pl.ds(index * rows, rows), pl.ds(at, rows)
    return (
        pltpu.make_async_copy(
            f_hbm.at[source, :], both_ref.at[target, pl.ds(0, rank)], sems.at[1]
        ),
        pltpu.make_async_copy(
            obs_hbm.at[source, :], both_ref.at[target, pl.ds(rank, width)], sems.at[2]
        ),
        pltpu.make_async_copy(bits_hbm.at[:, source], bits_ref.at[:, target], sems.at[0]),
    )


def prepare_kernel(
    rows, x_hbm, obs_hbm, bits_hbm, f_hbm, tail_ref, turned_ref, x_ref, both_ref, bits_ref, sem, sems
):
    copy = pltpu.make_async_copy(x_hbm.at[0], x_ref, sem)
    copy.start()
    rank = x_ref.shape[0]
    first = chunk_copies(rows, 0, rank, (obs_hbm, bits_hbm, f_hbm), both_ref, bits_ref, 0, sems)
    for other in first:
        other.start()
    copy.wait()
    turned_ref[...] = x_ref[...].T
    tail_ref[...] = turned_ref[turned_ref.shape[0] - SEASON :, :]
    for other in first:
        other.wait()


def prepare(x, obs, bits, factors, rows):
    rank, width = x.shape[1:]
    return pl.pallas_call(
        functools.partial(prepare_kernel, rows),
        out_shape=(
            jax.ShapeDtypeStruct((SEASON, rank), F32),
            jax.ShapeDtypeStruct((width, rank), F32),
            jax.ShapeDtypeStruct((rank, width), F32),
            jax.ShapeDtypeStruct((rows, rank + width), BF16),
            jax.ShapeDtypeStruct((bits.shape[0], rows), jnp.int32),
        ),
        in_specs=[far()] * 4,
        out_specs=(whole(),) * 5,
        scratch_shapes=[pltpu.SemaphoreType.DMA(()), pltpu.SemaphoreType.DMA((3,))],
        compiler_params=params(),
        cost_estimate=cost(0, 4 * rank * width * 4 + rows * (rank + width) * 4),
        name="prepare",
    )(held(x), held(obs), held(bits), held(factors))


def error_kernel(
    rows,
    obs_hbm,
    bits_hbm,
    f_hbm,
    turned_ref,
    first_ref,
    first_bits_ref,
    err_ref,
    both_ref,
    gd_ref,
    bits_ref,
    sems,
):
    width, series = err_ref.shape
    rank = turned_ref.shape[1]
    words = bits_ref.shape[0]
    per = width // words
    chunks = series // rows

    def copies(index):
        return chunk_copies(
            rows, index, rank, (obs_hbm, bits_hbm, f_hbm),
            both_ref, bits_ref, (index - 1) * rows, sems.at[index - 1],
        )

    def pair(index):
        if index == 0:
            return first_ref[...], first_bits_ref[...]
        part = pl.ds((index - 1) * rows, rows)
        return both_ref[part, :], bits_ref[:, part]

    for index in range(1, chunks):
        for copy in copies(index):
            copy.start()
    row = lax.broadcasted_iota(jnp.int32, (width, width), 0)
    column = lax.broadcasted_iota(jnp.int32, (width, width), 1)
    weights = jnp.concatenate(
        [turned_ref[...].astype(BF16), jnp.where(row == column, -1.0, 0.0).astype(BF16)], axis=1
    )
    flag = jnp.left_shift(1, lax.broadcasted_iota(jnp.int32, (1, per, 1), 1))

    def compare(index):
        if index > 0:
            for copy in copies(index)[:2]:
                copy.wait()
        return lax.dot_general(
            weights, pair(index)[0], (((1,), (1,)), ((), ())), preferred_element_type=F32
        )

    def settle(index, gap):
        part = pl.ds(index * rows, rows)
        if index > 0:
            copies(index)[2].wait()
        both, bits = pair(index)
        seen = jnp.bitwise_and(bits[:, None, :], flag) != 0
        error = jnp.where(seen, gap.reshape(words, per, rows), 0.0).reshape(width, rows)
        error = error.astype(BF16)
        err_ref[:, part] = error
        term = jnp.dot(error, both[:, :rank], preferred_element_type=F32)
        if index == 0:
            gd_ref[...] = term
        else:
            gd_ref[...] += term

    gap = compare(0)
    for index in range(chunks):
        later = compare(index + 1) if index + 1 < chunks else None
        settle(index, gap)
        gap = later


def error_step(obs, bits, factors, turned, first, first_bits):
    series, width = obs.shape
    rank = factors.shape[1]
    words = bits.shape[0]
    rows = first.shape[0]
    others = max(series - rows, rows)
    return pl.pallas_call(
        functools.partial(error_kernel, rows),
        out_shape=(
            jax.ShapeDtypeStruct((width, series), BF16),
            jax.ShapeDtypeStruct((others, rank + width), BF16),
            jax.ShapeDtypeStruct((width, rank), F32),
        ),
        in_specs=[far(), far(), far(), whole(), whole(), whole()],
        out_specs=(whole(), whole(), whole()),
        scratch_shapes=[
            pltpu.VMEM((words, others), jnp.int32),
            pltpu.SemaphoreType.DMA((others // rows, 3)),
        ],
        compiler_params=params(),
        cost_estimate=cost(8 * series * width * rank, series * (3 * width * 2 + words * 4)),
        name="errors",
    )(held(obs), held(bits), held(factors), turned, first, first_bits)


def factor_kernel(begin, rows, chunks, first_ref, both_ref, err_ref, turned_ref, *rest):
    out_hbm, out_ref, sems = rest[-3:]
    half = turned_ref[...].astype(BF16)
    size = rows // chunks

    def copy(index):
        return pltpu.make_async_copy(
            out_ref.at[pl.ds(index * size, size), :],
            out_hbm.at[pl.ds(begin + index * size, size), :],
            sems.at[index],
        )

    for index in range(chunks):
        part = pl.ds(begin + index * size, size)
        split = first_ref.shape[0]
        if begin + index * size < split:
            old = first_ref[part, pl.ds(0, half.shape[1])]
        else:
            old = both_ref[pl.ds(begin + index * size - split, size), pl.ds(0, half.shape[1])]
        gradient = lax.dot_general(
            err_ref[:, part], half, (((0,), (0,)), ((), ())), preferred_element_type=F32
        )
        out_ref[pl.ds(index * size, size), :] = (
            old.astype(F32) - factor_rate * gradient
        ).astype(BF16)
        copy(index).start()
    for index in range(chunks):
        copy(index).wait()


def factor_step(first, both, err, turned, after, sofar, begin, rows):
    width, series = err.shape
    rank = turned.shape[1]
    chunks = rows // math.gcd(first.shape[0], rows, begin)
    rest = (after,) if sofar is None else (after, sofar)
    return pl.pallas_call(
        functools.partial(factor_kernel, begin, rows, chunks),
        out_shape=jax.ShapeDtypeStruct((series, rank), BF16),
        in_specs=[whole()] * 4 + [pl.BlockSpec(memory_space=pl.ANY)] * len(rest),
        out_specs=far(),
        input_output_aliases={} if sofar is None else {5: 0},
        scratch_shapes=[pltpu.VMEM((rows, rank), BF16), pltpu.SemaphoreType.DMA((chunks,))],
        compiler_params=params(),
        cost_estimate=cost(2 * rows * width * rank, rows * 3 * width * 2),
        name="factors",
    )(first, both, err, turned, *rest)


def regress_kernel(
    lanes, turned_ref, w_ref, gd_ref, m_hbm, v_hbm, base_ref, m_ref, v_ref, z_ref, r_ref, sems
):
    m_copy = pltpu.make_async_copy(m_hbm.at[0], m_ref, sems.at[0])
    v_copy = pltpu.make_async_copy(v_hbm.at[0], v_ref, sems.at[1])
    m_copy.start()
    v_copy.start()
    width, rank = turned_ref.shape
    lags = list(range(1, w_ref.shape[0])) + [SEASON]
    for part in range(rank // lanes):
        columns = slice(part * lanes, (part + 1) * lanes)
        z_ref[part, :SEASON, :] = jnp.zeros((SEASON, lanes), F32)
        z_ref[part, SEASON:, :] = turned_ref[:, columns]
        r_ref[part, width:, :] = jnp.zeros((SEASON, lanes), F32)
        resid = turned_ref[:, columns]
        for index, lag in enumerate(lags):
            begin = SEASON - lag
            resid = resid - w_ref[index : index + 1, columns] * z_ref[part, begin : begin + width, :]
        r_ref[part, :width, :] = resid
        back = data_scale * gd_ref[:, columns] + resid
        for index, lag in enumerate(lags):
            back = back - w_ref[index : index + 1, columns] * r_ref[part, lag : lag + width, :]
        base_ref[:, columns] = back
    m_copy.wait()
    v_copy.wait()


def regress_step(turned, weights, gd, m, v):
    width, rank = gd.shape
    lanes = 128
    return pl.pallas_call(
        functools.partial(regress_kernel, lanes),
        out_shape=(
            jax.ShapeDtypeStruct((width, rank), F32),
            jax.ShapeDtypeStruct((rank, width), F32),
            jax.ShapeDtypeStruct((rank, width), F32),
        ),
        in_specs=[whole()] * 3 + [far()] * 2,
        out_specs=(whole(),) * 3,
        scratch_shapes=[
            pltpu.VMEM((rank // lanes, SEASON + width, lanes), F32),
            pltpu.VMEM((rank // lanes, SEASON + width, lanes), F32),
            pltpu.SemaphoreType.DMA((2,)),
        ],
        compiler_params=params(),
        cost_estimate=cost(100 * rank * width, 6 * rank * width * 4),
        name="regress",
    )(turned, weights, gd, held(m), held(v))


def update_kernel(
    count, sizes, lanes, stratum_ref, halo_ref, w_ref, base_ref, x_ref, m_ref, v_ref, *rest
):
    outs, (z_ref, r_ref, new_ref) = rest[: 2 * len(sizes)], rest[2 * len(sizes) :]
    width, rank = base_ref.shape
    share = rank // count
    short = w_ref.shape[0] - 1
    reach = -(-short // 8) * 8
    block_index = lax.rem(lax.axis_index("blk") + stratum_ref[...], lax.axis_size("blk"))
    for part in range(rank // lanes):
        columns = slice(part * lanes, (part + 1) * lanes)
        halo = jnp.where(block_index == 0, 0.0, halo_ref[:, columns])
        z_ref[part, :SEASON, :] = halo
        z_ref[part, SEASON:, :] = jnp.zeros((reach, lanes), F32)
        r_ref[part, :SEASON, :] = -w_ref[short : short + 1, columns] * halo
        r_ref[part, SEASON:, :] = jnp.zeros((reach, lanes), F32)
        first_rows = r_ref[part, :reach, :]
        for lag in range(1, short + 1):
            begin = SEASON - lag
            first_rows = first_rows - w_ref[lag - 1 : lag, columns] * z_ref[part, begin : begin + reach, :]
        r_ref[part, :reach, :] = first_rows
        back = r_ref[part, :SEASON, :]
        for lag in range(1, short + 1):
            back = back - w_ref[lag - 1 : lag, columns] * r_ref[part, lag : lag + SEASON, :]
        base_ref[:SEASON, columns] += back
    for part in range(rank // lanes):
        rows = slice(part * lanes, (part + 1) * lanes)
        gradient = base_ref[:, rows].T
        first = beta_one * m_ref[rows, :] + (1.0 - beta_one) * gradient
        second = beta_two * v_ref[rows, :] + (1.0 - beta_two) * gradient * gradient
        new_ref[0, rows, :] = x_ref[rows, :] - step_rate * first / (jnp.sqrt(second) + adam_eps)
        new_ref[1, rows, :] = first
        new_ref[2, rows, :] = second
    odd = lax.axis_index("grp") % 2
    begin = 0
    for piece, size in enumerate(sizes):
        for line in range(count // 2):
            for side in range(2):
                one = 2 * line + (odd if side == 0 else 1 - odd)
                start = pl.multiple_of(one * share + begin, 8)
                for which in range(3):
                    outs[2 * piece + side][which, line] = new_ref[which, pl.ds(start, size), :]
        begin += size


def update_step(stratum, halo, weights, base, x, m, v, count, sizes):
    width, rank = base.shape
    lanes = 128
    reach = -(-(weights.shape[0] - 1) // 8) * 8
    kinds = []
    for size in sizes:
        kinds += [jax.ShapeDtypeStruct((3, count // 2, size, width), F32)] * 2

    def kernel(stratum_ref, halo_ref, w_ref, base_ref, x_ref, m_ref, v_ref, *rest):
        work = rest[-1]
        work[...] = base_ref[...]
        update_kernel(
            count, sizes, lanes, stratum_ref, halo_ref, w_ref, work, x_ref, m_ref, v_ref, *rest[:-1]
        )

    outs = pl.pallas_call(
        kernel,
        out_shape=tuple(kinds),
        in_specs=[whole()] * 7,
        out_specs=(whole(),) * len(kinds),
        scratch_shapes=[
            pltpu.VMEM((rank // lanes, SEASON + reach, lanes), F32),
            pltpu.VMEM((rank // lanes, SEASON + reach, lanes), F32),
            pltpu.VMEM((3, rank, width), F32),
            pltpu.VMEM((width, rank), F32),
        ],
        compiler_params=params(),
        cost_estimate=cost(60 * rank * width, 10 * rank * width * 4),
        name="update",
    )(stratum.reshape(1, 1), halo, weights, base, x, m, v)
    return [(outs[2 * piece], outs[2 * piece + 1]) for piece in range(len(sizes))]


def halve_kernel(level, kept_ref, got_ref, keep_ref, send_ref):
    mine = (lax.axis_index("grp") // level) % 2
    for line in range(keep_ref.shape[1]):
        for out, side in ((keep_ref, mine), (send_ref, 1 - mine)):
            for which in range(3):
                out[which, line] = kept_ref[which, 2 * line + side] + got_ref[which, 2 * line + side]


def halve(kept, got, level):
    _, lines, size, width = kept.shape
    out = jax.ShapeDtypeStruct((3, lines // 2, size, width), F32)
    return pl.pallas_call(
        functools.partial(halve_kernel, level),
        out_shape=(out, out),
        in_specs=[whole(), whole()],
        out_specs=(whole(), whole()),
        compiler_params=params(),
        cost_estimate=cost(kept.size, 3 * kept.size * 4),
        name="halve",
    )(kept, got)


def mean_kernel(count, kept_ref, got_ref, out_ref):
    for which in range(3):
        out_ref[which] = (kept_ref[which, 0] + got_ref[which, 0]) / count


def mean(kept, got, count):
    _, _, size, width = kept.shape
    return pl.pallas_call(
        functools.partial(mean_kernel, count),
        out_shape=jax.ShapeDtypeStruct((3, size, width), F32),
        in_specs=[whole(), whole()],
        out_specs=whole(),
        compiler_params=params(),
        cost_estimate=cost(2 * kept.size, 3 * kept.size * 4),
        name="mean",
    )(kept, got)


def place_kernel(share, spots, *rest):
    outs, sems = rest[-4:-1], rest[-1]
    group = lax.axis_index("grp")
    copies = []
    for index, (step, begin) in enumerate(spots):
        part = rest[index]
        start = pl.multiple_of((group ^ step) * share + begin, 8)
        for which in range(3):
            copies.append(
                pltpu.make_async_copy(
                    part.at[which],
                    outs[which].at[0, pl.ds(start, part.shape[1]), :],
                    sems.at[index, which],
                )
            )
    for copy in copies:
        copy.start()
    for copy in copies:
        copy.wait()


def place(parts, spots, share, count, sofar):
    width = parts[0].shape[2]
    out = jax.ShapeDtypeStruct((1, count * share, width), F32)
    return pl.pallas_call(
        functools.partial(place_kernel, share, spots),
        out_shape=(out, out, out),
        in_specs=[pl.BlockSpec(memory_space=pl.ANY)] * (len(parts) + len(sofar)),
        out_specs=(far(), far(), far()),
        input_output_aliases={len(parts) + which: which for which in range(len(sofar))},
        scratch_shapes=[pltpu.SemaphoreType.DMA((len(parts), 3))],
        compiler_params=params(),
        cost_estimate=cost(0, 6 * sum(part.size for part in parts) * 4),
        name="place",
    )(*parts, *sofar)


def crossed(value, step):
    count = lax.axis_size("grp")
    return lax.ppermute(value, "grp", [(source, source ^ step) for source in range(count)])


def shifted(value, steps):
    count = lax.axis_size("blk")
    return lax.ppermute(value, "blk", [(source, (source + steps) % count) for source in range(count)])


def delivered(value, step):
    groups, slots = lax.axis_size("grp"), lax.axis_size("blk")
    pairs = [
        (group * slots + slot, (group ^ step) * slots + (slot - 1) % slots)
        for group in range(groups)
        for slot in range(slots)
    ]
    return lax.ppermute(value, ("grp", "blk"), pairs)


def body(obs, mask_bits, factors, x_blocks, first_moment, second_moment, ar_weights, stratum):
    count = lax.axis_size("grp")
    series = obs.shape[0]
    rows = rows_of(series, 1024)
    third = max(series // rows // 3, 1) * rows
    bits = mask_bits.T

    tail, turned, x, lead, lead_bits = prepare(x_blocks, obs, bits, factors, rows)
    halo = shifted(tail, 1)
    err, kept, gd = error_step(obs, bits, factors, turned, lead, lead_bits)
    base, first, second = regress_step(turned, ar_weights, gd, first_moment, second_moment)
    share = x.shape[0] // count
    half = share // 2
    (keep0, send0), (keep1, send1) = update_step(
        stratum, halo, ar_weights, base, x, first, second, count, (half, share - half)
    )

    got0 = crossed(send0, 1)
    got1 = crossed(send1, 1)
    keep0, send0 = halve(keep0, got0, 2)
    far0 = crossed(send0, 2)
    factor_new = factor_step(lead, kept, err, turned, send0, None, 0, third)
    got1, factor_new = lax.optimization_barrier((got1, factor_new))
    keep1, send1 = halve(keep1, got1, 2)
    far1 = crossed(send1, 2)
    mean0 = mean(keep0, far0, count)

    near0 = delivered(mean0, 0)
    mean1 = mean(keep1, far1, count)
    near1 = delivered(mean1, 0)
    side1 = delivered(mean1, 2)
    side0 = crossed(near0, 2)
    factor_new = factor_step(lead, kept, err, turned, near0, factor_new, third, series - third)
    near1, factor_new = lax.optimization_barrier((near1, factor_new))
    parts = [near0, crossed(near0, 1), side0]
    parts += [near1, crossed(near1, 1), side1, crossed(side1, 1)]
    spots = [(0, 0), (1, 0), (2, 0), (0, half), (1, half), (2, half), (3, half)]
    outs = place(parts, spots, share, count, ())
    outs = place([crossed(side0, 1)], [(3, 0)], share, count, outs)
    return (factor_new, *outs)


def solution(mesh):
    rows = P(("grp", "blk"), None)
    blocks = P("grp", None, "blk")
    return jax.shard_map(
        body,
        mesh=mesh,
        in_specs=(rows, rows, rows, blocks, blocks, blocks, P(), P()),
        out_specs=(rows, blocks, blocks, blocks),
        check_vma=False,
    )
```
